32 devices in a mesh: dp: 8 (over z, x), tensor: 4 (over y, core).
Axes of the slice: x: 2, y: 2, z: 4, core: 2. Of those that a mesh axis runs over, the one named last changes fastest.
Arguments:
- media: bfloat16 [24, 2048, 1024], P('dp'), may hold values from -6 to 6
- frame_counts: int32 [24], P('dp'), may hold values from 1 to 8, as said below
- time_embed: bfloat16 [8, 1024], replicated, may hold values from -3 to 3
- latents: bfloat16 [64, 1024], replicated, may hold values from -6 to 6
- media_gain: float32 [2, 1024], replicated, may hold values from 0.5 to 1.5
- media_bias: float32 [2, 1024], replicated, may hold values from -1.75 to 1.75
- latent_gain: float32 [2, 1024], replicated, may hold values from 0.5 to 1.5
- latent_bias: float32 [2, 1024], replicated, may hold values from -1.75 to 1.75
- ff_gain: float32 [2, 1024], replicated, may hold values from 0.5 to 1.5
- ff_bias: float32 [2, 1024], replicated, may hold values from -1.75 to 1.75
- w_query: bfloat16 [2, 1024, 512], P(None, None, 'tensor'), may hold values from -0.375 to 0.375
- w_key: bfloat16 [2, 1024, 512], P(None, None, 'tensor'), may hold values from -0.1875 to 0.1875
- w_value: bfloat16 [2, 1024, 512], P(None, None, 'tensor'), may hold values from -0.1875 to 0.1875
- w_out: bfloat16 [2, 512, 1024], P(None, 'tensor'), may hold values from -3 to 3
- w_up: bfloat16 [2, 1024, 4096], P(None, None, 'tensor'), may hold values from -0.1875 to 0.1875
- w_down: bfloat16 [2, 4096, 1024], P(None, 'tensor'), may hold values from -0.09375 to 0.09375
- cotangent: float32 [24, 64, 1024], P('dp'), may hold values from -6 to 6
Outputs:
- resampled: float32 [24, 64, 1024], P('dp')
- media_grad: bfloat16 [24, 2048, 1024], P('dp', None, 'tensor')
- time_grad: float32 [8, 1024], replicated
- latents_grad: float32 [64, 1024], replicated
- media_gain_grad: float32 [2, 1024], replicated
- media_bias_grad: float32 [2, 1024], replicated
- latent_gain_grad: float32 [2, 1024], replicated
- latent_bias_grad: float32 [2, 1024], replicated
- ff_gain_grad: float32 [2, 1024], replicated
- ff_bias_grad: float32 [2, 1024], replicated
- w_query_grad: float32 [2, 1024, 512], P(None, 'dp', 'tensor')
- w_key_grad: float32 [2, 1024, 512], P(None, 'dp', 'tensor')
- w_value_grad: float32 [2, 1024, 512], P(None, 'dp', 'tensor')
- w_out_grad: float32 [2, 512, 1024], P(None, 'tensor', 'dp')
- w_up_grad: float32 [2, 1024, 4096], P(None, 'dp', 'tensor')
- w_down_grad: float32 [2, 4096, 1024], P(None, 'tensor', 'dp')
The draws below stay inside these ranges and needn't reach their ends.
Inputs may be any that keep to these rules, and one draw needn't show every extreme that they name: `frame_counts`: frames of each clip; in every draw some clip has 8 frames and some clip has 1.
All inputs are finite; a program needn't handle non-finite values.
Results may differ from the reference program's by a relative error of at most 0.02.
The reference program's roundings to bfloat16 on the way count: a program that leaves them out, or rounds other values in their place, can miss the bound.
Values sent between devices are 32-bit elements; how exact they have to be, the bound alone decides.
A program may use at most 256 MiB of HBM per device.

```python
import jax
import jax.numpy as jnp
from jax import lax

D = 1024
HEAD_DIM = 64
FF = 4096
LATENTS = 64
FRAMES = 8
PATCH = 256
LAYERS = 2
INNER = 512
MEDIA = 2048
SAMPLES = 24


def draw_frame_counts(key, part):
    key = jax.random.fold_in(key, 11)
    first_key, second_key, third_key = jax.random.split(key, 3)
    counts = jax.random.randint(first_key, (SAMPLES,), 1, FRAMES + 1)
    longest = jax.random.randint(second_key, (), 0, SAMPLES)
    offset = jax.random.randint(third_key, (), 1, SAMPLES)
    shortest = (longest + offset) % SAMPLES
    counts = counts.at[longest].set(FRAMES)
    counts = counts.at[shortest].set(1)
    return counts.astype(jnp.int32)


def steps_of(stream_key, shape, pieces, low, top_value):
    gain = 1.0
    for dim, parts in pieces:
        draws = jax.random.uniform(jax.random.fold_in(jax.random.fold_in(stream_key, 6), dim), (parts,), jnp.float32, low / len(pieces), top_value / len(pieces))
        gain = gain * jnp.repeat(jnp.exp(draws), shape[dim] // parts).reshape((-1,) + (1,) * (len(shape) - 1 - dim))
    return gain


def scatter_about(rng, extent, scale, most, cuts=(), held_as=jnp.bfloat16):
    factor_of = steps_of(rng, extent, cuts, -0.22, 0.18) if cuts else 1.0
    array = jax.random.normal(rng, extent, jnp.float32) * scale * factor_of
    return jnp.minimum(jnp.maximum(array, -most), most).astype(held_as)


def setup_inputs(seed: int = 0) -> dict:
    arg_keys = jax.random.split(jax.random.key(seed), 18)
    return {
        "media": scatter_about(arg_keys[0], (SAMPLES, MEDIA, D), 1.0, 6.0, ((0, 8),)),
        "frame_counts": draw_frame_counts(jax.random.fold_in(arg_keys[17], 71), 0),
        "time_embed": scatter_about(arg_keys[2], (FRAMES, D), 0.5, 3.0),
        "latents": scatter_about(arg_keys[3], (LATENTS, D), 1.0, 6.0),
        "media_gain": jnp.clip(1.0 + 0.1 * jax.random.normal(arg_keys[4], (LAYERS, D), jnp.float32), 0.5, 1.5),
        "media_bias": scatter_about(arg_keys[5], (LAYERS, D), 0.3, 1.75, (), jnp.float32),
        "latent_gain": jnp.clip(1.0 + 0.1 * jax.random.normal(arg_keys[6], (LAYERS, D), jnp.float32), 0.5, 1.5),
        "latent_bias": scatter_about(arg_keys[7], (LAYERS, D), 0.3, 1.75, (), jnp.float32),
        "ff_gain": jnp.clip(1.0 + 0.1 * jax.random.normal(arg_keys[8], (LAYERS, D), jnp.float32), 0.5, 1.5),
        "ff_bias": scatter_about(arg_keys[9], (LAYERS, D), 0.3, 1.75, (), jnp.float32),
        "w_query": scatter_about(arg_keys[10], (LAYERS, D, INNER), (D // 4) ** -0.5, 0.375, ((2, 4),)),
        "w_key": scatter_about(arg_keys[11], (LAYERS, D, INNER), D ** -0.5, 0.1875, ((2, 4),)),
        "w_value": scatter_about(arg_keys[12], (LAYERS, D, INNER), D ** -0.5, 0.1875, ((2, 4),)),
        "w_out": scatter_about(arg_keys[13], (LAYERS, INNER, D), 0.5, 3.0, ((1, 4),)),
        "w_up": scatter_about(arg_keys[14], (LAYERS, D, FF), D ** -0.5, 0.1875, ((2, 4),)),
        "w_down": scatter_about(arg_keys[15], (LAYERS, FF, D), FF ** -0.5, 0.09375, ((1, 4),)),
        "cotangent": scatter_about(arg_keys[16], (SAMPLES, LATENTS, D), 1.0, 6.0, ((0, 8),), jnp.float32),
    }


@jax.custom_vjp
def low(v):
    return lax.optimization_barrier(v.astype(jnp.bfloat16)).astype(jnp.float32)

@jax.custom_vjp
def low_back(v):
    return v

def low_keep(v):
    return (low(v), None)

def low_pass(kept, grad):
    return (grad,)

def back_keep(v):
    return (v, None)

def back_low(kept, grad):
    return (low(grad),)
low.defvjp(low_keep, low_pass)
low_back.defvjp(back_keep, back_low)
EPS = 1e-05

def normalize(values, gain_row, bias_row):
    row_mean = lax.optimization_barrier(jnp.mean(values, axis=-1, keepdims=True))
    centered = values - row_mean
    inv_std = lax.rsqrt(lax.optimization_barrier(jnp.mean(centered * centered, axis=-1, keepdims=True)) + EPS)
    return centered * inv_std * gain_row + bias_row

def rounded(values):
    return low_back(low(values))

def project(values, weight):
    return jnp.einsum('srd,dc->src', values, weight, precision=lax.Precision.HIGHEST)

def one_layer(state, media_in, key_live, params):
    gain_media, bias_media, gain_latent, bias_latent, gain_ff, bias_ff, query_w, key_w, value_w, out_w, up_w, down_w = params
    group, latent_rows, model_width = state.shape
    head_count = query_w.shape[1] // HEAD_DIM
    media_x = low(normalize(media_in, gain_media, bias_media))
    latent_x = low(normalize(state, gain_latent, bias_latent))
    queries = rounded(project(latent_x, query_w))
    kv_input = jnp.concatenate([media_x, latent_x], axis=1)
    keys_all = rounded(project(kv_input, key_w))
    values_all = rounded(project(kv_input, value_w))
    key_count = kv_input.shape[1]
    query_heads = queries.reshape(group, latent_rows, head_count, HEAD_DIM)
    key_heads = keys_all.reshape(group, key_count, head_count, HEAD_DIM)
    value_heads = values_all.reshape(group, key_count, head_count, HEAD_DIM)
    scores = low_back(jnp.einsum('sqhd,skhd->shqk', query_heads, key_heads, precision=lax.Precision.HIGHEST) * HEAD_DIM ** (-0.5))
    scores = jnp.where(key_live[:, None, None, :], scores, -1e+30)
    attn_probs = jax.nn.softmax(scores, axis=-1)
    attended = jnp.einsum('shqk,skhd->sqhd', low(attn_probs), value_heads, precision=lax.Precision.HIGHEST)
    attended = rounded(attended.reshape(group, latent_rows, head_count * HEAD_DIM))
    middle = state + low_back(project(attended, out_w))
    ff_x = low(normalize(middle, gain_ff, bias_ff))
    hidden = low(jax.nn.gelu(low_back(project(ff_x, up_w)), approximate=False))
    return middle + low_back(project(hidden, down_w))

def reference(media, frame_counts, time_embed, latents, media_gain, media_bias, latent_gain, latent_bias, ff_gain, ff_bias, w_query, w_key, w_value, w_out, w_up, w_down, cotangent):
    position = jnp.arange(MEDIA + LATENTS)

    def forward(media_f, time_f, latents_f, *layer_params):
        group_media = media_f.reshape(SAMPLES // 2, 2, MEDIA, D)
        group_counts = frame_counts.reshape(SAMPLES // 2, 2)
        time_rows = jnp.repeat(time_f, PATCH, axis=0)

        def run_group(inputs):
            media_grp, counts_grp = inputs
            media_in = media_grp + time_rows[None]
            key_live = (position[None, :] >= MEDIA) | (position[None, :] // PATCH < counts_grp[:, None])
            state = jnp.broadcast_to(latents_f[None], (2, LATENTS, D))
            for depth in range(LAYERS):
                state = one_layer(state, media_in, key_live, tuple((member[depth] for member in layer_params)))
            return state
        result = lax.map(jax.checkpoint(run_group), (group_media, group_counts))
        return result.reshape(SAMPLES, LATENTS, D)
    inputs = (media.astype(jnp.float32), time_embed.astype(jnp.float32), latents.astype(jnp.float32), media_gain, media_bias, latent_gain, latent_bias, ff_gain, ff_bias, w_query.astype(jnp.float32), w_key.astype(jnp.float32), w_value.astype(jnp.float32), w_out.astype(jnp.float32), w_up.astype(jnp.float32), w_down.astype(jnp.float32))
    resampled, pullback = jax.vjp(forward, *inputs)
    grads = pullback(cotangent)
    return (resampled, grads[0].astype(jnp.bfloat16), grads[1], grads[2], grads[3], grads[4], grads[5], grads[6], grads[7], grads[8], grads[9], grads[10], grads[11], grads[12], grads[13], grads[14])
```

```python
import jax
import jax.numpy as jnp
from jax import lax
from jax.sharding import PartitionSpec as P

HEAD_DIM = 64
EPS = 1e-05
F32 = jnp.float32
BF16 = jnp.bfloat16


def normalize(values):
    row_mean = jnp.mean(values, axis=-1, keepdims=True)
    centered = values - row_mean
    inv_std = lax.rsqrt(jnp.mean(centered * centered, axis=-1, keepdims=True) + EPS)
    return (centered * inv_std, inv_std)


def norm_back(grad_out, gain_row, normed, inv_std):
    scaled = grad_out * gain_row
    return inv_std * (
        scaled
        - jnp.mean(scaled, axis=-1, keepdims=True)
        - normed * jnp.mean(scaled * normed, axis=-1, keepdims=True)
    )


def mm(left_side, right_side):
    return jnp.dot(left_side, right_side, preferred_element_type=F32)


def mm_bt(left_side, right_side):
    return lax.dot_general(left_side, right_side, (((1,), (1,)), ((), ())), preferred_element_type=F32)


def mm_at(left_side, right_side):
    return lax.dot_general(left_side, right_side, (((0,), (0,)), ((), ())), preferred_element_type=F32)


def gelu_slope(values):
    return (
        0.5 * (1.0 + lax.erf(values * 0.7071067811865476))
        + values * jnp.exp(-0.5 * values * values) * 0.3989422804014327
    )


class Links:

    def __init__(self, zero):
        self.zero = zero
        self.tensor_size = lax.axis_size("tensor")
        self.dp_size = lax.axis_size("dp")
        self.groups = self.tensor_size // 2
        self.planes = self.dp_size // 2
        tensor_at = lax.axis_index("tensor")
        dp_at = lax.axis_index("dp")
        self.core = lax.rem(tensor_at, 2)
        self.group = lax.div(tensor_at, 2)
        self.side = lax.rem(dp_at, 2)
        self.plane = lax.div(dp_at, 2)

    def arrive(self, value):
        return value + self.zero

    def core_swap(self, value):
        return lax.ppermute(value, "tensor", [(i, i ^ 1) for i in range(self.tensor_size)])

    def group_turn(self, value, turn):
        size = self.tensor_size
        return lax.ppermute(value, "tensor", [(i, (i + 2 * turn) % size) for i in range(size)])

    def side_swap(self, value):
        return lax.ppermute(value, "dp", [(i, i ^ 1) for i in range(self.dp_size)])

    def cut(self, value, index):
        half = value.shape[0] // 2
        return lax.dynamic_slice_in_dim(value, index * half, half, 0)

    def join(self, mine, other, index):
        first = index == 0
        return jnp.concatenate([jnp.where(first, mine, other), jnp.where(first, other, mine)], axis=0)

    def group_sum(self, value):
        if self.groups == 2:
            return value + self.group_turn(value, 1)
        turned = jnp.stack([value] + [self.group_turn(value, k) for k in range(1, self.groups)])
        total = None
        for source in range(self.groups):
            slot = lax.rem(self.group - source + self.groups, self.groups)
            term = lax.dynamic_index_in_dim(turned, slot, 0, keepdims=False)
            total = term if total is None else total + term
        return total

    def core_sum(self, value):
        return value + self.core_swap(value)

    def tensor_sum(self, value):
        mine = self.cut(value, self.core) + self.core_swap(self.cut(value, 1 - self.core))
        mine = self.group_sum(mine)
        return self.join(mine, self.core_swap(mine), self.core)

    def dp_sum(self, value):
        step = 1
        while step < self.dp_size:
            value = value + lax.ppermute(value, "dp", [(i, i ^ step) for i in range(self.dp_size)])
            step *= 2
        return value

    def line_scatter(self, partial):
        planes = self.planes
        chain = {}
        for way in (1, -1):
            place = self.plane if way == 1 else planes - 1 - self.plane
            arrived = None
            for step in range(1, planes):
                index = jnp.minimum(planes - step + place, planes - 1)
                if way == -1:
                    index = planes - 1 - index
                share = partial(index)
                if arrived is not None:
                    share = share + arrived
                pairs = []
                for at in range(step):
                    source, target = at, at + 1
                    if way == -1:
                        source, target = planes - 1 - source, planes - 1 - target
                    pairs += [(2 * source + s, 2 * target + s) for s in range(2)]
                arrived = lax.ppermute(share, "dp", pairs)
            chain[way] = arrived
        return partial(self.plane) + chain[1] + chain[-1]

    def side_rows(self, value):
        value = value.astype(F32)
        return jnp.concatenate([value.astype(BF16), self.arrive(self.side_swap(value)).astype(BF16)], axis=0)

    def side_columns(self, value):
        rows, width = value.shape
        split = value.astype(F32).reshape(rows, self.planes, 2, width // self.dp_size)
        mine = lax.dynamic_index_in_dim(split, self.side, 2, keepdims=False)
        theirs = lax.dynamic_index_in_dim(split, 1 - self.side, 2, keepdims=False)
        half = self.side_swap(self.cut(theirs, self.core))
        other = self.arrive(self.join(half, self.core_swap(half), self.core))
        both = jnp.concatenate([mine.astype(BF16), other.astype(BF16)], axis=0)
        return jnp.transpose(both, (1, 0, 2))


def local(
    media,
    frame_counts,
    time_embed,
    latents,
    media_gain,
    media_bias,
    latent_gain,
    latent_bias,
    ff_gain,
    ff_bias,
    w_query,
    w_key,
    w_value,
    w_out,
    w_up,
    w_down,
    cotangent,
):
    links = Links(jnp.where(frame_counts[0] > 1000000, 1.0, 0.0).astype(F32))
    samples, media_len, width = media.shape
    frames = time_embed.shape[0]
    patches = media_len // frames
    latent_rows = latents.shape[0]
    own = w_query.shape[2]
    layers = w_query.shape[0]
    wide = own * links.groups
    heads = wide // HEAD_DIM
    key_count = media_len + latent_rows
    score_scale = HEAD_DIM ** (-0.5)
    rows = samples * latent_rows

    def gather(weight):
        mine = weight.astype(F32)
        half = links.cut(mine, links.side)
        parts = [weight]
        for turn in range(1, links.groups):
            arrived = links.group_turn(half, turn)
            parts.append(links.arrive(links.join(arrived, links.side_swap(arrived), links.side)).astype(BF16))
        return parts

    query4, key4, value4, out4 = [], [], [], []
    for depth in range(layers):
        parts = gather(jnp.concatenate([w_key[depth], w_value[depth]], axis=1))
        key4.append(jnp.concatenate([p[:, :own] for p in parts], axis=1))
        value4.append(jnp.concatenate([p[:, own:] for p in parts], axis=1))
        parts = gather(jnp.concatenate([w_query[depth], w_out[depth].T], axis=1))
        query4.append(jnp.concatenate([p[:, :own] for p in parts], axis=1))
        out4.append(jnp.concatenate([p[:, own:] for p in parts], axis=1))
    pair4 = [jnp.concatenate([key4[l], value4[l]], axis=1) for l in range(layers)]

    media_in = (
        media.astype(F32).reshape(samples, frames, patches, width)
        + time_embed.astype(F32)[None, :, None, :]
    ).reshape(samples * media_len, width)
    media_normed, media_rstd = normalize(media_in)
    position = lax.broadcasted_iota(jnp.int32, (samples, key_count), 1)
    key_live = (position >= media_len) | (position // patches < frame_counts[:, None])
    key_mask = key_live[:, None, None, :]
    state = jnp.broadcast_to(latents.astype(F32)[None], (samples, latent_rows, width)).reshape(rows, width)

    def heads_of(value):
        return value.reshape(samples, -1, heads, HEAD_DIM)

    def score_block(queries, keys):
        scores = jnp.einsum("sqhd,skhd->shqk", heads_of(queries), keys, preferred_element_type=F32)
        return jnp.where(key_mask, scores * score_scale, -1e30)

    media_x = [(media_normed * media_gain[l] + media_bias[l]).astype(BF16) for l in range(layers)]
    media_pair = [mm(media_x[l], pair4[l]).astype(BF16) for l in range(layers)]

    saved = []
    for depth in range(layers):
        latent_normed, latent_rstd = normalize(state)
        latent_x = (latent_normed * latent_gain[depth] + latent_bias[depth]).astype(BF16)
        queries = mm(latent_x, query4[depth]).astype(BF16)
        latent_pair = mm(latent_x, pair4[depth]).astype(BF16)
        pair = jnp.concatenate(
            [media_pair[depth].reshape(samples, media_len, -1), latent_pair.reshape(samples, latent_rows, -1)], axis=1
        )
        keys, values = heads_of(pair[..., :wide]), heads_of(pair[..., wide:])
        scores = score_block(queries, keys)
        row_max = jnp.max(scores, axis=-1, keepdims=True)
        exp_scores = jnp.exp(scores - row_max)
        row_total = jnp.sum(exp_scores, axis=-1, keepdims=True)
        probs = exp_scores / row_total
        log_total = row_max + jnp.log(row_total)
        attended = jnp.einsum("shqk,skhd->sqhd", probs.astype(BF16), values, preferred_element_type=F32)
        attended = attended.astype(BF16).reshape(rows, wide)
        middle = state + links.core_sum(mm_bt(attended, out4[depth]))
        ff_normed, ff_rstd = normalize(middle)
        ff_x = (ff_normed * ff_gain[depth] + ff_bias[depth]).astype(BF16)
        up_pre = mm(ff_x, w_up[depth])
        hidden = jax.nn.gelu(up_pre, approximate=False).astype(BF16)
        state = middle + links.tensor_sum(mm(hidden, w_down[depth]))
        saved.append(
            (latent_normed, latent_rstd, latent_x, queries, keys, values, log_total, attended,
             ff_normed, ff_rstd, ff_x, up_pre, hidden)
        )

    upstream = cotangent.reshape(rows, width)
    grads = [None] * layers
    gains = [None] * layers
    pair_grads = [None] * layers
    for depth in reversed(range(layers)):
        (latent_normed, latent_rstd, latent_x, queries, keys, values, log_total, attended,
         ff_normed, ff_rstd, ff_x, up_pre, hidden) = saved[depth]
        upstream_low = upstream.astype(BF16)
        down_left = links.side_rows(hidden)
        down_right = links.side_columns(upstream_low)
        grad_down = links.line_scatter(lambda i: mm_at(down_left, lax.dynamic_index_in_dim(down_right, i, 0, keepdims=False)))
        grad_pre = (mm_bt(upstream_low, w_down[depth]) * gelu_slope(up_pre)).astype(BF16)
        up_left = links.side_columns(ff_x)
        up_right = links.side_rows(grad_pre)
        grad_up = links.line_scatter(lambda i: mm_at(lax.dynamic_index_in_dim(up_left, i, 0, keepdims=False), up_right))
        grad_ffx = links.tensor_sum(mm_bt(grad_pre, w_up[depth]))
        grad_middle = upstream + norm_back(grad_ffx, ff_gain[depth], ff_normed, ff_rstd)
        middle_low = grad_middle.astype(BF16)
        grad_att = mm(middle_low, out4[depth]).astype(BF16)
        grad_heads = heads_of(grad_att)
        probs = jnp.exp(score_block(queries, keys) - log_total)
        grad_probs = jnp.einsum("sqhd,skhd->shqk", grad_heads, values, preferred_element_type=F32)
        row_delta = jnp.sum(probs * grad_probs, axis=-1, keepdims=True)
        grad_scores = (probs * (grad_probs - row_delta)).astype(BF16)
        grad_query = (
            jnp.einsum("shqk,skhd->sqhd", grad_scores, keys, preferred_element_type=F32) * score_scale
        ).astype(BF16).reshape(rows, wide)
        grad_key = (
            jnp.einsum("shqk,sqhd->skhd", grad_scores, heads_of(queries), preferred_element_type=F32) * score_scale
        ).astype(BF16).reshape(samples, key_count, wide)
        grad_value = jnp.einsum(
            "shqk,sqhd->skhd", probs.astype(BF16), grad_heads, preferred_element_type=F32
        ).astype(BF16).reshape(samples, key_count, wide)
        grad_pair = jnp.concatenate([grad_key, grad_value], axis=-1)
        media_pair_grad = grad_pair[:, :media_len].reshape(samples * media_len, 2 * wide)
        latent_pair_grad = grad_pair[:, media_len:].reshape(rows, 2 * wide)
        pair_grads[depth] = media_pair_grad
        grad_latx = links.core_sum(mm_bt(grad_query, query4[depth]) + mm_bt(latent_pair_grad, pair4[depth]))

        def own_pair(value):
            return jnp.concatenate([value[:, :own], value[:, wide:wide + own]], axis=1)

        media_own = own_pair(media_pair_grad)
        media_w = mm_at(media_x[depth], media_own)
        latent_w = mm_at(latent_x, jnp.concatenate([own_pair(latent_pair_grad), grad_query[:, :own]], axis=1))
        out_w = mm_at(middle_low, attended[:, :own])
        sums = jnp.sum(media_own.astype(F32), axis=0)
        weight_own = jnp.concatenate([w_key[depth], w_value[depth]], axis=1).astype(F32)
        media_gain_part = jnp.sum(weight_own * (media_w - media_bias[depth][:, None] * sums), axis=1) / media_gain[depth]
        media_bias_part = jnp.sum(weight_own * sums, axis=1)
        attn_w = jnp.concatenate([media_w + latent_w[:, :2 * own], latent_w[:, 2 * own:], out_w], axis=1)
        split = attn_w.reshape(links.planes, 2, width // links.dp_size, 4 * own)
        halves = lax.dynamic_index_in_dim(split, links.side, 1, keepdims=False) + links.side_swap(
            lax.dynamic_index_in_dim(split, 1 - links.side, 1, keepdims=False)
        )
        grad_attn = links.line_scatter(lambda i: lax.dynamic_index_in_dim(halves, i, 0, keepdims=False))
        grads[depth] = (grad_attn, grad_up, grad_down)
        upstream = grad_middle + norm_back(grad_latx, latent_gain[depth], latent_normed, latent_rstd)
        share = 1.0 / links.tensor_size
        gains[depth] = (
            media_gain_part,
            media_bias_part,
            jnp.sum(grad_latx * latent_normed, axis=0) * share,
            jnp.sum(grad_latx, axis=0) * share,
            jnp.sum(grad_ffx * ff_normed, axis=0) * share,
            jnp.sum(grad_ffx, axis=0) * share,
        )

    chip_width = width // links.groups
    core_width = width // links.tensor_size

    def chip_columns(value):
        return lax.dynamic_slice_in_dim(value, links.group * chip_width, chip_width, value.ndim - 1)

    total = 0.0
    mean_one = 0.0
    mean_two = 0.0
    for depth in range(layers):
        grad_pair = pair_grads[depth]
        weight = pair4[depth]
        weight_chip = lax.dynamic_slice_in_dim(weight, links.group * chip_width, chip_width, 0)
        total = total + mm_bt(grad_pair, weight_chip) * chip_columns(media_gain[depth])
        weight_long = weight.astype(F32)
        gain_mean = jnp.sum(weight_long * media_gain[depth][:, None], axis=0) / width
        bias_mean = jnp.sum(weight_long * media_bias[depth][:, None], axis=0)
        grad_long = grad_pair.astype(F32)
        mean_one = mean_one + jnp.sum(grad_long * gain_mean, axis=1, keepdims=True)
        mean_two = mean_two + jnp.sum(
            grad_long * (media_pair[depth].astype(F32) - bias_mean), axis=1, keepdims=True
        ) / width
    media_part = media_rstd * (total - mean_one - chip_columns(media_normed) * mean_two)
    mine = lax.dynamic_slice_in_dim(media_part, links.core * core_width, core_width, 1)
    theirs = lax.dynamic_slice_in_dim(media_part, (1 - links.core) * core_width, core_width, 1)
    media_total = mine + links.core_swap(theirs)
    media_grad = media_total.astype(BF16).reshape(samples, media_len, core_width)
    time_part = jnp.sum(media_total.reshape(samples, frames, patches, core_width), axis=(0, 2))

    latent_part = jnp.sum(upstream.reshape(samples, latent_rows, width), axis=0)
    tensor_at = lax.axis_index("tensor")
    latent_share = lax.dynamic_slice_in_dim(latent_part, tensor_at * core_width, core_width, 1)
    gain_flat = jnp.stack([jnp.stack([gains[l][m] for l in range(layers)]) for m in range(6)]).reshape(6 * layers, width)
    gain_split = gain_flat.reshape(6 * layers, links.groups, 2, core_width)
    core_mine = lax.dynamic_index_in_dim(gain_split, links.core, 2, keepdims=False)
    core_theirs = lax.dynamic_index_in_dim(gain_split, 1 - links.core, 2, keepdims=False)
    gain_share = core_mine + links.core_swap(core_theirs)
    gain_sum = lax.dynamic_index_in_dim(gain_share, links.group, 1, keepdims=False)
    for turn in range(1, links.groups):
        target = lax.rem(links.group + turn, links.groups)
        gain_sum = gain_sum + links.group_turn(lax.dynamic_index_in_dim(gain_share, target, 1, keepdims=False), turn)
    small = links.dp_sum(jnp.concatenate([gain_sum, time_part, latent_share], axis=0))
    by_core = jnp.stack([small, links.core_swap(small)])
    by_core = jnp.where(links.core == 0, by_core, by_core[::-1])
    turned = jnp.stack([by_core] + [links.group_turn(by_core, k) for k in range(1, links.groups)])
    order = lax.rem(links.group - jnp.arange(links.groups) + links.groups, links.groups)
    ordered = jnp.take(turned, order, axis=0)
    small_all = jnp.transpose(ordered, (2, 0, 1, 3)).reshape(small.shape[0], width)
    gain_all = small_all[: 6 * layers].reshape(6, layers, width)
    time_grad = small_all[6 * layers : 6 * layers + frames]
    latents_grad = small_all[6 * layers + frames :]

    attn = jnp.stack([grads[l][0] for l in range(layers)])
    return (
        state.reshape(samples, latent_rows, width),
        media_grad,
        time_grad,
        latents_grad,
        gain_all[0],
        gain_all[1],
        gain_all[2],
        gain_all[3],
        gain_all[4],
        gain_all[5],
        attn[..., 2 * own : 3 * own],
        attn[..., :own],
        attn[..., own : 2 * own],
        jnp.transpose(attn[..., 3 * own :], (0, 2, 1)),
        jnp.stack([grads[l][1] for l in range(layers)]),
        jnp.stack([grads[l][2] for l in range(layers)]),
    )


def solution(mesh):
    in_specs = (
        P("dp", None, None),
        P("dp"),
        P(),
        P(),
        P(),
        P(),
        P(),
        P(),
        P(),
        P(),
        P(None, None, "tensor"),
        P(None, None, "tensor"),
        P(None, None, "tensor"),
        P(None, "tensor", None),
        P(None, None, "tensor"),
        P(None, "tensor", None),
        P("dp", None, None),
    )
    out_specs = (
        P("dp", None, None),
        P("dp", None, "tensor"),
        P(),
        P(),
        P(),
        P(),
        P(),
        P(),
        P(),
        P(),
        P(None, "dp", "tensor"),
        P(None, "dp", "tensor"),
        P(None, "dp", "tensor"),
        P(None, "tensor", "dp"),
        P(None, "dp", "tensor"),
        P(None, "tensor", "dp"),
    )
    return jax.shard_map(local, mesh=mesh, in_specs=in_specs, out_specs=out_specs, check_vma=False)
```

```python
import jax
import jax.numpy as jnp
from jax import lax
from jax.experimental import pallas as pl
from jax.experimental.pallas import tpu as pltpu
from jax.sharding import PartitionSpec as P

HEAD_DIM = 64
EPS = 1e-05
F32 = jnp.float32
BF16 = jnp.bfloat16
VMEM_LIMIT = 62 * 1024 * 1024


def mm(left_side, right_side):
    return jnp.dot(left_side, right_side, preferred_element_type=F32)


def mm_bt(left_side, right_side):
    return lax.dot_general(left_side, right_side, (((1,), (1,)), ((), ())), preferred_element_type=F32)


def mm_at(left_side, right_side):
    return lax.dot_general(left_side, right_side, (((0,), (0,)), ((), ())), preferred_element_type=F32)


def dot_rows(left_side, right_side):
    return lax.dot_general(left_side, right_side, (((0,), (0,)), ((), ())), preferred_element_type=F32)


def row_norm(values):
    count = values.shape[-1]
    mean = jnp.sum(values, axis=-1, keepdims=True) * (1.0 / count)
    centered = values - mean
    rstd = lax.rsqrt(jnp.sum(centered * centered, axis=-1, keepdims=True) * (1.0 / count) + EPS)
    return centered * rstd, mean, rstd


def row_norm_back(grad, gain, normed, rstd):
    count = grad.shape[-1]
    scaled = grad * gain
    mean_one = jnp.sum(scaled, axis=-1, keepdims=True) * (1.0 / count)
    mean_two = jnp.sum(scaled * normed, axis=-1, keepdims=True) * (1.0 / count)
    return rstd * (scaled - mean_one - normed * mean_two)


def whole(shape):
    zeros = (0,) * len(shape)
    return pl.BlockSpec(shape, lambda *_: zeros)


def call(body, scalars, grid, ins, outs, scratch, name, flops, moved, exps=0, aliases=None):
    return pl.pallas_call(
        body,
        out_shape=[jax.ShapeDtypeStruct(shape, dtype) for shape, dtype, _ in outs],
        grid_spec=pltpu.PrefetchScalarGridSpec(
            num_scalar_prefetch=len(scalars),
            grid=grid,
            in_specs=[spec for _, spec in ins],
            out_specs=[spec for _, _, spec in outs],
            scratch_shapes=scratch,
        ),
        compiler_params=pltpu.CompilerParams(
            dimension_semantics=("arbitrary",) * len(grid), vmem_limit_bytes=VMEM_LIMIT
        ),
        cost_estimate=pl.CostEstimate(flops=flops, bytes_accessed=moved, transcendentals=exps),
        name=name,
        input_output_aliases=aliases or {},
    )(*scalars, *[array for array, _ in ins])


def frames_in_block(frames):
    return 4 if frames % 4 == 0 else 1


def live_block(group, groups):
    def block(clip, at, counts_ref, *_):
        return (clip * groups + jnp.minimum(at, (counts_ref[clip] - 1) // group), 0)

    return block


def pack(place, wanted, name):
    ins, outs, counts = [], [], []
    for weights, depth, halved in wanted:
        count = weights[0].shape[1] // (2 if halved else 1)
        for weight in weights:
            spec = lambda i, place_ref, depth=depth, halved=halved: (depth, place_ref[2] if halved else 0, 0)
            ins.append((weight, pl.BlockSpec((None, count, weight.shape[2]), spec)))
        shape = (count, sum(weight.shape[2] for weight in weights))
        outs.append((shape, F32, whole(shape)))
        counts.append(len(weights))

    def body(place_ref, *refs):
        in_refs, out_refs = list(refs[: len(ins)]), refs[len(ins) :]
        for out_ref, count in zip(out_refs, counts):
            at = 0
            for _ in range(count):
                part = in_refs.pop(0)
                out_ref[:, at : at + part.shape[1]] = part[...].astype(F32)
                at += part.shape[1]

    moved = sum(6 * shape[0] * shape[1] for shape, _, _ in outs)
    return call(body, [place], (1,), ins, outs, [], name, moved, moved)


def keep_rows(ref, first, columns, side, near, far):
    if far is None:
        ref[first : first + near.shape[0], columns] = near[...].astype(BF16)
        return
    half = near.shape[0]
    ref[pl.ds(pl.multiple_of(first + side * half, half), half), columns] = near[...].astype(BF16)
    ref[pl.ds(pl.multiple_of(first + (1 - side) * half, half), half), columns] = far[...].astype(BF16)


class Gathered:

    def __init__(self, value, groups, turn):
        self.value = value
        self.groups = groups
        self.turn = turn
        self.shape = (value.shape[0] // groups, value.shape[1])

    def spec(self):
        def block(*at):
            return (lax.rem(at[-1][1] + self.groups - self.turn, self.groups), 0)

        return pl.BlockSpec(self.shape, block)


def with_spec(value):
    if isinstance(value, Gathered):
        return (value.value, value.spec())
    return (value, whole(value.shape))


def prepare(media, counts, time_rows, gain, bias, w_key, w_value, depth, turns, frames, patches):
    rows, width = media.shape
    samples = counts.shape[0]
    own = w_key.shape[2]
    group = frames_in_block(frames)
    groups = frames // group

    def body(counts_ref, media_ref, time_ref, gain_ref, bias_ref, wk_ref, wv_ref, x_ref, stat_ref, pair_ref, weight_ref):
        clip, at = pl.program_id(0), pl.program_id(1)

        @pl.when((clip == 0) & (at == 0))
        def _():
            weight_ref[...] = jnp.concatenate([wk_ref[...], wv_ref[...]], axis=1)

        for inner in range(group):
            frame = at * group + inner
            here = slice(inner * patches, (inner + 1) * patches)

            @pl.when(frame < counts_ref[clip])
            def _():
                values = media_ref[here, :].astype(F32) + time_ref[pl.ds(frame, 1), :]
                normed, mean, rstd = row_norm(values)
                x = (normed * gain_ref[...] + bias_ref[...]).astype(BF16)
                x_ref[here, :] = x
                lane = lax.broadcasted_iota(jnp.int32, (patches, 128), 1)
                stat_ref[here, :] = jnp.where(lane < 64, mean, rstd)
                pair_ref[here, :] = jnp.dot(x, weight_ref[...], preferred_element_type=F32).astype(BF16)

            @pl.when((frame >= counts_ref[clip]) & (at * group < counts_ref[clip]))
            def _():
                x_ref[here, :] = jnp.zeros((patches, width), BF16)
                pair_ref[here, :] = jnp.zeros((patches, 2 * own), BF16)

    block = live_block(group, groups)
    deep = group * patches
    row_spec = pl.BlockSpec((deep, width), block)
    weight_spec = pl.BlockSpec((None, width, own), lambda *_: (depth, 0, 0))
    return call(
        body, [counts], (samples, groups),
        [(media, row_spec), (time_rows, whole(time_rows.shape)), (gain, whole(gain.shape)), (bias, whole(bias.shape)),
         (w_key, weight_spec), (w_value, weight_spec)],
        [((rows, width), BF16, row_spec), ((rows, 128), F32, pl.BlockSpec((deep, 128), block)),
         ((rows, 2 * own * turns), BF16, pl.BlockSpec((deep, 2 * own), block)),
         ((width, 2 * own), BF16, whole((width, 2 * own)))],
        [], "prepare", 2 * rows * width * 2 * own, rows * width * 4,
    )


def project_more(media_x, counts, place, pair, near, far, turn, frames, patches):
    rows, width = media_x.shape
    wide = near.shape[1]
    group = frames_in_block(frames)
    groups = frames // group
    parts = 1 if far is None else 2

    def body(counts_ref, place_ref, x_ref, pair_in_ref, *refs):
        out_ref, weight_ref = refs[parts:]
        clip, at = pl.program_id(0), pl.program_id(1)

        @pl.when((clip == 0) & (at == 0))
        def _():
            keep_rows(weight_ref, 0, slice(None), place_ref[2], refs[0], refs[1] if parts == 2 else None)

        for inner in range(group):
            frame = at * group + inner
            here = slice(inner * patches, (inner + 1) * patches)

            @pl.when(frame < counts_ref[clip])
            def _():
                out_ref[here, :] = jnp.dot(x_ref[here, :], weight_ref[...], preferred_element_type=F32).astype(BF16)

            @pl.when((frame >= counts_ref[clip]) & (at * group < counts_ref[clip]))
            def _():
                out_ref[here, :] = jnp.zeros((patches, wide), BF16)

    block = live_block(group, groups)
    deep = group * patches
    halves = [near] if far is None else [near, far]
    return call(
        body, [counts, place], (counts.shape[0], groups),
        [(media_x, pl.BlockSpec((deep, width), block)), (pair, pl.BlockSpec(memory_space=pl.ANY))]
        + [with_spec(half) for half in halves],
        [(pair.shape, BF16, pl.BlockSpec((deep, wide), lambda clip, at, counts_ref, *_: (block(clip, at, counts_ref)[0], turn))),
         ((width, wide), BF16, whole((width, wide)))],
        [], "project_more", 2 * rows * width * wide, 2 * rows * (width + wide), aliases={3: 0},
    )


def spread(rows_of_heads, heads):
    rows, wide = rows_of_heads.shape
    tiled = jnp.concatenate([rows_of_heads] * heads, axis=0)
    head_row = lax.broadcasted_iota(jnp.int32, tiled.shape, 0) // rows
    head_col = lax.broadcasted_iota(jnp.int32, tiled.shape, 1) // (wide // heads)
    return jnp.where(head_row == head_col, tiled, jnp.zeros_like(tiled))


def collect(blocks, heads):
    rows = blocks.shape[0] // heads
    head_col = lax.broadcasted_iota(jnp.int32, (rows, blocks.shape[1]), 1) // (blocks.shape[1] // heads)
    total = jnp.zeros((rows, blocks.shape[1]), blocks.dtype)
    for head in range(heads):
        total = jnp.where(head_col == head, blocks[head * rows : (head + 1) * rows], total)
    return total


def joined(core, mine, other):
    first = core == 0
    return jnp.concatenate([jnp.where(first, mine, other), jnp.where(first, other, mine)], axis=0)


def keys_of(ref, at, own):
    return jnp.concatenate([ref[at, first : first + own] for first in range(0, ref.shape[1], 2 * own)], axis=1)


def values_of(ref, at, own):
    return jnp.concatenate([ref[at, first + own : first + 2 * own] for first in range(0, ref.shape[1], 2 * own)], axis=1)


def attend(state_in, place, counts, gain, bias, w_query, w_out, more, w_pairs, depth, media_pair, latent_rows, frames, patches):
    rows, width = state_in[0].shape
    samples = counts.shape[0]
    own = w_query.shape[2]
    turns = len(w_pairs)
    wide = own * turns
    heads = wide // HEAD_DIM
    scale = HEAD_DIM ** (-0.5)
    media_len = frames * patches
    parts = len(state_in)
    chunk = 2 * patches

    def body(counts_ref, place_ref, *refs):
        state_refs = refs[:parts]
        gain_ref, bias_ref, wq_own_ref, wo_own_ref = refs[parts : parts + 4]
        at_more = parts + 4
        at_pairs = at_more + len(flat)
        more_refs = list(refs[at_more:at_pairs])
        wp_refs = refs[at_pairs : at_pairs + turns]
        pair_ref = refs[at_pairs + turns]
        state_ref, x_ref, q_ref, lat_ref, att_ref, log_ref, part_ref, wq_ref, wo_ref, score_ref = refs[at_pairs + turns + 1 :]
        clip = pl.program_id(0)

        @pl.when(clip == 0)
        def _():
            state = state_refs[0][...]
            if parts == 3:
                state = state + joined(place_ref[0], state_refs[1][...], state_refs[2][...])
            state_ref[...] = state
            normed, _, _ = row_norm(state)
            x = (normed * gain_ref[...] + bias_ref[...]).astype(BF16)
            x_ref[...] = x
            wq_ref[:, :own] = wq_own_ref[...]
            wo_ref[:own, :] = wo_own_ref[...]
            for turn, halves in enumerate(more, 1):
                loaded = [None if half is None else more_refs.pop(0) for half in halves]
                keep_rows(wq_ref, 0, slice(turn * own, (turn + 1) * own), place_ref[2], *loaded[:2])
                keep_rows(wo_ref, turn * own, slice(None), place_ref[2], *loaded[2:])
            q_ref[...] = jnp.dot(x, wq_ref[...], preferred_element_type=F32).astype(BF16)
            for turn in range(turns):
                lat_ref[:, 2 * own * turn : 2 * own * (turn + 1)] = jnp.dot(
                    x, wp_refs[turn][...], preferred_element_type=F32
                ).astype(BF16)

        at = pl.ds(pl.multiple_of(clip * latent_rows, latent_rows), latent_rows)
        queries = spread(q_ref[at, :], heads)
        live = counts_ref[clip] * patches
        chunks = (counts_ref[clip] + 1) // 2

        def rows_of(index):
            return pl.ds(pl.multiple_of(index * chunk, chunk), chunk)

        lat_score = mm_bt(keys_of(lat_ref, at, own), queries) * scale

        def first(index, top):
            score = mm_bt(keys_of(pair_ref, rows_of(index), own), queries) * scale
            row = index * chunk + lax.broadcasted_iota(jnp.int32, score.shape, 0)
            score = jnp.where(row < live, score, -1e30)
            score_ref[rows_of(index), :] = score
            return jnp.maximum(top, jnp.max(score, axis=0, keepdims=True))

        top = lax.fori_loop(0, chunks, first, jnp.max(lat_score, axis=0, keepdims=True))
        lat_exp = jnp.exp(lat_score - top)

        def second(index, total):
            exps = jnp.exp(score_ref[rows_of(index), :] - top)
            score_ref[rows_of(index), :] = exps
            return total + jnp.sum(exps, axis=0, keepdims=True)

        total = lax.fori_loop(0, chunks, second, jnp.sum(lat_exp, axis=0, keepdims=True))
        inverse = 1.0 / total
        log_ref[0] = jnp.broadcast_to(top + jnp.log(total), (8, wide))

        def third(index, sums):
            probs = (score_ref[rows_of(index), :] * inverse).astype(BF16)
            return sums + dot_rows(probs, values_of(pair_ref, rows_of(index), own))

        sums = lax.fori_loop(0, chunks, third, dot_rows((lat_exp * inverse).astype(BF16), values_of(lat_ref, at, own)))
        attended = collect(sums, heads)
        att_ref[...] = attended
        part_ref[...] = jnp.dot(attended.astype(BF16), wo_ref[...], preferred_element_type=F32)

    clip_rows = lambda cols, count: pl.BlockSpec((count, cols), lambda clip, *_: (clip, 0))
    flat = [half for halves in more for half in halves if half is not None]
    ins = [(value, whole(value.shape)) for value in (*state_in, gain, bias)]
    ins += [(w_query, pl.BlockSpec((None, width, own), lambda *_: (depth, 0, 0))),
            (w_out, pl.BlockSpec((None, own, width), lambda *_: (depth, 0, 0)))]
    ins += [with_spec(value) for value in (*flat, *w_pairs)]
    ins.append((media_pair, clip_rows(2 * wide, media_len)))
    outs = [
        ((rows, width), F32, whole((rows, width))),
        ((rows, width), BF16, whole((rows, width))),
        ((rows, wide), BF16, whole((rows, wide))),
        ((rows, 2 * wide), BF16, whole((rows, 2 * wide))),
        ((rows, wide), F32, clip_rows(wide, latent_rows)),
        ((samples, 8, wide), F32, pl.BlockSpec((1, 8, wide), lambda clip, *_: (clip, 0, 0))),
        ((rows, width), F32, clip_rows(width, latent_rows)),
        ((width, wide), BF16, whole((width, wide))),
        ((wide, width), BF16, whole((wide, width))),
    ]
    return call(
        body, [counts, place], (samples,), ins, outs, [pltpu.VMEM((media_len, wide), F32)], "attend",
        2 * samples * media_len * wide * wide * 3, samples * media_len * wide * 4 + 8 * width * wide + 16 * rows * width,
        samples * media_len * wide,
    )


def gelu_parts(values):
    half_more = 0.5 * (1.0 + lax.erf(values * 0.7071067811865476))
    slope = half_more + values * jnp.exp(-0.5 * values * values) * 0.3989422804014327
    return values * half_more, slope


def feed_forward(place, state, part, part_other, gain, bias, w_up, w_down, depth, cotangent=None):
    rows, width = state.shape
    units = w_up.shape[2]
    step = min(256, units)
    steps = units // step
    back = cotangent is not None
    halved = part.shape[0] < rows

    def body(place_ref, state_ref, part_ref, other_ref, gain_ref, bias_ref, up_ref, down_ref, *refs):
        if back:
            cot_ref, mid_ref, x_ref, pre_ref, hid_ref, out_ref, du_ref, dx_ref, dyb_ref = refs
        else:
            mid_ref, x_ref, pre_ref, hid_ref, out_ref = refs
        at = pl.program_id(0)

        @pl.when(at == 0)
        def _():
            if halved:
                middle = state_ref[...] + joined(place_ref[0], part_ref[...], other_ref[...])
            else:
                middle = state_ref[...] + (part_ref[...] + other_ref[...])
            mid_ref[...] = middle
            normed, _, _ = row_norm(middle)
            x_ref[...] = (normed * gain_ref[...] + bias_ref[...]).astype(BF16)
            out_ref[...] = jnp.zeros_like(out_ref)
            if back:
                dx_ref[...] = jnp.zeros_like(dx_ref)
                dyb_ref[...] = cot_ref[...].astype(BF16)

        pre = jnp.dot(x_ref[...], up_ref[...], preferred_element_type=F32)
        pre_ref[...] = pre
        hidden, slope = gelu_parts(pre)
        hidden = hidden.astype(BF16)
        hid_ref[...] = hidden.astype(F32)
        out_ref[...] += jnp.dot(hidden, down_ref[...], preferred_element_type=F32)
        if back:
            du = (mm_bt(dyb_ref[...], down_ref[...]) * slope).astype(BF16)
            du_ref[...] = du.astype(F32)
            dx_ref[...] += mm_bt(du, up_ref[...])

    full = whole((rows, width))
    columns = pl.BlockSpec((rows, step), lambda i, *_: (0, i))
    ins = [(value, whole(value.shape)) for value in (state, part, part_other, gain, bias)]
    ins += [(w_up, pl.BlockSpec((None, width, step), lambda i, *_: (depth, 0, i))), (w_down, pl.BlockSpec((None, step, width), lambda i, *_: (depth, i, 0)))]
    outs = [
        ((rows, width), F32, full),
        ((rows, width), BF16, full),
        ((rows, units), F32, columns),
        ((rows, units), F32, columns),
        ((rows, width), F32, full),
    ]
    scratch = []
    if back:
        ins.append((cotangent, full))
        outs += [((rows, units), F32, columns), ((rows, width), F32, full)]
        scratch = [pltpu.VMEM((rows, width), BF16)]
    return call(
        body, [place], (steps,), ins, outs, scratch, "feed_forward",
        2 * rows * width * units * (4 if back else 2), 4 * width * units + 30 * rows * width, rows * units,
    )


def feed_back(middle_grad, state, grad_x, grad_x_other, gain, pre, w_up, w_down, depth):
    rows, width = state.shape
    units = w_up.shape[2]
    step = min(256, units)
    steps = units // step

    def body(grad_ref, state_ref, gx_ref, gy_ref, gain_ref, pre_ref, up_ref, down_ref, up_out, sums_ref, du_ref, dx_ref, dyb_ref):
        at = pl.program_id(0)

        @pl.when(at == 0)
        def _():
            upstream, sums = latent_back(grad_ref[...], state_ref[...], gx_ref[...] + gy_ref[...], gain_ref[...])
            up_out[...] = upstream
            sums_ref[...] = sums
            dyb_ref[...] = upstream.astype(BF16)
            dx_ref[...] = jnp.zeros_like(dx_ref)

        _, slope = gelu_parts(pre_ref[...])
        du = (mm_bt(dyb_ref[...], down_ref[...]) * slope).astype(BF16)
        du_ref[...] = du.astype(F32)
        dx_ref[...] += mm_bt(du, up_ref[...])

    full = whole((rows, width))
    columns = pl.BlockSpec((rows, step), lambda i: (0, i))
    ins = [(value, whole(value.shape)) for value in (middle_grad, state, grad_x, grad_x_other, gain)]
    ins += [(pre, columns)]
    ins += [(w_up, pl.BlockSpec((None, width, step), lambda i: (depth, 0, i))), (w_down, pl.BlockSpec((None, step, width), lambda i: (depth, i, 0)))]
    return call(
        body, [], (steps,), ins,
        [((rows, width), F32, full), ((8, width), F32, whole((8, width))), ((rows, units), F32, columns), ((rows, width), F32, full)],
        [pltpu.VMEM((rows, width), BF16)], "feed_back",
        4 * rows * width * units, 4 * width * units + 30 * rows * width, rows * units,
    )


def latent_back(middle_grad, state, grad_x, gain):
    normed, _, rstd = row_norm(state)
    upstream = middle_grad + row_norm_back(grad_x, gain, normed, rstd)
    gain_sum = jnp.sum(grad_x * normed, axis=0, keepdims=True)
    bias_sum = jnp.sum(grad_x, axis=0, keepdims=True)
    return upstream, jnp.concatenate([gain_sum, bias_sum, jnp.zeros((6, gain_sum.shape[1]), F32)], axis=0)


def latent_end(middle_grad, state, grad_x, grad_x_other, gain, latent_rows):
    rows, width = state.shape

    def body(grad_ref, state_ref, gx_ref, gy_ref, gain_ref, out_ref):
        upstream, sums = latent_back(grad_ref[...], state_ref[...], gx_ref[...] + gy_ref[...], gain_ref[...])
        total = upstream[:latent_rows]
        for clip in range(1, rows // latent_rows):
            total = total + upstream[clip * latent_rows : (clip + 1) * latent_rows]
        out_ref[...] = jnp.concatenate([sums, total], axis=0)

    ins = [(value, whole(value.shape)) for value in (middle_grad, state, grad_x, grad_x_other, gain)]
    shape = (8 + latent_rows, width)
    return call(body, [], (1,), ins, [(shape, F32, whole(shape))], [], "latent_end", rows * width * 20, rows * width * 16)[0]


def attend_back(
    upstream, middle, grad_mine, grad_other, place, counts, ff_gain, media_gain, media_bias,
    w_query, w_pairs, w_out, w_key, w_value, depth, queries, lat_pair, attended, log_total, latent_x, media_pair, media_x,
    latent_rows, frames, patches,
):
    rows, width = middle.shape
    samples = counts.shape[0]
    wide = w_query.shape[1]
    own = w_key.shape[2]
    turns = len(w_pairs)
    heads = wide // HEAD_DIM
    scale = HEAD_DIM ** (-0.5)
    media_len = frames * patches
    chunk = 2 * patches

    def body(
        counts_ref, place_ref, up_ref, mid_ref, mine_ref, other_ref, ffg_ref, mg_ref, mb_ref,
        wq_ref, wo_ref, *refs,
    ):
        wp_refs = refs[:turns]
        wk_ref, wv_ref, q_ref, lat_ref, att_ref, log_ref, x_ref, pair_ref, mx_ref = refs[turns : turns + 9]
        grad_mid_ref, grad_pair_ref, grad_x_ref, grad_w_ref, sums_ref = refs[turns + 9 : turns + 14]
        low_ref, dq_ref, dlat_ref, col_ref = refs[turns + 14 :]
        clip = pl.program_id(0)

        @pl.when(clip == 0)
        def _():
            grad_x = joined(place_ref[0], mine_ref[...], other_ref[...])
            normed, _, rstd = row_norm(mid_ref[...])
            sums_ref[...] = jnp.zeros_like(sums_ref)
            sums_ref[0:1, :] = jnp.sum(grad_x * normed, axis=0, keepdims=True)
            sums_ref[1:2, :] = jnp.sum(grad_x, axis=0, keepdims=True)
            grad_mid = up_ref[...] + row_norm_back(grad_x, ffg_ref[...], normed, rstd)
            grad_mid_ref[...] = grad_mid
            low_ref[...] = grad_mid.astype(BF16)
            grad_w_ref[...] = jnp.zeros_like(grad_w_ref)
            col_ref[...] = jnp.zeros_like(col_ref)

        at = pl.ds(pl.multiple_of(clip * latent_rows, latent_rows), latent_rows)
        query = spread(q_ref[at, :], heads)
        grad_rows = mm_bt(low_ref[at, :], wo_ref[...]).astype(BF16)
        grad_att = spread(grad_rows, heads)
        cross = spread(grad_rows.astype(F32) * att_ref[at, :], heads)
        cross = jnp.broadcast_to(jnp.sum(cross, axis=1, keepdims=True), (wide, 128))
        delta = jnp.transpose(cross, (1, 0))[0:1, :]
        log = log_ref[0][0:1, :]
        live = counts_ref[clip] * patches
        chunks = (counts_ref[clip] + 1) // 2

        def rows_of(index):
            return pl.ds(pl.multiple_of(index * chunk, chunk), chunk)

        def grads_of(keys, values, row):
            score = mm_bt(keys, query) * scale
            dprob = mm_bt(values, grad_att)
            probs = jnp.exp(score - log)
            if row is not None:
                probs = jnp.where(row < live, probs, 0.0)
            dscore = (probs * (dprob - delta)).astype(BF16)
            grad_key = (jnp.dot(dscore, query, preferred_element_type=F32) * scale).astype(BF16)
            grad_value = jnp.dot(probs.astype(BF16), grad_att, preferred_element_type=F32).astype(BF16)
            grad_pair = []
            for turn in range(turns):
                grad_pair += [grad_key[:, turn * own : (turn + 1) * own], grad_value[:, turn * own : (turn + 1) * own]]
            return dscore, jnp.concatenate(grad_pair, axis=1)

        lat_keys = keys_of(lat_ref, at, own)
        lat_dscore, dlat_ref[at, :] = grads_of(lat_keys, values_of(lat_ref, at, own), None)

        def step(index, dq):
            here = rows_of(index)
            row = index * chunk + lax.broadcasted_iota(jnp.int32, (chunk, wide), 0)
            keys = keys_of(pair_ref, here, own)
            dscore, grad_pair = grads_of(keys, values_of(pair_ref, here, own), row)
            grad_pair_ref[here, :] = grad_pair
            grad_own = grad_pair[:, : 2 * own]
            grad_w_ref[: 2 * own, :] += dot_rows(grad_own, mx_ref[here, :])
            col_ref[0:1, :] += jnp.sum(grad_own.astype(F32), axis=0, keepdims=True)
            return dq + dot_rows(dscore, keys)

        dq = lax.fori_loop(0, chunks, step, dot_rows(lat_dscore, lat_keys))
        dq_ref[at, :] = (collect(dq, heads) * scale).astype(BF16)

        @pl.when(clip == samples - 1)
        def _():
            dq_all = dq_ref[...]
            dlat = dlat_ref[...]
            grad_x = mm_bt(dq_all, wq_ref[...])
            for turn in range(turns):
                grad_x += mm_bt(dlat[:, 2 * own * turn : 2 * own * (turn + 1)], wp_refs[turn][...])
            grad_x_ref[...] = grad_x
            columns = jnp.transpose(col_ref[...], (1, 0))
            total_one = jnp.zeros((1, width), F32)
            total_two = jnp.zeros((1, width), F32)
            for slot, own_ref in enumerate((wk_ref, wv_ref)):
                weight = jnp.transpose(own_ref[...].astype(F32), (1, 0))
                column = columns[slot * own : (slot + 1) * own, 0:1]
                media_w = grad_w_ref[slot * own : (slot + 1) * own, :]
                total_one += jnp.sum(weight * (media_w - column * mb_ref[...]), axis=0, keepdims=True)
                total_two += jnp.sum(weight * column, axis=0, keepdims=True)
            sums_ref[2:3, :] = total_one / mg_ref[...]
            sums_ref[3:4, :] = total_two
            x = x_ref[...]
            grad_w_ref[: 2 * own, :] += dot_rows(dlat[:, : 2 * own], x)
            grad_w_ref[2 * own : 3 * own, :] = dot_rows(dq_all[:, :own], x)
            grad_w_ref[3 * own :, :] = dot_rows(att_ref[:, :own].astype(BF16), low_ref[...])

    clip_rows = lambda cols, count: pl.BlockSpec((count, cols), lambda clip, *_: (clip, 0))
    full = whole((rows, width))
    ins = [(value, whole(value.shape)) for value in (
        upstream, middle, grad_mine, grad_other, ff_gain, media_gain, media_bias,
        w_query, w_out, *w_pairs)]
    ins += [(value, pl.BlockSpec((None, width, own), lambda *_: (depth, 0, 0))) for value in (w_key, w_value)]
    ins += [(value, whole(value.shape)) for value in (queries, lat_pair, attended)]
    ins += [(log_total, pl.BlockSpec((1, 8, wide), lambda clip, *_: (clip, 0, 0))), (latent_x, full)]
    ins += [(media_pair, clip_rows(2 * wide, media_len)), (media_x, clip_rows(width, media_len))]
    outs = [
        ((rows, width), F32, full),
        (media_pair.shape, BF16, clip_rows(2 * wide, media_len)),
        ((rows, width), F32, full),
        ((4 * own, width), F32, whole((4 * own, width))),
        ((8, width), F32, whole((8, width))),
    ]
    scratch = [
        pltpu.VMEM((rows, width), BF16),
        pltpu.VMEM((rows, wide), BF16),
        pltpu.VMEM((rows, 2 * wide), BF16),
        pltpu.VMEM((8, 2 * own), F32),
    ]
    return call(
        body, [counts, place], (samples,), ins, outs, scratch, "attend_back",
        2 * samples * media_len * (5 * wide * wide + 2 * own * width),
        samples * media_len * (8 * wide + 2 * width) + 40 * rows * width, samples * media_len * wide,
    )


def outer_sums(pairs, planes, name):
    count, wide = pairs[0][0].shape
    units = pairs[0][2].shape[1]
    chunk = wide // planes
    step = min(512, units)

    def body(*refs):
        out_ref = refs[-1]
        for pair in range(len(pairs)):
            mine, other, rows, rows_other = [ref[...].astype(BF16) for ref in refs[4 * pair : 4 * pair + 4]]
            total = dot_rows(mine, rows) + dot_rows(other, rows_other)
            for plane in range(planes):
                out_ref[plane, pair] = total[plane * chunk : (plane + 1) * chunk, :]

    ins = []
    for pair in pairs:
        ins += [(value, whole(value.shape)) for value in pair[:2]]
        ins += [(value, pl.BlockSpec((count, step), lambda i: (0, i))) for value in pair[2:]]
    shape = (planes, len(pairs), chunk, units)
    return call(
        body, [], (units // step,), ins,
        [(shape, F32, pl.BlockSpec((planes, len(pairs), chunk, step), lambda i: (0, 0, 0, i)))], [], name,
        4 * len(pairs) * count * wide * units, 4 * len(pairs) * wide * units,
    )[0]


def media_back(grad_pairs, pairs, weights, gain_means, bias_means, gains, media, time_rows, stats, counts, place, frames, patches, groups):
    rows, width = media.shape
    layers = len(pairs)
    turns = len(weights[0])
    wide2 = pairs[0].shape[1]
    chip = width // groups
    half = chip // 2
    group = frames_in_block(frames)
    groups_of = frames // group
    samples = counts.shape[0]

    def body(counts_ref, place_ref, *refs):
        grad_refs = refs[:layers]
        pair_refs = refs[layers : 2 * layers]
        weight_refs = refs[2 * layers : (2 + turns) * layers]
        gm_ref, bm_ref, gain_ref, media_ref, time_ref, stat_ref, mine_ref, theirs_ref = refs[(2 + turns) * layers :]
        part = wide2 // turns
        clip, at = pl.program_id(0), pl.program_id(1)
        for inner in range(group):
            frame = at * group + inner
            here = slice(inner * patches, (inner + 1) * patches)
            live = frame < counts_ref[clip]

            @pl.when(live)
            def _():
                total = jnp.zeros((patches, chip), F32)
                one = jnp.zeros((patches, wide2), F32)
                two = jnp.zeros((patches, wide2), F32)
                for layer in range(layers):
                    grad = grad_refs[layer][here, :]
                    product = jnp.zeros((patches, chip), F32)
                    for turn in range(turns):
                        product += mm_bt(grad[:, turn * part : (turn + 1) * part], weight_refs[layer * turns + turn][...])
                    total = total + product * gain_ref[layer : layer + 1, :]
                    grad = grad.astype(F32)
                    one = one + grad * gm_ref[layer : layer + 1, :]
                    two = two + grad * (pair_refs[layer][here, :].astype(F32) - bm_ref[layer : layer + 1, :])
                mean_one = jnp.sum(one, axis=1, keepdims=True)
                mean_two = jnp.sum(two, axis=1, keepdims=True) * (1.0 / width)
                stat = stat_ref[here, :]
                mean, rstd = stat[:, 0:1], stat[:, 64:65]
                normed = (media_ref[here, :].astype(F32) + time_ref[pl.ds(frame, 1), :] - mean) * rstd
                out = rstd * (total - mean_one - normed * mean_two)
                low, high = out[:, :half], out[:, half:]
                first = place_ref[0] == 0
                mine_ref[here, :] = jnp.where(first, low, high)
                theirs_ref[here, :] = jnp.where(first, high, low)

            @pl.when(jnp.logical_not(live))
            def _():
                mine_ref[here, :] = jnp.zeros((patches, half), F32)
                theirs_ref[here, :] = jnp.zeros((patches, half), F32)

    block = live_block(group, groups_of)

    def chip_block(clip, at, counts_ref, place_ref):
        return (block(clip, at, counts_ref)[0], place_ref[1])

    deep = group * patches
    pair_spec = pl.BlockSpec((deep, wide2), block)
    out_spec = pl.BlockSpec((deep, half), lambda clip, at, *_: (clip * groups_of + at, 0))
    by_chip = lambda count: pl.BlockSpec((count, chip), lambda clip, at, counts_ref, place_ref: (0, place_ref[1]))
    ins = [(value, pair_spec) for value in (*grad_pairs, *pairs)]
    ins += [
        (value, pl.BlockSpec((chip, wide2 // turns), lambda clip, at, counts_ref, place_ref: (place_ref[1], 0)))
        for pieces in weights for value in pieces
    ]
    ins += [
        (gain_means, whole(gain_means.shape)), (bias_means, whole(bias_means.shape)),
        (gains, by_chip(layers)), (media, pl.BlockSpec((deep, chip), chip_block)), (time_rows, by_chip(frames)),
        (stats, pl.BlockSpec((deep, 128), block)),
    ]
    return call(
        body, [counts, place], (samples, groups_of), ins,
        [((rows, half), F32, out_spec)] * 2, [], "media_back",
        2 * rows * wide2 * chip * layers, rows * (wide2 * 4 * layers + 6 * chip),
    )


def media_sum(mine, arrived, frames, patches, samples):
    rows, width = mine.shape
    group = frames_in_block(frames)
    groups = frames // group
    deep = group * patches

    def body(mine_ref, arrived_ref, out_ref, sum_ref):
        clip, at = pl.program_id(0), pl.program_id(1)

        @pl.when((clip == 0) & (at == 0))
        def _():
            sum_ref[...] = jnp.zeros_like(sum_ref)

        total = mine_ref[...] + arrived_ref[...]
        out_ref[...] = total.astype(BF16)
        lines = [jnp.sum(total[i * patches : (i + 1) * patches], axis=0, keepdims=True) for i in range(group)]
        for piece in range(groups):

            @pl.when(at == piece)
            def _():
                for i in range(group):
                    frame = piece * group + i
                    sum_ref[frame : frame + 1, :] += lines[i]

    spec = pl.BlockSpec((deep, width), lambda clip, at: (clip * groups + at, 0))
    return call(
        body, [], (samples, groups), [(mine, spec), (arrived, spec)],
        [((rows, width), BF16, spec), ((frames, width), F32, whole((frames, width)))], [], "media_sum",
        2 * rows * width, 10 * rows * width,
    )


def finish_ff(ups, downs):
    layers = len(ups)
    chunk, units = ups[0][2], ups[0][0].shape[1]

    def body(*refs):
        up_ref, down_ref = refs[2 * layers :]
        for layer in range(layers):
            up_ref[layer] = refs[layer][...]
            down_ref[layer] = jnp.transpose(refs[layers + layer][...], (1, 0))

    ins = [
        (value, pl.BlockSpec((chunk, units), lambda i, at=at: (at, 0))) for value, at, _ in (*ups, *downs)
    ]
    shapes = [(layers, chunk, units), (layers, units, chunk)]
    return call(
        body, [], (1,), ins, [(shape, F32, whole(shape)) for shape in shapes], [], "finish_ff",
        4 * layers * chunk * units, 16 * layers * chunk * units,
    )


def finish_attn(attn, layers, own):
    chunk = attn.shape[1]

    def body(attn_ref, query_ref, key_ref, value_ref, out_ref):
        for layer in range(layers):
            for slot, ref in enumerate((key_ref, value_ref, query_ref, out_ref)):
                at = (4 * layer + slot) * own
                part = attn_ref[at : at + own, :]
                ref[layer] = part if slot == 3 else jnp.transpose(part, (1, 0))

    shapes = [(layers, chunk, own)] * 3 + [(layers, own, chunk)]
    return call(
        body, [], (1,), [(attn, whole(attn.shape))], [(shape, F32, whole(shape)) for shape in shapes], [], "finish_attn",
        attn.size, 8 * attn.size,
    )


class Links:

    def __init__(self, zero):
        self.zero = zero
        self.planes = lax.axis_size("plane")
        self.groups = lax.axis_size("group")
        self.plane = lax.axis_index("plane")
        self.side = lax.axis_index("side")
        self.group = lax.axis_index("group")
        self.core = lax.axis_index("core")

    def rounded(self, value):
        return (value + self.zero).astype(BF16)

    def core_swap(self, value):
        return lax.ppermute(value, "core", [(0, 1), (1, 0)])

    def side_swap(self, value):
        return lax.ppermute(value, "side", [(0, 1), (1, 0)])

    def group_turn(self, value, turn):
        return lax.ppermute(value, "group", [(i, (i + turn) % self.groups) for i in range(self.groups)])

    def cut(self, value, index):
        half = value.shape[0] // 2
        return lax.dynamic_slice_in_dim(value, index * half, half, 0)

    def join(self, mine, other, index):
        first = index == 0
        return jnp.concatenate([jnp.where(first, mine, other), jnp.where(first, other, mine)], axis=0)

    def core_half(self, value):
        return self.cut(value, self.core) + self.core_swap(self.cut(value, 1 - self.core))

    def group_turns(self, value):
        return [self.group_turn(value, k) for k in range(1, self.groups)]

    def group_total(self, value, turned):
        if self.groups == 2:
            return value + turned[0]
        turned = jnp.stack([value] + turned)
        total = None
        for source in range(self.groups):
            slot = lax.rem(self.group - source + self.groups, self.groups)
            term = lax.dynamic_index_in_dim(turned, slot, 0, keepdims=False)
            total = term if total is None else total + term
        return total

    def tensor_halves(self, value):
        mine = self.core_half(value)
        mine = self.group_total(mine, self.group_turns(mine))
        return mine, self.core_swap(mine)

    def dp_sum(self, value):
        value = value + self.side_swap(value)
        step = 1
        while step < self.planes:
            value = value + lax.ppermute(value, "plane", [(i, i ^ step) for i in range(self.planes)])
            step *= 2
        return value

    def columns(self, value, side):
        wide = value.shape[1] // (2 * self.planes)
        cuts = [value[:, i * wide : (i + 1) * wide] for i in range(2 * self.planes)]
        return jnp.where(side == 0, jnp.concatenate(cuts[0::2], axis=1), jnp.concatenate(cuts[1::2], axis=1))

    def both_columns(self, value):
        return self.columns(value, self.side), self.side_swap(self.columns(value, 1 - self.side))

    def scatter(self, value, dimension):
        return lax.psum_scatter(value, "plane", scatter_dimension=dimension, tiled=True)


def local(
    media,
    frame_counts,
    time_embed,
    latents,
    media_gain,
    media_bias,
    latent_gain,
    latent_bias,
    ff_gain,
    ff_bias,
    w_query,
    w_key,
    w_value,
    w_out,
    w_up,
    w_down,
    cotangent,
):
    links = Links(jnp.where(frame_counts[0] > 1000000, 1.0, 0.0).astype(F32))
    samples, media_len, width = media.shape
    frames = time_embed.shape[0]
    patches = media_len // frames
    latent_rows = latents.shape[0]
    own = w_query.shape[2]
    layers = w_query.shape[0]
    wide = own * links.groups
    rows = samples * latent_rows
    tensor_size = 2 * links.groups
    turns = range(1, links.groups)
    place = jnp.stack([links.core, links.group, links.side]).astype(jnp.int32)

    def row(value, depth):
        return value[depth : depth + 1]

    def after(values, event):
        return lax.optimization_barrier((values, event))

    def project(depth, x, pair, weight, nears, fars):
        pieces = [weight]
        for k in turns:
            far = None if fars is None else fars[k - 1]
            pair, weight = project_more(x, frame_counts, place, pair, nears[k - 1], far, k, frames, patches)
            pieces.append(weight)
        return pair, pieces

    def packed(depth, event):
        weights, event = after((w_key, w_value, w_query, w_out), event)
        wanted = [(weights[:2], depth, depth > 0), (weights[2:3], depth, False), (weights[3:], depth, False)]
        return lax.optimization_barrier((pack(place, wanted, "pack"), event))

    def near_of(depth, values):
        for name, value in zip(("pair", "query", "out"), values):
            nears[name, depth] = links.group_turns(value)

    def by_side(nears):
        return [links.side_swap(value) for value in nears]

    def more_of(depth):
        return [(query, None, out, None) for query, out in zip(nears["query", depth], nears["out", depth])]

    media_rows = media.reshape(samples * media_len, width)
    time_rows = time_embed.astype(F32)

    def prepared(depth, media_then):
        return prepare(
            media_then, frame_counts, time_rows, row(media_gain, depth), row(media_bias, depth),
            w_key, w_value, depth, links.groups, frames, patches,
        )

    nears = {}
    media_then = media_rows
    if layers > 1:
        sent, media_then = packed(1, media_rows)
        near_of(1, sent)
    x, stats, pair, weight = prepared(0, media_then)
    media_x, media_pair, w_pairs = [x], [pair], [[weight]]
    fars = {}
    if layers > 1:
        sent, pair = after(nears["pair", 1], pair)
        media_pair[0] = pair
        fars["pair", 1] = by_side(sent)
    more = [[]]

    state_in = (jnp.broadcast_to(latents.astype(F32)[None], (samples, latent_rows, width)).reshape(rows, width),)
    cotangent_rows = cotangent.reshape(rows, width)
    low_cotangent, stats = after(cotangent_rows.astype(BF16).astype(F32), stats)
    upstream_cols = links.both_columns(low_cotangent)
    saved = []
    early = []

    def attended_layer(depth, state_in, more, pieces, pair):
        return attend(
            state_in, place, frame_counts, row(latent_gain, depth), row(latent_bias, depth),
            w_query, w_out, more, pieces, depth, pair, latent_rows, frames, patches,
        )

    for depth in range(layers):
        last = depth == layers - 1
        state, latent_x, queries, lat_pair, attended, log_total, part, query4, out4 = attended_layer(
            depth, state_in, more[depth], w_pairs[depth], media_pair[depth]
        )
        if depth == 0:
            if not last:
                (nears["query", 1], nears["out", 1]), part = after((nears["query", 1], nears["out", 1]), part)
            mine = links.core_half(part)
            if last:
                part = links.tensor_halves(part)
            else:
                media_then, mine = after(media_rows, mine)
                sent, mine = packed(0, mine)
                turned = links.group_turns(mine)
                first_sent = sent[1:]
                x, _, pair, weight = prepared(1, media_then)
                (turned, first_pair), x = after((turned, sent[0]), x)
                nears["pair", 0] = links.group_turns(first_pair)
                mine = links.group_total(mine, turned)
                fars["pair", 1], mine = after(fars["pair", 1], mine)
                part = (mine, links.core_swap(mine))
        else:
            part = (part, links.core_swap(part))
        middle, ff_x, pre, hidden, out_part, *back = feed_forward(
            place, state, *part, row(ff_gain, depth), row(ff_bias, depth),
            w_up, w_down, depth, cotangent_rows if last else None,
        )
        saved.append((state, latent_x, queries, lat_pair, attended, log_total, middle, pre, hidden, query4, out4))
        if last:
            hidden_other = links.side_swap(hidden)
            (ff_x, back[0]), hidden_other = after((ff_x, back[0]), hidden_other)
            early.append((hidden_other, links.both_columns(ff_x.astype(F32))))
            continue
        early.append((hidden, ff_x))
        mine = links.core_half(out_part)
        if depth > 0:
            media_then, mine = after(media_rows, mine)
            x, _, pair, weight = prepared(depth + 1, media_then)
        if depth == 0:
            nears["pair", 0], mine = after(nears["pair", 0], mine)
        (x, fars["pair", depth + 1]), mine = after((x, fars["pair", depth + 1]), mine)
        turned = links.group_turns(mine)
        pair, pieces = project(depth + 1, x, pair, weight, nears["pair", depth + 1], fars["pair", depth + 1])
        turned, pair = after(turned, pair)
        media_x.append(x)
        media_pair.append(pair)
        w_pairs.append(pieces)
        mine = links.group_total(mine, turned)
        if depth == 0:
            first_sent, mine = after(first_sent, mine)
            for name, value in zip(("query", "out"), first_sent):
                gathered = lax.all_gather(value, "group", axis=0, tiled=True)
                nears[name, 0] = [Gathered(gathered, links.groups, k) for k in turns]
        state_in = (middle, mine, links.core_swap(mine))
        upstream_cols, state_in = after(upstream_cols, state_in)
        more.append(more_of(depth + 1))
    sums = links.tensor_halves(out_part)
    sums, hidden_other = after(sums, early[-1][0])
    early[-1] = (hidden_other, early[-1][1])
    resampled = middle + links.join(*sums, links.core)

    upstream = cotangent_rows
    grads = [None] * layers
    gains = [None] * layers
    pair_grads = [None] * layers
    attn_ws = [None] * layers
    units = w_up.shape[2]
    for depth in reversed(range(layers)):
        state, latent_x, queries, lat_pair, attended, log_total, middle, pre, hidden, query4, out4 = saved[depth]
        if depth == layers - 1:
            grad_pre, grad_ffx = back
        else:
            upstream, latent_sums, grad_pre, grad_ffx = feed_back(
                grad_middle, saved[depth + 1][0], grad_x, grad_x_other, row(latent_gain, depth + 1),
                pre, w_up, w_down, depth,
            )
            gains[depth + 1] += (latent_sums[0], latent_sums[1])
            upstream_cols = links.both_columns(upstream.astype(BF16).astype(F32))
            if depth == 0:
                (x, pair), (grad_pre, up_sums) = after((media_x[0], media_pair[0]), (grad_pre, up_sums))
                media_pair[0], w_pairs[0] = project(0, x, pair, w_pairs[0][0], nears["pair", 0], None)
                more[0] = more_of(0)
                _, latent_x, queries, lat_pair, attended, log_total, _, query4, out4 = attended_layer(
                    0, (state,), more[0], w_pairs[0], media_pair[0]
                )
                upstream_cols, queries = after(upstream_cols, queries)
        hidden_other, ff_x_cols = early[depth]
        down = (*upstream_cols, hidden, hidden_other)
        up = (*ff_x_cols, grad_pre, links.side_swap(grad_pre))
        grad_mine, grad_other = links.tensor_halves(grad_ffx)
        if depth == layers - 1:
            down = outer_sums([down], links.planes, "down_sums")
            grad_mine, down = after(grad_mine, down)
            grad_down = links.scatter(down.reshape(-1, units), 0)
            grad_down = (grad_down, 0, grad_down.shape[0])
        else:
            both = outer_sums([down, up], links.planes, "ff_sums")
            grad_mine, both = after(grad_mine, both)
            above, both = after(attn_ws[depth + 1], both)
            attn_ws[depth + 1] = above[0] + links.side_swap(above[1])
            both = links.scatter(both.reshape(-1, units), 0)
            grad_down, grad_up = (both, 0, both.shape[0] // 2), (both, 1, both.shape[0] // 2)
        grad_middle, pair_grads[depth], grad_x, attn_w, sums = attend_back(
            upstream, middle, grad_mine, grad_other, place, frame_counts,
            row(ff_gain, depth), row(media_gain, depth), row(media_bias, depth),
            query4, w_pairs[depth], out4, w_key, w_value, depth, queries, lat_pair, attended, log_total, latent_x,
            media_pair[depth], media_x[depth], latent_rows, frames, patches,
        )
        if depth == layers - 1:
            pre_other, grad_x = after(up[3], grad_x)
            up_sums = outer_sums([(*up[:3], pre_other)], links.planes, "up_sums")
            if depth > 0:
                (hidden, ff_x), up_sums = after(early[depth - 1], up_sums)
                early[depth - 1] = (links.side_swap(hidden), links.both_columns(ff_x.astype(F32)))
            grad_up = links.scatter(up_sums.reshape(-1, units), 0)
            grad_up = (grad_up, 0, grad_up.shape[0])
        grad_x_other = links.core_swap(grad_x)
        attn_ws[depth] = (links.columns(attn_w, links.side), links.columns(attn_w, 1 - links.side))
        grads[depth] = (grad_up, grad_down)
        gains[depth] = (sums[0], sums[1], sums[2], sums[3])
    ending = latent_end(grad_middle, saved[0][0], grad_x, grad_x_other, row(latent_gain, 0), latent_rows)
    gains[0] += (ending[0], ending[1])
    latent_part = ending[8:]
    share = 1.0 / tensor_size
    gains = [(g[2], g[3], g[4] * share, g[5] * share, g[0] * share, g[1] * share) for g in gains]

    core_width = width // tensor_size
    weight_long = [jnp.concatenate(w_pairs[l], axis=1).astype(F32) for l in range(layers)]
    gain_means = jnp.stack([jnp.sum(weight_long[l] * media_gain[l][:, None], axis=0) / width for l in range(layers)])
    bias_means = jnp.stack([jnp.sum(weight_long[l] * media_bias[l][:, None], axis=0) for l in range(layers)])
    (attn_mine, attn_theirs), stats = after(attn_ws[0], stats)
    attn_theirs = links.side_swap(attn_theirs)
    if layers > 1:
        attn_ws[1:], stats = after(attn_ws[1:], stats)
    (stats, *tied) = lax.optimization_barrier((stats, *[value[0] for pair in grads[1:] for value in pair]))
    for depth in range(1, layers):
        grads[depth] = tuple((tied.pop(0), *value[1:]) for value in grads[depth])
    mine, theirs = media_back(
        pair_grads, media_pair, w_pairs, gain_means, bias_means, media_gain, media_rows, time_rows, stats,
        frame_counts, place, frames, patches, links.groups,
    )
    (mine, theirs), attn_theirs = after((mine, theirs), attn_theirs)
    attn_ws[0] = attn_mine + attn_theirs
    media_grad, time_part = media_sum(mine, links.core_swap(theirs), frames, patches, samples)
    media_grad = media_grad.reshape(samples, media_len, core_width)

    def column_cuts(value):
        return [value[:, i * core_width : (i + 1) * core_width] for i in range(tensor_size)]

    def column_cut(value, index):
        return lax.dynamic_slice_in_dim(value, index * core_width, core_width, 1)

    gain_flat = jnp.stack([gains[l][m] for m in range(6) for l in range(layers)])
    by_core = [jnp.concatenate(column_cuts(gain_flat)[c::2], axis=1) for c in range(2)]
    core_mine = jnp.where(links.core == 0, by_core[0], by_core[1])
    core_theirs = jnp.where(links.core == 0, by_core[1], by_core[0])
    gain_share = core_mine + links.core_swap(core_theirs)
    gain_sum = column_cut(gain_share, links.group)
    for turn in turns:
        target = lax.rem(links.group + turn, links.groups)
        gain_sum = gain_sum + links.group_turn(column_cut(gain_share, target), turn)
    latent_share = column_cut(latent_part, links.group * 2 + links.core)
    attn_all, (both_grads, media_grad) = after(jnp.concatenate(attn_ws, axis=0), (grads[0][0][0], media_grad))
    small_in = jnp.concatenate([gain_sum, time_part, latent_share], axis=0)
    small_in, attn_all = after(small_in, attn_all)
    attn = links.scatter(attn_all, 1)
    small = links.dp_sum(small_in)
    swapped = links.core_swap(small)
    pair = jnp.concatenate(
        [jnp.where(links.core == 0, small, swapped), jnp.where(links.core == 0, swapped, small)], axis=1
    )
    turned = jnp.stack([pair] + [links.group_turn(pair, k) for k in turns])
    order = [lax.rem(links.group - source + links.groups, links.groups) for source in range(links.groups)]
    small_all = jnp.concatenate(
        [lax.dynamic_index_in_dim(turned, slot, 0, keepdims=False) for slot in order], axis=1
    )
    gain_all = small_all[: 6 * layers].reshape(6, layers, width)
    time_grad = small_all[6 * layers : 6 * layers + frames]
    latents_grad = small_all[6 * layers + frames :]
    ups, downs = [grads[l][0] for l in range(layers)], [grads[l][1] for l in range(layers)]
    ups[0], downs[0] = (both_grads, *ups[0][1:]), (both_grads, *downs[0][1:])
    w_up_grad, w_down_grad = finish_ff(ups, downs)
    w_query_grad, w_key_grad, w_value_grad, w_out_grad = finish_attn(attn, layers, own)

    return (
        resampled.reshape(samples, latent_rows, width),
        media_grad,
        time_grad,
        latents_grad,
        gain_all[0],
        gain_all[1],
        gain_all[2],
        gain_all[3],
        gain_all[4],
        gain_all[5],
        w_query_grad,
        w_key_grad,
        w_value_grad,
        w_out_grad,
        w_up_grad,
        w_down_grad,
    )


def solution(mesh):
    dp_size, tensor_size = mesh.devices.shape
    split = jax.sharding.Mesh(
        mesh.devices.reshape(dp_size // 2, 2, tensor_size // 2, 2), ("plane", "side", "group", "core")
    )
    dp, tensor = ("plane", "side"), ("group", "core")
    in_specs = (
        P(dp, None, None),
        P(dp),
        P(),
        P(),
        P(),
        P(),
        P(),
        P(),
        P(),
        P(),
        P(None, None, tensor),
        P(None, None, tensor),
        P(None, None, tensor),
        P(None, tensor, None),
        P(None, None, tensor),
        P(None, tensor, None),
        P(dp, None, None),
    )
    out_specs = (
        P(dp, None, None),
        P(dp, None, tensor),
        P(),
        P(),
        P(),
        P(),
        P(),
        P(),
        P(),
        P(),
        P(None, dp, tensor),
        P(None, dp, tensor),
        P(None, dp, tensor),
        P(None, tensor, dp),
        P(None, dp, tensor),
        P(None, tensor, dp),
    )
    return jax.shard_map(local, mesh=split, in_specs=in_specs, out_specs=out_specs, check_vma=False)
```

```python
import functools

import jax
import jax.numpy as jnp
from jax import lax
from jax.experimental import pallas as pl
from jax.experimental.pallas import tpu as pltpu
from jax.sharding import PartitionSpec as P

HEAD_DIM = 64
EPS = 1e-05
F32 = jnp.float32
BF16 = jnp.bfloat16
VMEM_LIMIT = 62 * 1024 * 1024


def mm(left_side, right_side):
    return jnp.dot(left_side, right_side, preferred_element_type=F32)


def mm_bt(left_side, right_side):
    return lax.dot_general(left_side, right_side, (((1,), (1,)), ((), ())), preferred_element_type=F32)


def mm_at(left_side, right_side):
    return lax.dot_general(left_side, right_side, (((0,), (0,)), ((), ())), preferred_element_type=F32)


def dot_rows(left_side, right_side):
    return lax.dot_general(left_side, right_side, (((0,), (0,)), ((), ())), preferred_element_type=F32)


def row_norm(values):
    count = values.shape[-1]
    mean = jnp.sum(values, axis=-1, keepdims=True) * (1.0 / count)
    centered = values - mean
    rstd = lax.rsqrt(jnp.sum(centered * centered, axis=-1, keepdims=True) * (1.0 / count) + EPS)
    return centered * rstd, mean, rstd


def row_norm_back(grad, gain, normed, rstd):
    count = grad.shape[-1]
    scaled = grad * gain
    mean_one = jnp.sum(scaled, axis=-1, keepdims=True) * (1.0 / count)
    mean_two = jnp.sum(scaled * normed, axis=-1, keepdims=True) * (1.0 / count)
    return rstd * (scaled - mean_one - normed * mean_two)


def whole(shape):
    zeros = (0,) * len(shape)
    return pl.BlockSpec(shape, lambda *_: zeros)


def call(body, scalars, grid, ins, outs, scratch, name, flops, moved, exps=0, aliases=None):
    return pl.pallas_call(
        body,
        out_shape=[jax.ShapeDtypeStruct(shape, dtype) for shape, dtype, _ in outs],
        grid_spec=pltpu.PrefetchScalarGridSpec(
            num_scalar_prefetch=len(scalars),
            grid=grid,
            in_specs=[spec for _, spec in ins],
            out_specs=[spec for _, _, spec in outs],
            scratch_shapes=scratch,
        ),
        compiler_params=pltpu.CompilerParams(
            dimension_semantics=("arbitrary",) * len(grid), vmem_limit_bytes=VMEM_LIMIT
        ),
        cost_estimate=pl.CostEstimate(flops=flops, bytes_accessed=moved, transcendentals=exps),
        name=name,
        input_output_aliases=aliases or {},
    )(*scalars, *[array for array, _ in ins])


def frames_in_block(frames):
    return 4 if frames % 4 == 0 else 1


def by_live_spans(at, live, group, work, dead):
    span = group
    spans = []
    while span:
        spans.append(span)
        span //= 2

    def visit(first, span):
        if span == 1:

            @pl.when(at * group + first < live)
            def _():
                work(range(first, first + 1))

            @pl.when((at * group + first >= live) & (at * group < live))
            def _():
                dead(first)

            return

        @pl.when(at * group + first + span <= live)
        def _():
            work(range(first, first + span))

        @pl.when(at * group + first + span > live)
        def _():
            visit(first, span // 2)
            visit(first + span // 2, span // 2)

    visit(0, group)


def live_block(group, groups):
    def block(clip, at, counts_ref, *_):
        return (clip * groups + jnp.minimum(at, (counts_ref[clip] - 1) // group), 0)

    return block


def pack(place, wanted, name):
    ins, outs, counts = [], [], []
    for weights, depth, halved in wanted:
        count = weights[0].shape[1] // (2 if halved else 1)
        for weight in weights:
            spec = lambda i, place_ref, depth=depth, halved=halved: (depth, place_ref[2] if halved else 0, 0)
            ins.append((weight, pl.BlockSpec((None, count, weight.shape[2]), spec)))
        shape = (count, sum(weight.shape[2] for weight in weights))
        outs.append((shape, F32, whole(shape)))
        counts.append(len(weights))

    def body(place_ref, *refs):
        in_refs, out_refs = list(refs[: len(ins)]), refs[len(ins) :]
        for out_ref, count in zip(out_refs, counts):
            at = 0
            for _ in range(count):
                part = in_refs.pop(0)
                out_ref[:, at : at + part.shape[1]] = part[...].astype(F32)
                at += part.shape[1]

    moved = sum(6 * shape[0] * shape[1] for shape, _, _ in outs)
    return call(body, [place], (1,), ins, outs, [], name, moved, moved)


def keep_rows(ref, first, columns, side, near, far):
    if far is None:
        ref[first : first + near.shape[0], columns] = near[...].astype(BF16)
        return
    half = near.shape[0]
    ref[pl.ds(pl.multiple_of(first + side * half, half), half), columns] = near[...].astype(BF16)
    ref[pl.ds(pl.multiple_of(first + (1 - side) * half, half), half), columns] = far[...].astype(BF16)


def scaled_rows(values, gain, bias):
    normed, mean, rstd = row_norm(values)
    return (normed * gain + bias).astype(BF16), mean, rstd


def prepare(media, counts, time_rows, gain, bias, w_key, w_value, depth, turns, frames, patches):
    rows, width = media.shape
    samples = counts.shape[0]
    own = w_key.shape[2]
    group = frames_in_block(frames)
    groups = frames // group

    def body(counts_ref, media_ref, time_ref, gain_ref, bias_ref, wk_ref, wv_ref, kept_ref, pair_ref, weight_ref):
        clip, at = pl.program_id(0), pl.program_id(1)

        @pl.when((clip == 0) & (at == 0))
        def _():
            weight_ref[...] = jnp.concatenate([wk_ref[...], wv_ref[...]], axis=1)

        def rows_at(inner):
            return slice(inner * patches, (inner + 1) * patches)

        def work(inners):
            for inner in inners:
                here = rows_at(inner)
                values = media_ref[here, :].astype(F32) + time_ref[pl.ds(at * group + inner, 1), :]
                x, mean, rstd = scaled_rows(values, gain_ref[...], bias_ref[...])
                if depth == 0:
                    lane = lax.broadcasted_iota(jnp.int32, (patches, 128), 1)
                    kept_ref[here, :] = jnp.where(lane < 64, mean, rstd)
                else:
                    kept_ref[here, :] = x
                pair_ref[here, :] = jnp.dot(x, weight_ref[...], preferred_element_type=F32).astype(BF16)

        def dead(inner):
            if depth > 0:
                kept_ref[rows_at(inner), :] = jnp.zeros((patches, width), BF16)
            pair_ref[rows_at(inner), :] = jnp.zeros((patches, 2 * own), BF16)

        by_live_spans(at, counts_ref[clip], group, work, dead)

    block = live_block(group, groups)
    deep = group * patches
    row_spec = pl.BlockSpec((deep, width), block)
    weight_spec = pl.BlockSpec((None, width, own), lambda *_: (depth, 0, 0))
    kept = ((rows, 128), F32, pl.BlockSpec((deep, 128), block)) if depth == 0 else ((rows, width), BF16, row_spec)
    return call(
        body, [counts], (samples, groups),
        [(media, row_spec), (time_rows, whole(time_rows.shape)), (gain, whole(gain.shape)), (bias, whole(bias.shape)),
         (w_key, weight_spec), (w_value, weight_spec)],
        [kept, ((rows, 2 * own * turns), BF16, pl.BlockSpec((deep, 2 * own), block)),
         ((width, 2 * own), BF16, whole((width, 2 * own)))],
        [], "prepare", 2 * rows * width * 2 * own, rows * width * 4,
    )


def project_more(source, counts, place, pair, near, far, turn, frames, patches):
    made = isinstance(source, tuple)
    rows, width = (source[0] if made else source).shape
    wide = near.shape[1]
    group = frames_in_block(frames)
    groups = frames // group
    parts = 1 if far is None else 2

    def body(counts_ref, place_ref, *refs):
        x_ref, pair_in_ref, *refs = refs
        halves, refs = refs[:parts], refs[parts:]
        if made:
            time_ref, gain_ref, bias_ref, out_ref, weight_ref, made_ref = refs
        else:
            out_ref, weight_ref = refs
        clip, at = pl.program_id(0), pl.program_id(1)

        @pl.when((clip == 0) & (at == 0))
        def _():
            keep_rows(weight_ref, 0, slice(None), place_ref[2], halves[0], halves[1] if parts == 2 else None)

        def work(inners):
            if made:
                for inner in inners:
                    here = slice(inner * patches, (inner + 1) * patches)
                    values = x_ref[here, :].astype(F32) + time_ref[pl.ds(at * group + inner, 1), :]
                    x, _, _ = scaled_rows(values, gain_ref[...], bias_ref[...])
                    made_ref[here, :] = x
                    out_ref[here, :] = jnp.dot(x, weight_ref[...], preferred_element_type=F32).astype(BF16)
            else:
                here = slice(inners[0] * patches, (inners[-1] + 1) * patches)
                out_ref[here, :] = jnp.dot(x_ref[here, :], weight_ref[...], preferred_element_type=F32).astype(BF16)

        def dead(inner):
            here = slice(inner * patches, (inner + 1) * patches)
            out_ref[here, :] = jnp.zeros((patches, wide), BF16)
            if made:
                made_ref[here, :] = jnp.zeros((patches, width), BF16)

        by_live_spans(at, counts_ref[clip], group, work, dead)

    block = live_block(group, groups)
    deep = group * patches
    row_spec = pl.BlockSpec((deep, width), block)
    halves = [near] if far is None else [near, far]
    ins = [(source[0] if made else source, row_spec), (pair, pl.BlockSpec(memory_space=pl.ANY))]
    ins += [(half, whole(half.shape)) for half in halves]
    outs = [
        (pair.shape, BF16, pl.BlockSpec((deep, wide), lambda clip, at, counts_ref, *_: (block(clip, at, counts_ref)[0], turn))),
        ((width, wide), BF16, whole((width, wide))),
    ]
    if made:
        ins += [(value, whole(value.shape)) for value in source[1:]]
        outs.append(((rows, width), BF16, row_spec))
    return call(
        body, [counts, place], (counts.shape[0], groups), ins, outs, [], "project_more",
        2 * rows * width * wide, 2 * rows * (width + wide), aliases={3: 0},
    )


def spread(rows_of_heads, heads):
    rows, wide = rows_of_heads.shape
    tiled = jnp.concatenate([rows_of_heads] * heads, axis=0)
    head_row = lax.broadcasted_iota(jnp.int32, tiled.shape, 0) // rows
    head_col = lax.broadcasted_iota(jnp.int32, tiled.shape, 1) // (wide // heads)
    return jnp.where(head_row == head_col, tiled, jnp.zeros_like(tiled))


def collect(blocks, heads):
    rows = blocks.shape[0] // heads
    head_col = lax.broadcasted_iota(jnp.int32, (rows, blocks.shape[1]), 1) // (blocks.shape[1] // heads)
    total = jnp.zeros((rows, blocks.shape[1]), blocks.dtype)
    for head in range(heads):
        total = jnp.where(head_col == head, blocks[head * rows : (head + 1) * rows], total)
    return total


def joined(core, mine, other):
    first = core == 0
    return jnp.concatenate([jnp.where(first, mine, other), jnp.where(first, other, mine)], axis=0)


def keys_of(ref, at, own):
    return jnp.concatenate([ref[at, first : first + own] for first in range(0, ref.shape[1], 2 * own)], axis=1)


def values_of(ref, at, own):
    return jnp.concatenate([ref[at, first + own : first + 2 * own] for first in range(0, ref.shape[1], 2 * own)], axis=1)


def attend(state_in, place, counts, gain, bias, w_query, w_out, more, w_pairs, depth, media_pair, latent_rows, frames, patches):
    rows, width = state_in[0].shape
    samples = counts.shape[0]
    own = w_query.shape[2]
    turns = len(w_pairs)
    wide = own * turns
    heads = wide // HEAD_DIM
    scale = HEAD_DIM ** (-0.5)
    media_len = frames * patches
    parts = len(state_in)

    def body(counts_ref, place_ref, *refs):
        state_refs = refs[:parts]
        gain_ref, bias_ref, wq_own_ref, wo_own_ref = refs[parts : parts + 4]
        at_more = parts + 4
        at_pairs = at_more + len(flat)
        more_refs = list(refs[at_more:at_pairs])
        wp_refs = refs[at_pairs : at_pairs + turns]
        pair_ref = refs[at_pairs + turns]
        state_ref, x_ref, q_ref, lat_ref, att_ref, log_ref, part_ref, wq_ref, wo_ref, score_ref, sum_ref = refs[at_pairs + turns + 1 :]
        clip = pl.program_id(0)

        @pl.when(clip == 0)
        def _():
            state = state_refs[0][...]
            if parts == 3:
                state = state + joined(place_ref[0], state_refs[1][...], state_refs[2][...])
            state_ref[...] = state
            normed, _, _ = row_norm(state)
            x = (normed * gain_ref[...] + bias_ref[...]).astype(BF16)
            x_ref[...] = x
            wq_ref[:, :own] = wq_own_ref[...]
            wo_ref[:own, :] = wo_own_ref[...]
            for turn, halves in enumerate(more, 1):
                loaded = [None if half is None else more_refs.pop(0) for half in halves]
                keep_rows(wq_ref, 0, slice(turn * own, (turn + 1) * own), place_ref[2], *loaded[:2])
                keep_rows(wo_ref, turn * own, slice(None), place_ref[2], *loaded[2:])
            q_ref[...] = jnp.dot(x, wq_ref[...], preferred_element_type=F32).astype(BF16)
            for turn in range(turns):
                lat_ref[:, 2 * own * turn : 2 * own * (turn + 1)] = jnp.dot(
                    x, wp_refs[turn][...], preferred_element_type=F32
                ).astype(BF16)

        at = pl.ds(pl.multiple_of(clip * latent_rows, latent_rows), latent_rows)
        queries = spread(q_ref[at, :], heads)
        lat_score = mm_bt(keys_of(lat_ref, at, own), queries) * scale
        lat_top = jnp.max(lat_score, axis=0, keepdims=True)

        def over(count):
            scores, top = [], lat_top
            for frame in range(count):
                score = mm_bt(keys_of(pair_ref, slice(frame * patches, (frame + 1) * patches), own), queries) * scale
                if frame == count - 1:
                    score = jnp.where(counts_ref[clip] > frame, score, -1e30)
                score_ref[frame * patches : (frame + 1) * patches, :] = score
                top = jnp.maximum(top, jnp.max(score, axis=0, keepdims=True))
            exps = jnp.exp(lat_score - top)
            total = jnp.sum(exps, axis=0, keepdims=True)
            sums = dot_rows(values_of(lat_ref, at, own), exps.astype(BF16))
            for frame in range(count):
                here = slice(frame * patches, (frame + 1) * patches)
                exps = jnp.exp(score_ref[here, :] - top)
                total = total + jnp.sum(exps, axis=0, keepdims=True)
                sums = sums + dot_rows(values_of(pair_ref, here, own), exps.astype(BF16))
            log_ref[0] = jnp.broadcast_to(top + jnp.log(total), (8, wide))
            sum_ref[...] = jnp.transpose(sums * (1.0 / total), (1, 0))

        for count in range(2, frames + 1, 2):
            pl.when((counts_ref[clip] + 1) // 2 * 2 == count)(functools.partial(over, count))
        sums = sum_ref[...]
        attended = collect(sums, heads)
        att_ref[...] = attended
        part_ref[...] = jnp.dot(attended.astype(BF16), wo_ref[...], preferred_element_type=F32)

    clip_rows = lambda cols, count: pl.BlockSpec((count, cols), lambda clip, *_: (clip, 0))
    flat = [half for halves in more for half in halves if half is not None]
    ins = [(value, whole(value.shape)) for value in (*state_in, gain, bias)]
    ins += [(w_query, pl.BlockSpec((None, width, own), lambda *_: (depth, 0, 0))),
            (w_out, pl.BlockSpec((None, own, width), lambda *_: (depth, 0, 0)))]
    ins += [(value, whole(value.shape)) for value in (*flat, *w_pairs)]
    ins.append((media_pair, clip_rows(2 * wide, media_len)))
    outs = [
        ((rows, width), F32, whole((rows, width))),
        ((rows, width), BF16, whole((rows, width))),
        ((rows, wide), BF16, whole((rows, wide))),
        ((rows, 2 * wide), BF16, whole((rows, 2 * wide))),
        ((rows, wide), F32, clip_rows(wide, latent_rows)),
        ((samples, 8, wide), F32, pl.BlockSpec((1, 8, wide), lambda clip, *_: (clip, 0, 0))),
        ((rows, width), F32, clip_rows(width, latent_rows)),
        ((width, wide), BF16, whole((width, wide))),
        ((wide, width), BF16, whole((wide, width))),
    ]
    return call(
        body, [counts, place], (samples,), ins, outs,
        [pltpu.VMEM((media_len, wide), F32), pltpu.VMEM((wide, wide), F32)], "attend",
        2 * samples * media_len * wide * wide * 3, samples * media_len * wide * 4 + 8 * width * wide + 16 * rows * width,
        samples * media_len * wide,
    )


def gelu_parts(values):
    half_more = 0.5 * (1.0 + lax.erf(values * 0.7071067811865476))
    slope = half_more + values * jnp.exp(-0.5 * values * values) * 0.3989422804014327
    return values * half_more, slope


def feed_forward(place, state, part, part_other, gain, bias, w_up, w_down, depth, cotangent=None):
    rows, width = state.shape
    units = w_up.shape[2]
    step = min(256, units)
    steps = units // step
    back = cotangent is not None
    halved = part.shape[0] < rows

    def body(place_ref, state_ref, part_ref, other_ref, gain_ref, bias_ref, up_ref, down_ref, *refs):
        if back:
            cot_ref, mid_ref, x_ref, pre_ref, hid_ref, out_ref, du_ref, dx_ref, dyb_ref = refs
        else:
            mid_ref, x_ref, pre_ref, hid_ref, out_ref = refs
        at = pl.program_id(0)

        @pl.when(at == 0)
        def _():
            if halved:
                middle = state_ref[...] + joined(place_ref[0], part_ref[...], other_ref[...])
            else:
                middle = state_ref[...] + (part_ref[...] + other_ref[...])
            mid_ref[...] = middle
            normed, _, _ = row_norm(middle)
            x_ref[...] = (normed * gain_ref[...] + bias_ref[...]).astype(BF16)
            out_ref[...] = jnp.zeros_like(out_ref)
            if back:
                dx_ref[...] = jnp.zeros_like(dx_ref)
                dyb_ref[...] = cot_ref[...].astype(BF16)

        pre = jnp.dot(x_ref[...], up_ref[...], preferred_element_type=F32)
        pre_ref[...] = pre
        hidden, slope = gelu_parts(pre)
        hidden = hidden.astype(BF16)
        hid_ref[...] = hidden.astype(F32)
        out_ref[...] += jnp.dot(hidden, down_ref[...], preferred_element_type=F32)
        if back:
            du = (mm_bt(dyb_ref[...], down_ref[...]) * slope).astype(BF16)
            du_ref[...] = du.astype(F32)
            dx_ref[...] += mm_bt(du, up_ref[...])

    full = whole((rows, width))
    columns = pl.BlockSpec((rows, step), lambda i, *_: (0, i))
    ins = [(value, whole(value.shape)) for value in (state, part, part_other, gain, bias)]
    ins += [(w_up, pl.BlockSpec((None, width, step), lambda i, *_: (depth, 0, i))), (w_down, pl.BlockSpec((None, step, width), lambda i, *_: (depth, i, 0)))]
    outs = [
        ((rows, width), F32, full),
        ((rows, width), BF16, full),
        ((rows, units), F32, columns),
        ((rows, units), F32, columns),
        ((rows, width), F32, full),
    ]
    scratch = []
    if back:
        ins.append((cotangent, full))
        outs += [((rows, units), F32, columns), ((rows, width), F32, full)]
        scratch = [pltpu.VMEM((rows, width), BF16)]
    return call(
        body, [place], (steps,), ins, outs, scratch, "feed_forward",
        2 * rows * width * units * (4 if back else 2), 4 * width * units + 30 * rows * width, rows * units,
    )


def feed_back(middle_grad, state, grad_x, grad_x_other, gain, pre, w_up, w_down, depth):
    rows, width = state.shape
    units = w_up.shape[2]
    step = min(256, units)
    steps = units // step

    def body(grad_ref, state_ref, gx_ref, gy_ref, gain_ref, pre_ref, up_ref, down_ref, up_out, sums_ref, du_ref, dx_ref, dyb_ref):
        at = pl.program_id(0)

        @pl.when(at == 0)
        def _():
            upstream, sums = latent_back(grad_ref[...], state_ref[...], gx_ref[...] + gy_ref[...], gain_ref[...])
            up_out[...] = upstream
            sums_ref[...] = sums
            dyb_ref[...] = upstream.astype(BF16)
            dx_ref[...] = jnp.zeros_like(dx_ref)

        _, slope = gelu_parts(pre_ref[...])
        du = (mm_bt(dyb_ref[...], down_ref[...]) * slope).astype(BF16)
        du_ref[...] = du.astype(F32)
        dx_ref[...] += mm_bt(du, up_ref[...])

    full = whole((rows, width))
    columns = pl.BlockSpec((rows, step), lambda i: (0, i))
    ins = [(value, whole(value.shape)) for value in (middle_grad, state, grad_x, grad_x_other, gain)]
    ins += [(pre, columns)]
    ins += [(w_up, pl.BlockSpec((None, width, step), lambda i: (depth, 0, i))), (w_down, pl.BlockSpec((None, step, width), lambda i: (depth, i, 0)))]
    return call(
        body, [], (steps,), ins,
        [((rows, width), F32, full), ((8, width), F32, whole((8, width))), ((rows, units), F32, columns), ((rows, width), F32, full)],
        [pltpu.VMEM((rows, width), BF16)], "feed_back",
        4 * rows * width * units, 4 * width * units + 30 * rows * width, rows * units,
    )


def latent_back(middle_grad, state, grad_x, gain):
    normed, _, rstd = row_norm(state)
    upstream = middle_grad + row_norm_back(grad_x, gain, normed, rstd)
    gain_sum = jnp.sum(grad_x * normed, axis=0, keepdims=True)
    bias_sum = jnp.sum(grad_x, axis=0, keepdims=True)
    return upstream, jnp.concatenate([gain_sum, bias_sum, jnp.zeros((6, gain_sum.shape[1]), F32)], axis=0)


def latent_end(middle_grad, state, grad_x, grad_x_other, gain, latent_rows):
    rows, width = state.shape

    def body(grad_ref, state_ref, gx_ref, gy_ref, gain_ref, out_ref):
        upstream, sums = latent_back(grad_ref[...], state_ref[...], gx_ref[...] + gy_ref[...], gain_ref[...])
        total = upstream[:latent_rows]
        for clip in range(1, rows // latent_rows):
            total = total + upstream[clip * latent_rows : (clip + 1) * latent_rows]
        out_ref[...] = jnp.concatenate([sums, total], axis=0)

    ins = [(value, whole(value.shape)) for value in (middle_grad, state, grad_x, grad_x_other, gain)]
    shape = (8 + latent_rows, width)
    return call(body, [], (1,), ins, [(shape, F32, whole(shape))], [], "latent_end", rows * width * 20, rows * width * 16)[0]


def attend_back(
    upstream, middle, grad_mine, grad_other, place, counts, ff_gain, media_gain, media_bias,
    w_query, w_pairs, w_out, w_key, w_value, depth, queries, lat_pair, attended, log_total, latent_x, media_pair, media_x,
    latent_rows, frames, patches,
):
    rows, width = middle.shape
    samples = counts.shape[0]
    wide = w_query.shape[1]
    own = w_key.shape[2]
    turns = len(w_pairs)
    heads = wide // HEAD_DIM
    scale = HEAD_DIM ** (-0.5)
    media_len = frames * patches

    def body(
        counts_ref, place_ref, up_ref, mid_ref, mine_ref, other_ref, ffg_ref, mg_ref, mb_ref,
        wq_ref, wo_ref, *refs,
    ):
        wp_refs = refs[:turns]
        wk_ref, wv_ref, q_ref, lat_ref, att_ref, log_ref, x_ref, pair_ref, mx_ref = refs[turns : turns + 9]
        grad_mid_ref, grad_pair_ref, grad_x_ref, grad_w_ref, sums_ref = refs[turns + 9 : turns + 14]
        low_ref, dq_ref, dlat_ref, col_ref, sum_ref = refs[turns + 14 :]
        clip = pl.program_id(0)

        @pl.when(clip == 0)
        def _():
            grad_x = joined(place_ref[0], mine_ref[...], other_ref[...])
            normed, _, rstd = row_norm(mid_ref[...])
            sums_ref[...] = jnp.zeros_like(sums_ref)
            sums_ref[0:1, :] = jnp.sum(grad_x * normed, axis=0, keepdims=True)
            sums_ref[1:2, :] = jnp.sum(grad_x, axis=0, keepdims=True)
            grad_mid = up_ref[...] + row_norm_back(grad_x, ffg_ref[...], normed, rstd)
            grad_mid_ref[...] = grad_mid
            low_ref[...] = grad_mid.astype(BF16)
            grad_w_ref[...] = jnp.zeros_like(grad_w_ref)
            col_ref[...] = jnp.zeros_like(col_ref)

        at = pl.ds(pl.multiple_of(clip * latent_rows, latent_rows), latent_rows)
        query = spread(q_ref[at, :], heads)
        grad_rows = mm_bt(low_ref[at, :], wo_ref[...]).astype(BF16)
        grad_att = spread(grad_rows, heads)
        cross = spread(grad_rows.astype(F32) * att_ref[at, :], heads)
        cross = jnp.broadcast_to(jnp.sum(cross, axis=1, keepdims=True), (wide, 128))
        delta = jnp.transpose(cross, (1, 0))[0:1, :]
        log = log_ref[0][0:1, :]

        def grads_of(keys, values, alive):
            score = mm_bt(keys, query) * scale
            dprob = mm_bt(values, grad_att)
            probs = jnp.exp(score - log)
            if alive is not None:
                probs = jnp.where(alive, probs, 0.0)
            dscore = (probs * (dprob - delta)).astype(BF16)
            grad_key = (jnp.dot(dscore, query, preferred_element_type=F32) * scale).astype(BF16)
            grad_value = jnp.dot(probs.astype(BF16), grad_att, preferred_element_type=F32).astype(BF16)
            grad_pair = []
            for turn in range(turns):
                grad_pair += [grad_key[:, turn * own : (turn + 1) * own], grad_value[:, turn * own : (turn + 1) * own]]
            return dscore, jnp.concatenate(grad_pair, axis=1)

        lat_keys = keys_of(lat_ref, at, own)
        lat_dscore, dlat_ref[at, :] = grads_of(lat_keys, values_of(lat_ref, at, own), None)

        def over(count):
            dq = dot_rows(lat_dscore, lat_keys)
            for frame in range(count):
                here = slice(frame * patches, (frame + 1) * patches)
                keys = keys_of(pair_ref, here, own)
                alive = counts_ref[clip] > frame if frame == count - 1 else None
                dscore, grad_pair = grads_of(keys, values_of(pair_ref, here, own), alive)
                grad_pair_ref[here, :] = grad_pair
                dq = dq + dot_rows(dscore, keys)
            rows_live = slice(0, count * patches)
            grad_own = grad_pair_ref[rows_live, : 2 * own]
            grad_w_ref[: 2 * own, :] += dot_rows(grad_own, mx_ref[rows_live, :])
            col_ref[0:1, :] += jnp.sum(grad_own.astype(F32), axis=0, keepdims=True)
            sum_ref[...] = dq

        for count in range(2, frames + 1, 2):
            pl.when((counts_ref[clip] + 1) // 2 * 2 == count)(functools.partial(over, count))
        dq = sum_ref[...]
        dq_ref[at, :] = (collect(dq, heads) * scale).astype(BF16)

        @pl.when(clip == samples - 1)
        def _():
            dq_all = dq_ref[...]
            dlat = dlat_ref[...]
            grad_x = mm_bt(dq_all, wq_ref[...])
            for turn in range(turns):
                grad_x += mm_bt(dlat[:, 2 * own * turn : 2 * own * (turn + 1)], wp_refs[turn][...])
            grad_x_ref[...] = grad_x
            columns = jnp.transpose(col_ref[...], (1, 0))
            total_one = jnp.zeros((1, width), F32)
            total_two = jnp.zeros((1, width), F32)
            for slot, own_ref in enumerate((wk_ref, wv_ref)):
                weight = jnp.transpose(own_ref[...].astype(F32), (1, 0))
                column = columns[slot * own : (slot + 1) * own, 0:1]
                media_w = grad_w_ref[slot * own : (slot + 1) * own, :]
                total_one += jnp.sum(weight * (media_w - column * mb_ref[...]), axis=0, keepdims=True)
                total_two += jnp.sum(weight * column, axis=0, keepdims=True)
            sums_ref[2:3, :] = total_one / mg_ref[...]
            sums_ref[3:4, :] = total_two
            x = x_ref[...]
            grad_w_ref[: 2 * own, :] += dot_rows(dlat[:, : 2 * own], x)
            grad_w_ref[2 * own : 3 * own, :] = dot_rows(dq_all[:, :own], x)
            grad_w_ref[3 * own :, :] = dot_rows(att_ref[:, :own].astype(BF16), low_ref[...])

    clip_rows = lambda cols, count: pl.BlockSpec((count, cols), lambda clip, *_: (clip, 0))
    full = whole((rows, width))
    ins = [(value, whole(value.shape)) for value in (
        upstream, middle, grad_mine, grad_other, ff_gain, media_gain, media_bias,
        w_query, w_out, *w_pairs)]
    ins += [(value, pl.BlockSpec((None, width, own), lambda *_: (depth, 0, 0))) for value in (w_key, w_value)]
    ins += [(value, whole(value.shape)) for value in (queries, lat_pair, attended)]
    ins += [(log_total, pl.BlockSpec((1, 8, wide), lambda clip, *_: (clip, 0, 0))), (latent_x, full)]
    ins += [(media_pair, clip_rows(2 * wide, media_len)), (media_x, clip_rows(width, media_len))]
    outs = [
        ((rows, width), F32, full),
        (media_pair.shape, BF16, clip_rows(2 * wide, media_len)),
        ((rows, width), F32, full),
        ((4 * own, width), F32, whole((4 * own, width))),
        ((8, width), F32, whole((8, width))),
    ]
    scratch = [
        pltpu.VMEM((rows, width), BF16),
        pltpu.VMEM((rows, wide), BF16),
        pltpu.VMEM((rows, 2 * wide), BF16),
        pltpu.VMEM((8, 2 * own), F32),
        pltpu.VMEM((wide, wide), F32),
    ]
    return call(
        body, [counts, place], (samples,), ins, outs, scratch, "attend_back",
        2 * samples * media_len * (5 * wide * wide + 2 * own * width),
        samples * media_len * (8 * wide + 2 * width) + 40 * rows * width, samples * media_len * wide,
    )


def outer_sums(pairs, planes, name):
    count, wide = pairs[0][0].shape
    units = pairs[0][2].shape[1]
    chunk = wide // planes
    step = min(512, units)

    def body(*refs):
        out_ref = refs[-1]
        for pair in range(len(pairs)):
            mine, other, rows, rows_other = [ref[...].astype(BF16) for ref in refs[4 * pair : 4 * pair + 4]]
            total = dot_rows(mine, rows) + dot_rows(other, rows_other)
            for plane in range(planes):
                out_ref[plane, pair] = total[plane * chunk : (plane + 1) * chunk, :]

    ins = []
    for pair in pairs:
        ins += [(value, whole(value.shape)) for value in pair[:2]]
        ins += [(value, pl.BlockSpec((count, step), lambda i: (0, i))) for value in pair[2:]]
    shape = (planes, len(pairs), chunk, units)
    return call(
        body, [], (units // step,), ins,
        [(shape, F32, pl.BlockSpec((planes, len(pairs), chunk, step), lambda i: (0, 0, 0, i)))], [], name,
        4 * len(pairs) * count * wide * units, 4 * len(pairs) * wide * units,
    )[0]


def media_back(grad_pairs, pairs, weights, gain_means, bias_means, gains, media, time_rows, stats, counts, place, frames, patches, groups):
    rows, width = media.shape
    layers = len(pairs)
    turns = len(weights[0])
    wide2 = pairs[0].shape[1]
    chip = width // groups
    half = chip // 2
    group = frames_in_block(frames)
    groups_of = frames // group
    samples = counts.shape[0]

    def body(counts_ref, place_ref, *refs):
        grad_refs = refs[:layers]
        pair_refs = refs[layers : 2 * layers]
        weight_refs = refs[2 * layers : (2 + turns) * layers]
        gm_ref, bm_ref, gain_ref, media_ref, time_ref, stat_ref, mine_ref, theirs_ref = refs[(2 + turns) * layers :]
        part = wide2 // turns
        clip, at = pl.program_id(0), pl.program_id(1)
        def work(inners):
            for inner in inners:
                here = slice(inner * patches, (inner + 1) * patches)
                total = jnp.zeros((patches, chip), F32)
                one = jnp.zeros((patches, wide2), F32)
                two = jnp.zeros((patches, wide2), F32)
                for layer in range(layers):
                    grad = grad_refs[layer][here, :]
                    product = jnp.zeros((patches, chip), F32)
                    for turn in range(turns):
                        product += mm_bt(grad[:, turn * part : (turn + 1) * part], weight_refs[layer * turns + turn][...])
                    total = total + product * gain_ref[layer : layer + 1, :]
                    grad = grad.astype(F32)
                    one = one + grad * gm_ref[layer : layer + 1, :]
                    two = two + grad * (pair_refs[layer][here, :].astype(F32) - bm_ref[layer : layer + 1, :])
                mean_one = jnp.sum(one, axis=1, keepdims=True)
                mean_two = jnp.sum(two, axis=1, keepdims=True) * (1.0 / width)
                stat = stat_ref[here, :]
                mean, rstd = stat[:, 0:1], stat[:, 64:65]
                normed = (media_ref[here, :].astype(F32) + time_ref[pl.ds(at * group + inner, 1), :] - mean) * rstd
                out = rstd * (total - mean_one - normed * mean_two)
                low, high = out[:, :half], out[:, half:]
                first = place_ref[0] == 0
                mine_ref[here, :] = jnp.where(first, low, high)
                theirs_ref[here, :] = jnp.where(first, high, low)

        def dead(inner):
            here = slice(inner * patches, (inner + 1) * patches)
            mine_ref[here, :] = jnp.zeros((patches, half), F32)
            theirs_ref[here, :] = jnp.zeros((patches, half), F32)

        by_live_spans(at, counts_ref[clip], group, work, dead)

        @pl.when(at * group >= counts_ref[clip])
        def _():
            for inner in range(group):
                dead(inner)

    block = live_block(group, groups_of)

    def chip_block(clip, at, counts_ref, place_ref):
        return (block(clip, at, counts_ref)[0], place_ref[1])

    deep = group * patches
    pair_spec = pl.BlockSpec((deep, wide2), block)
    out_spec = pl.BlockSpec((deep, half), lambda clip, at, *_: (clip * groups_of + at, 0))
    by_chip = lambda count: pl.BlockSpec((count, chip), lambda clip, at, counts_ref, place_ref: (0, place_ref[1]))
    ins = [(value, pair_spec) for value in (*grad_pairs, *pairs)]
    ins += [
        (value, pl.BlockSpec((chip, wide2 // turns), lambda clip, at, counts_ref, place_ref: (place_ref[1], 0)))
        for pieces in weights for value in pieces
    ]
    ins += [
        (gain_means, whole(gain_means.shape)), (bias_means, whole(bias_means.shape)),
        (gains, by_chip(layers)), (media, pl.BlockSpec((deep, chip), chip_block)), (time_rows, by_chip(frames)),
        (stats, pl.BlockSpec((deep, 128), block)),
    ]
    return call(
        body, [counts, place], (samples, groups_of), ins,
        [((rows, half), F32, out_spec)] * 2, [], "media_back",
        2 * rows * wide2 * chip * layers, rows * (wide2 * 4 * layers + 6 * chip),
    )


def media_sum(mine, arrived, frames, patches, samples):
    rows, width = mine.shape
    group = frames_in_block(frames)
    groups = frames // group
    deep = group * patches

    def body(mine_ref, arrived_ref, out_ref, sum_ref):
        clip, at = pl.program_id(0), pl.program_id(1)

        @pl.when((clip == 0) & (at == 0))
        def _():
            sum_ref[...] = jnp.zeros_like(sum_ref)

        total = mine_ref[...] + arrived_ref[...]
        out_ref[...] = total.astype(BF16)
        lines = [jnp.sum(total[i * patches : (i + 1) * patches], axis=0, keepdims=True) for i in range(group)]
        for piece in range(groups):

            @pl.when(at == piece)
            def _():
                for i in range(group):
                    frame = piece * group + i
                    sum_ref[frame : frame + 1, :] += lines[i]

    spec = pl.BlockSpec((deep, width), lambda clip, at: (clip * groups + at, 0))
    return call(
        body, [], (samples, groups), [(mine, spec), (arrived, spec)],
        [((rows, width), BF16, spec), ((frames, width), F32, whole((frames, width)))], [], "media_sum",
        2 * rows * width, 10 * rows * width,
    )


def finish_ff(ups, downs):
    layers = len(ups)
    chunk, units = ups[0][2], ups[0][0].shape[1]

    def body(*refs):
        up_ref, down_ref = refs[2 * layers :]
        for layer in range(layers):
            up_ref[layer] = refs[layer][...]
            down_ref[layer] = jnp.transpose(refs[layers + layer][...], (1, 0))

    ins = [
        (value, pl.BlockSpec((chunk, units), lambda i, at=at: (at, 0))) for value, at, _ in (*ups, *downs)
    ]
    shapes = [(layers, chunk, units), (layers, units, chunk)]
    return call(
        body, [], (1,), ins, [(shape, F32, whole(shape)) for shape in shapes], [], "finish_ff",
        4 * layers * chunk * units, 16 * layers * chunk * units,
    )


def finish_attn(attn, layers, own):
    chunk = attn.shape[1]

    def body(attn_ref, query_ref, key_ref, value_ref, out_ref):
        for layer in range(layers):
            for slot, ref in enumerate((key_ref, value_ref, query_ref, out_ref)):
                at = (4 * layer + slot) * own
                part = attn_ref[at : at + own, :]
                ref[layer] = part if slot == 3 else jnp.transpose(part, (1, 0))

    shapes = [(layers, chunk, own)] * 3 + [(layers, own, chunk)]
    return call(
        body, [], (1,), [(attn, whole(attn.shape))], [(shape, F32, whole(shape)) for shape in shapes], [], "finish_attn",
        attn.size, 8 * attn.size,
    )


class Links:

    def __init__(self, zero):
        self.zero = zero
        self.planes = lax.axis_size("plane")
        self.groups = lax.axis_size("group")
        self.plane = lax.axis_index("plane")
        self.side = lax.axis_index("side")
        self.group = lax.axis_index("group")
        self.core = lax.axis_index("core")

    def rounded(self, value):
        return (value + self.zero).astype(BF16)

    def core_swap(self, value):
        return lax.ppermute(value, "core", [(0, 1), (1, 0)])

    def side_swap(self, value):
        return lax.ppermute(value, "side", [(0, 1), (1, 0)])

    def group_turn(self, value, turn):
        return lax.ppermute(value, "group", [(i, (i + turn) % self.groups) for i in range(self.groups)])

    def cut(self, value, index):
        half = value.shape[0] // 2
        return lax.dynamic_slice_in_dim(value, index * half, half, 0)

    def join(self, mine, other, index):
        first = index == 0
        return jnp.concatenate([jnp.where(first, mine, other), jnp.where(first, other, mine)], axis=0)

    def core_half(self, value):
        return self.cut(value, self.core) + self.core_swap(self.cut(value, 1 - self.core))

    def group_turns(self, value):
        return [self.group_turn(value, k) for k in range(1, self.groups)]

    def group_total(self, value, turned):
        if self.groups == 2:
            return value + turned[0]
        turned = jnp.stack([value] + turned)
        total = None
        for source in range(self.groups):
            slot = lax.rem(self.group - source + self.groups, self.groups)
            term = lax.dynamic_index_in_dim(turned, slot, 0, keepdims=False)
            total = term if total is None else total + term
        return total

    def tensor_halves(self, value):
        mine = self.core_half(value)
        mine = self.group_total(mine, self.group_turns(mine))
        return mine, self.core_swap(mine)

    def dp_sum(self, value):
        value = value + self.side_swap(value)
        step = 1
        while step < self.planes:
            value = value + lax.ppermute(value, "plane", [(i, i ^ step) for i in range(self.planes)])
            step *= 2
        return value

    def columns(self, value, side):
        wide = value.shape[1] // (2 * self.planes)
        cuts = [value[:, i * wide : (i + 1) * wide] for i in range(2 * self.planes)]
        return jnp.where(side == 0, jnp.concatenate(cuts[0::2], axis=1), jnp.concatenate(cuts[1::2], axis=1))

    def both_columns(self, value):
        return self.columns(value, self.side), self.side_swap(self.columns(value, 1 - self.side))

    def scatter(self, value, dimension):
        return lax.psum_scatter(value, "plane", scatter_dimension=dimension, tiled=True)


def local(
    media,
    frame_counts,
    time_embed,
    latents,
    media_gain,
    media_bias,
    latent_gain,
    latent_bias,
    ff_gain,
    ff_bias,
    w_query,
    w_key,
    w_value,
    w_out,
    w_up,
    w_down,
    cotangent,
):
    links = Links(jnp.where(frame_counts[0] > 1000000, 1.0, 0.0).astype(F32))
    samples, media_len, width = media.shape
    frames = time_embed.shape[0]
    patches = media_len // frames
    latent_rows = latents.shape[0]
    own = w_query.shape[2]
    layers = w_query.shape[0]
    wide = own * links.groups
    rows = samples * latent_rows
    tensor_size = 2 * links.groups
    turns = range(1, links.groups)
    place = jnp.stack([links.core, links.group, links.side]).astype(jnp.int32)

    def row(value, depth):
        return value[depth : depth + 1]

    def after(values, event):
        return lax.optimization_barrier((values, event))

    def project(depth, x, pair, weight, nears, fars):
        pieces = [weight]
        for k in turns:
            far = None if fars is None else fars[k - 1]
            pair, weight, *x_made = project_more(x, frame_counts, place, pair, nears[k - 1], far, k, frames, patches)
            if x_made:
                (x,) = x_made
            pieces.append(weight)
        return x, pair, pieces

    def packed(wanted, event):
        (pairs, queries, outs), event = after(((w_key, w_value), (w_query,), (w_out,)), event)
        weights = {"pair": pairs, "query": queries, "out": outs}
        values = pack(place, [(weights[name], depth, name == "pair") for name, depth in wanted], "pack")
        return lax.optimization_barrier((values, event))

    def by_side(nears):
        return [links.side_swap(value) for value in nears]

    def more_of(depth):
        return [(query, None, out, None) for query, out in zip(nears["query", depth], nears["out", depth])]

    media_rows = media.reshape(samples * media_len, width)
    time_rows = time_embed.astype(F32)

    def prepared(depth, media_then):
        return prepare(
            media_then, frame_counts, time_rows, row(media_gain, depth), row(media_bias, depth),
            w_key, w_value, depth, links.groups, frames, patches,
        )

    nears = {}
    media_then = media_rows
    if layers > 1:
        wanted = [("pair", 1), ("query", 1), ("pair", 0), ("out", 1)]
        values, media_then = packed(wanted, media_rows)
        nears.update((name, links.group_turns(value)) for name, value in zip(wanted, values))
    stats, pair, weight = prepared(0, media_then)
    media_x, media_pair, w_pairs = [None], [pair], [[weight]]
    fars = {}
    more = [[]]

    state_in = (jnp.broadcast_to(latents.astype(F32)[None], (samples, latent_rows, width)).reshape(rows, width),)
    cotangent_rows = cotangent.reshape(rows, width)
    low_cotangent, stats = after(cotangent_rows.astype(BF16).astype(F32), stats)
    upstream_cols = links.both_columns(low_cotangent)
    saved = []
    early = []

    def attended_layer(depth, state_in, more, pieces, pair):
        return attend(
            state_in, place, frame_counts, row(latent_gain, depth), row(latent_bias, depth),
            w_query, w_out, more, pieces, depth, pair, latent_rows, frames, patches,
        )

    for depth in range(layers):
        last = depth == layers - 1
        state, latent_x, queries, lat_pair, attended, log_total, part, query4, out4 = attended_layer(
            depth, state_in, more[depth], w_pairs[depth], media_pair[depth]
        )
        if depth == 0:
            if not last:
                names = [(name, 1) for name in ("pair", "query")]
                arrived, part = after([nears[name] for name in names], part)
                nears.update(zip(names, arrived))
                fars["pair", 1] = by_side(nears["pair", 1])
            mine = links.core_half(part)
            if last:
                part = links.tensor_halves(part)
            else:
                media_then, mine = after(media_rows, mine)
                first_sent, mine = packed([("query", 0), ("out", 0)], mine)
                turned = links.group_turns(mine)
                x, pair, weight = prepared(1, media_then)
                arrived = (turned, nears["out", 1], nears["pair", 0], upstream_cols)
                (turned, nears["out", 1], nears["pair", 0], upstream_cols), x = after(arrived, x)
                mine = links.group_total(mine, turned)
                fars["pair", 1], mine = after(fars["pair", 1], mine)
                part = (mine, links.core_swap(mine))
        else:
            if depth == 1:
                fars["pair", 0], part = after(fars["pair", 0], part)
            part = (part, links.core_swap(part))
        middle, ff_x, pre, hidden, out_part, *back = feed_forward(
            place, state, *part, row(ff_gain, depth), row(ff_bias, depth),
            w_up, w_down, depth, cotangent_rows if last else None,
        )
        saved.append((state, latent_x, queries, lat_pair, attended, log_total, middle, pre, hidden, query4, out4))
        if last:
            hidden_other = links.side_swap(hidden)
            (ff_x, back[0]), hidden_other = after((ff_x, back[0]), hidden_other)
            early.append((hidden_other, links.both_columns(ff_x.astype(F32))))
            continue
        early.append((hidden, ff_x))
        mine = links.core_half(out_part)
        if depth > 0:
            media_then, mine = after(media_rows, mine)
            x, pair, weight = prepared(depth + 1, media_then)
        (x, fars["pair", depth + 1], ff_x), mine = after((x, fars["pair", depth + 1], ff_x), mine)
        ff_x_cols = links.both_columns(ff_x.astype(F32))
        turned = links.group_turns(mine)
        _, pair, pieces = project(depth + 1, x, pair, weight, nears["pair", depth + 1], fars["pair", depth + 1])
        if depth == 0:
            (turned, nears["pair", 0]), pair = after((turned, nears["pair", 0]), pair)
            fars["pair", 0] = by_side(nears["pair", 0])
        else:
            turned, pair = after(turned, pair)
        media_x.append(x)
        media_pair.append(pair)
        w_pairs.append(pieces)
        mine = links.group_total(mine, turned)
        state_in = (middle, mine, links.core_swap(mine))
        ff_x_cols, state_in = after(ff_x_cols, state_in)
        early[depth] = (early[depth][0], ff_x_cols)
        more.append(more_of(depth + 1))
    mine, out_mine = links.core_half(back[1]), links.core_half(out_part)
    turned, out_turned = links.group_turns(mine), links.group_turns(out_mine)
    hidden_other = early[-1][0]
    if layers > 1:
        (media_then, pair), mine = after((media_rows, media_pair[0]), mine)
        source = (media_then, time_rows, row(media_gain, 0), row(media_bias, 0))
        media_x[0], media_pair[0], w_pairs[0] = project(
            0, source, pair, w_pairs[0][0], nears["pair", 0], fars["pair", 0]
        )
        arrived = (turned, out_turned, hidden_other)
        (turned, out_turned, hidden_other), media_pair[0] = after(arrived, media_pair[0])
    early[-1] = (hidden_other, early[-1][1])
    back[1] = links.group_total(mine, turned)
    out_mine = links.group_total(out_mine, out_turned)
    sums = (out_mine, links.core_swap(out_mine))
    resampled = middle + links.join(*sums, links.core)

    upstream = cotangent_rows
    grads = [None] * layers
    gains = [None] * layers
    pair_grads = [None] * layers
    attn_ws = [None] * layers
    units = w_up.shape[2]
    for depth in reversed(range(layers)):
        state, latent_x, queries, lat_pair, attended, log_total, middle, pre, hidden, query4, out4 = saved[depth]
        if depth == layers - 1:
            grad_pre, grad_ffx = back
        else:
            upstream, latent_sums, grad_pre, grad_ffx = feed_back(
                grad_middle, saved[depth + 1][0], grad_x, grad_x_other, row(latent_gain, depth + 1),
                pre, w_up, w_down, depth,
            )
            gains[depth + 1] += (latent_sums[0], latent_sums[1])
            upstream_cols = links.both_columns(upstream.astype(BF16).astype(F32))
            if depth == 0:
                media_pair[0], (grad_pre, up_sums) = after(media_pair[0], (grad_pre, up_sums))
                more[0] = more_of(0)
                _, latent_x, queries, lat_pair, attended, log_total, _, query4, out4 = attended_layer(
                    0, (state,), more[0], w_pairs[0], media_pair[0]
                )
                upstream_cols, queries = after(upstream_cols, queries)
        hidden_other, ff_x_cols = early[depth]
        down = (*upstream_cols, hidden, hidden_other)
        up = (*ff_x_cols, grad_pre, links.side_swap(grad_pre))
        if depth == layers - 1:
            grad_mine, grad_other = grad_ffx, links.core_swap(grad_ffx)
        else:
            grad_mine, grad_other = links.tensor_halves(grad_ffx)
        if depth == layers - 1:
            down = outer_sums([down], links.planes, "down_sums")
            grad_mine, down = after(grad_mine, down)
            if depth > 0:
                first_sent, down = after(first_sent, down)
                first_near = [links.group_turns(value) for value in first_sent]
            grad_down = links.scatter(down.reshape(-1, units), 0)
            grad_down = (grad_down, 0, grad_down.shape[0])
        else:
            both = outer_sums([down, up], links.planes, "ff_sums")
            grad_mine, both = after(grad_mine, both)
            above, both = after(attn_ws[depth + 1], both)
            attn_ws[depth + 1] = above[0] + links.side_swap(above[1])
            both = links.scatter(both.reshape(-1, units), 0)
            grad_down, grad_up = (both, 0, both.shape[0] // 2), (both, 1, both.shape[0] // 2)
        grad_middle, pair_grads[depth], grad_x, attn_w, sums = attend_back(
            upstream, middle, grad_mine, grad_other, place, frame_counts,
            row(ff_gain, depth), row(media_gain, depth), row(media_bias, depth),
            query4, w_pairs[depth], out4, w_key, w_value, depth, queries, lat_pair, attended, log_total, latent_x,
            media_pair[depth], media_x[depth], latent_rows, frames, patches,
        )
        if depth == layers - 1:
            (pre_other, first_near), grad_x = after((up[3], first_near), grad_x)
            nears["query", 0], nears["out", 0] = first_near
            up_sums = outer_sums([(*up[:3], pre_other)], links.planes, "up_sums")
            hidden, up_sums = after(early[0][0], up_sums)
            early[0] = (links.side_swap(hidden), early[0][1])
            grad_up = links.scatter(up_sums.reshape(-1, units), 0)
            grad_up = (grad_up, 0, grad_up.shape[0])
        if depth < layers - 1:
            attn_ws[depth + 1], attn_w = after(attn_ws[depth + 1], attn_w)
        grad_x_other = links.core_swap(grad_x)
        attn_ws[depth] = (links.columns(attn_w, links.side), links.columns(attn_w, 1 - links.side))
        grads[depth] = (grad_up, grad_down)
        gains[depth] = (sums[0], sums[1], sums[2], sums[3])
    ending = latent_end(grad_middle, saved[0][0], grad_x, grad_x_other, row(latent_gain, 0), latent_rows)
    gains[0] += (ending[0], ending[1])
    latent_part = ending[8:]
    share = 1.0 / tensor_size
    gains = [(g[2], g[3], g[4] * share, g[5] * share, g[0] * share, g[1] * share) for g in gains]

    core_width = width // tensor_size
    weight_long = [jnp.concatenate(w_pairs[l], axis=1).astype(F32) for l in range(layers)]
    gain_means = jnp.stack([jnp.sum(weight_long[l] * media_gain[l][:, None], axis=0) / width for l in range(layers)])
    bias_means = jnp.stack([jnp.sum(weight_long[l] * media_bias[l][:, None], axis=0) for l in range(layers)])
    (attn_mine, attn_theirs, grad_x_other), stats = after((*attn_ws[0], grad_x_other), stats)
    attn_theirs = links.side_swap(attn_theirs)
    (stats, *tied) = lax.optimization_barrier((stats, *[value[0] for pair in grads[1:] for value in pair]))
    for depth in range(1, layers):
        grads[depth] = tuple((tied.pop(0), *value[1:]) for value in grads[depth])
    mine, theirs = media_back(
        pair_grads, media_pair, w_pairs, gain_means, bias_means, media_gain, media_rows, time_rows, stats,
        frame_counts, place, frames, patches, links.groups,
    )
    (mine, theirs), attn_theirs = after((mine, theirs), attn_theirs)
    attn_ws[0] = attn_mine + attn_theirs
    media_grad, time_part = media_sum(mine, links.core_swap(theirs), frames, patches, samples)
    media_grad = media_grad.reshape(samples, media_len, core_width)

    def column_cuts(value):
        return [value[:, i * core_width : (i + 1) * core_width] for i in range(tensor_size)]

    def column_cut(value, index):
        return lax.dynamic_slice_in_dim(value, index * core_width, core_width, 1)

    gain_flat = jnp.stack([gains[l][m] for m in range(6) for l in range(layers)])
    by_core = [jnp.concatenate(column_cuts(gain_flat)[c::2], axis=1) for c in range(2)]
    core_mine = jnp.where(links.core == 0, by_core[0], by_core[1])
    core_theirs = jnp.where(links.core == 0, by_core[1], by_core[0])
    gain_share = core_mine + links.core_swap(core_theirs)
    gain_sum = column_cut(gain_share, links.group)
    for turn in turns:
        target = lax.rem(links.group + turn, links.groups)
        gain_sum = gain_sum + links.group_turn(column_cut(gain_share, target), turn)
    latent_share = column_cut(latent_part, links.group * 2 + links.core)
    small_in = jnp.concatenate([gain_sum, time_part, latent_share], axis=0)
    attn_all, (both_grads, small_in) = after(jnp.concatenate(attn_ws, axis=0), (grads[0][0][0], small_in))
    attn = links.scatter(attn_all, 1)
    small = links.dp_sum(small_in)
    swapped = links.core_swap(small)
    pair = jnp.concatenate(
        [jnp.where(links.core == 0, small, swapped), jnp.where(links.core == 0, swapped, small)], axis=1
    )
    turned = jnp.stack([pair] + [links.group_turn(pair, k) for k in turns])
    order = [lax.rem(links.group - source + links.groups, links.groups) for source in range(links.groups)]
    small_all = jnp.concatenate(
        [lax.dynamic_index_in_dim(turned, slot, 0, keepdims=False) for slot in order], axis=1
    )
    gain_all = small_all[: 6 * layers].reshape(6, layers, width)
    time_grad = small_all[6 * layers : 6 * layers + frames]
    latents_grad = small_all[6 * layers + frames :]
    ups, downs = [grads[l][0] for l in range(layers)], [grads[l][1] for l in range(layers)]
    ups[0], downs[0] = (both_grads, *ups[0][1:]), (both_grads, *downs[0][1:])
    w_up_grad, w_down_grad = finish_ff(ups, downs)
    w_query_grad, w_key_grad, w_value_grad, w_out_grad = finish_attn(attn, layers, own)

    return (
        resampled.reshape(samples, latent_rows, width),
        media_grad,
        time_grad,
        latents_grad,
        gain_all[0],
        gain_all[1],
        gain_all[2],
        gain_all[3],
        gain_all[4],
        gain_all[5],
        w_query_grad,
        w_key_grad,
        w_value_grad,
        w_out_grad,
        w_up_grad,
        w_down_grad,
    )


def solution(mesh):
    dp_size, tensor_size = mesh.devices.shape
    split = jax.sharding.Mesh(
        mesh.devices.reshape(dp_size // 2, 2, tensor_size // 2, 2), ("plane", "side", "group", "core")
    )
    dp, tensor = ("plane", "side"), ("group", "core")
    in_specs = (
        P(dp, None, None),
        P(dp),
        P(),
        P(),
        P(),
        P(),
        P(),
        P(),
        P(),
        P(),
        P(None, None, tensor),
        P(None, None, tensor),
        P(None, None, tensor),
        P(None, tensor, None),
        P(None, None, tensor),
        P(None, tensor, None),
        P(dp, None, None),
    )
    out_specs = (
        P(dp, None, None),
        P(dp, None, tensor),
        P(),
        P(),
        P(),
        P(),
        P(),
        P(),
        P(),
        P(),
        P(None, dp, tensor),
        P(None, dp, tensor),
        P(None, dp, tensor),
        P(None, tensor, dp),
        P(None, dp, tensor),
        P(None, tensor, dp),
    )
    return jax.shard_map(local, mesh=split, in_specs=in_specs, out_specs=out_specs, check_vma=False)
```

```python
import functools

import jax
import jax.numpy as jnp
from jax import lax
from jax.experimental import pallas as pl
from jax.experimental.pallas import tpu as pltpu
from jax.sharding import PartitionSpec as P

HEAD_DIM = 64
EPS = 1e-05
F32 = jnp.float32
BF16 = jnp.bfloat16
VMEM_LIMIT = 62 * 1024 * 1024


def mm(left_side, right_side):
    return jnp.dot(left_side, right_side, preferred_element_type=F32)


def mm_bt(left_side, right_side):
    return lax.dot_general(left_side, right_side, (((1,), (1,)), ((), ())), preferred_element_type=F32)


def mm_at(left_side, right_side):
    return lax.dot_general(left_side, right_side, (((0,), (0,)), ((), ())), preferred_element_type=F32)


def dot_rows(left_side, right_side):
    return lax.dot_general(left_side, right_side, (((0,), (0,)), ((), ())), preferred_element_type=F32)


def row_norm(values):
    count = values.shape[-1]
    mean = jnp.sum(values, axis=-1, keepdims=True) * (1.0 / count)
    centered = values - mean
    rstd = lax.rsqrt(jnp.sum(centered * centered, axis=-1, keepdims=True) * (1.0 / count) + EPS)
    return centered * rstd, mean, rstd


def row_norm_back(grad, gain, normed, rstd):
    count = grad.shape[-1]
    scaled = grad * gain
    mean_one = jnp.sum(scaled, axis=-1, keepdims=True) * (1.0 / count)
    mean_two = jnp.sum(scaled * normed, axis=-1, keepdims=True) * (1.0 / count)
    return rstd * (scaled - mean_one - normed * mean_two)


def whole(shape):
    zeros = (0,) * len(shape)
    return pl.BlockSpec(shape, lambda *_: zeros)


def call(body, scalars, grid, ins, outs, scratch, name, flops, moved, exps=0, aliases=None):
    return pl.pallas_call(
        body,
        out_shape=[jax.ShapeDtypeStruct(shape, dtype) for shape, dtype, _ in outs],
        grid_spec=pltpu.PrefetchScalarGridSpec(
            num_scalar_prefetch=len(scalars),
            grid=grid,
            in_specs=[spec for _, spec in ins],
            out_specs=[spec for _, _, spec in outs],
            scratch_shapes=scratch,
        ),
        compiler_params=pltpu.CompilerParams(
            dimension_semantics=("arbitrary",) * len(grid), vmem_limit_bytes=VMEM_LIMIT
        ),
        cost_estimate=pl.CostEstimate(flops=flops, bytes_accessed=moved, transcendentals=exps),
        name=name,
        input_output_aliases=aliases or {},
    )(*scalars, *[array for array, _ in ins])


def frames_in_block(frames):
    return 4 if frames % 4 == 0 else 1


def by_live_spans(at, live, group, work, dead):
    span = group
    spans = []
    while span:
        spans.append(span)
        span //= 2

    def visit(first, span):
        if span == 1:

            @pl.when(at * group + first < live)
            def _():
                work(range(first, first + 1))

            @pl.when((at * group + first >= live) & (at * group < live))
            def _():
                dead(first)

            return

        @pl.when(at * group + first + span <= live)
        def _():
            work(range(first, first + span))

        @pl.when(at * group + first + span > live)
        def _():
            visit(first, span // 2)
            visit(first + span // 2, span // 2)

    visit(0, group)


def live_block(group, groups):
    def block(clip, at, counts_ref, *_):
        return (clip * groups + jnp.minimum(at, (counts_ref[clip] - 1) // group), 0)

    return block


def pack(place, wanted, name):
    ins, outs, counts = [], [], []
    for weights, depth, halved in wanted:
        count = weights[0].shape[1] // (2 if halved else 1)
        for weight in weights:
            spec = lambda i, place_ref, depth=depth, halved=halved: (depth, place_ref[2] if halved else 0, 0)
            ins.append((weight, pl.BlockSpec((None, count, weight.shape[2]), spec)))
        shape = (count, sum(weight.shape[2] for weight in weights))
        outs.append((shape, F32, whole(shape)))
        counts.append(len(weights))

    def body(place_ref, *refs):
        in_refs, out_refs = list(refs[: len(ins)]), refs[len(ins) :]
        for out_ref, count in zip(out_refs, counts):
            at = 0
            for _ in range(count):
                part = in_refs.pop(0)
                out_ref[:, at : at + part.shape[1]] = part[...].astype(F32)
                at += part.shape[1]

    moved = sum(6 * shape[0] * shape[1] for shape, _, _ in outs)
    return call(body, [place], (1,), ins, outs, [], name, moved, moved)


def keep_rows(ref, first, columns, side, near, far):
    if far is None:
        ref[first : first + near.shape[0], columns] = near[...].astype(BF16)
        return
    half = near.shape[0]
    ref[pl.ds(pl.multiple_of(first + side * half, half), half), columns] = near[...].astype(BF16)
    ref[pl.ds(pl.multiple_of(first + (1 - side) * half, half), half), columns] = far[...].astype(BF16)


def scaled_rows(values, gain, bias):
    normed, mean, rstd = row_norm(values)
    return (normed * gain + bias).astype(BF16), mean, rstd


def prepare(media, counts, time_rows, gain, bias, w_key, w_value, depth, turns, frames, patches):
    rows, width = media.shape
    samples = counts.shape[0]
    own = w_key.shape[2]
    group = frames_in_block(frames)
    groups = frames // group

    def body(counts_ref, media_ref, time_ref, gain_ref, bias_ref, wk_ref, wv_ref, kept_ref, pair_ref, weight_ref):
        clip, at = pl.program_id(0), pl.program_id(1)

        @pl.when((clip == 0) & (at == 0))
        def _():
            weight_ref[...] = jnp.concatenate([wk_ref[...], wv_ref[...]], axis=1)

        def rows_at(inner):
            return slice(inner * patches, (inner + 1) * patches)

        def work(inners):
            for inner in inners:
                here = rows_at(inner)
                values = media_ref[here, :].astype(F32) + time_ref[pl.ds(at * group + inner, 1), :]
                x, mean, rstd = scaled_rows(values, gain_ref[...], bias_ref[...])
                if depth == 0:
                    lane = lax.broadcasted_iota(jnp.int32, (patches, 128), 1)
                    kept_ref[here, :] = jnp.where(lane < 64, mean, rstd)
                else:
                    kept_ref[here, :] = x
                pair_ref[here, :] = jnp.dot(x, weight_ref[...], preferred_element_type=F32).astype(BF16)

        def dead(inner):
            if depth > 0:
                kept_ref[rows_at(inner), :] = jnp.zeros((patches, width), BF16)
            pair_ref[rows_at(inner), :] = jnp.zeros((patches, 2 * own), BF16)

        by_live_spans(at, counts_ref[clip], group, work, dead)

    block = live_block(group, groups)
    deep = group * patches
    row_spec = pl.BlockSpec((deep, width), block)
    weight_spec = pl.BlockSpec((None, width, own), lambda *_: (depth, 0, 0))
    kept = ((rows, 128), F32, pl.BlockSpec((deep, 128), block)) if depth == 0 else ((rows, width), BF16, row_spec)
    return call(
        body, [counts], (samples, groups),
        [(media, row_spec), (time_rows, whole(time_rows.shape)), (gain, whole(gain.shape)), (bias, whole(bias.shape)),
         (w_key, weight_spec), (w_value, weight_spec)],
        [kept, ((rows, 2 * own * turns), BF16, pl.BlockSpec((deep, 2 * own), block)),
         ((width, 2 * own), BF16, whole((width, 2 * own)))],
        [], "prepare", 2 * rows * width * 2 * own, rows * width * 4,
    )


def project_more(source, counts, place, pair, near, far, turn, frames, patches):
    made = isinstance(source, tuple)
    rows, width = (source[0] if made else source).shape
    wide = near.shape[1]
    group = frames_in_block(frames)
    groups = frames // group
    parts = 1 if far is None else 2

    def body(counts_ref, place_ref, *refs):
        x_ref, pair_in_ref, *refs = refs
        halves, refs = refs[:parts], refs[parts:]
        if made:
            time_ref, gain_ref, bias_ref, out_ref, weight_ref, made_ref = refs
        else:
            out_ref, weight_ref = refs
        clip, at = pl.program_id(0), pl.program_id(1)

        @pl.when((clip == 0) & (at == 0))
        def _():
            keep_rows(weight_ref, 0, slice(None), place_ref[2], halves[0], halves[1] if parts == 2 else None)

        def work(inners):
            if made:
                for inner in inners:
                    here = slice(inner * patches, (inner + 1) * patches)
                    values = x_ref[here, :].astype(F32) + time_ref[pl.ds(at * group + inner, 1), :]
                    x, _, _ = scaled_rows(values, gain_ref[...], bias_ref[...])
                    made_ref[here, :] = x
                    out_ref[here, :] = jnp.dot(x, weight_ref[...], preferred_element_type=F32).astype(BF16)
            else:
                here = slice(inners[0] * patches, (inners[-1] + 1) * patches)
                out_ref[here, :] = jnp.dot(x_ref[here, :], weight_ref[...], preferred_element_type=F32).astype(BF16)

        def dead(inner):
            here = slice(inner * patches, (inner + 1) * patches)
            out_ref[here, :] = jnp.zeros((patches, wide), BF16)
            if made:
                made_ref[here, :] = jnp.zeros((patches, width), BF16)

        by_live_spans(at, counts_ref[clip], group, work, dead)

    block = live_block(group, groups)
    deep = group * patches
    row_spec = pl.BlockSpec((deep, width), block)
    halves = [near] if far is None else [near, far]
    ins = [(source[0] if made else source, row_spec), (pair, pl.BlockSpec(memory_space=pl.ANY))]
    ins += [(half, whole(half.shape)) for half in halves]
    outs = [
        (pair.shape, BF16, pl.BlockSpec((deep, wide), lambda clip, at, counts_ref, *_: (block(clip, at, counts_ref)[0], turn))),
        ((width, wide), BF16, whole((width, wide))),
    ]
    if made:
        ins += [(value, whole(value.shape)) for value in source[1:]]
        outs.append(((rows, width), BF16, row_spec))
    return call(
        body, [counts, place], (counts.shape[0], groups), ins, outs, [], "project_more",
        2 * rows * width * wide, 2 * rows * (width + wide), aliases={3: 0},
    )


def spread(rows_of_heads, heads):
    rows, wide = rows_of_heads.shape
    tiled = jnp.concatenate([rows_of_heads] * heads, axis=0)
    head_row = lax.broadcasted_iota(jnp.int32, tiled.shape, 0) // rows
    head_col = lax.broadcasted_iota(jnp.int32, tiled.shape, 1) // (wide // heads)
    return jnp.where(head_row == head_col, tiled, jnp.zeros_like(tiled))


def collect(blocks, heads):
    rows = blocks.shape[0] // heads
    head_col = lax.broadcasted_iota(jnp.int32, (rows, blocks.shape[1]), 1) // (blocks.shape[1] // heads)
    total = jnp.zeros((rows, blocks.shape[1]), blocks.dtype)
    for head in range(heads):
        total = jnp.where(head_col == head, blocks[head * rows : (head + 1) * rows], total)
    return total


def joined(core, mine, other):
    first = core == 0
    return jnp.concatenate([jnp.where(first, mine, other), jnp.where(first, other, mine)], axis=0)


def keys_of(ref, at, own):
    return jnp.concatenate([ref[at, first : first + own] for first in range(0, ref.shape[1], 2 * own)], axis=1)


def values_of(ref, at, own):
    return jnp.concatenate([ref[at, first + own : first + 2 * own] for first in range(0, ref.shape[1], 2 * own)], axis=1)


def attend(state_in, place, counts, gain, bias, w_query, w_out, more, w_pairs, depth, media_pair, latent_rows, frames, patches):
    rows, width = state_in[0].shape
    samples = counts.shape[0]
    own = w_query.shape[2]
    turns = len(w_pairs)
    wide = own * turns
    heads = wide // HEAD_DIM
    scale = HEAD_DIM ** (-0.5)
    media_len = frames * patches
    parts = len(state_in)

    def body(counts_ref, place_ref, *refs):
        state_refs = refs[:parts]
        gain_ref, bias_ref, wq_own_ref, wo_own_ref = refs[parts : parts + 4]
        at_more = parts + 4
        at_pairs = at_more + len(flat)
        more_refs = list(refs[at_more:at_pairs])
        wp_refs = refs[at_pairs : at_pairs + turns]
        pair_ref = refs[at_pairs + turns]
        state_ref, x_ref, q_ref, lat_ref, att_ref, log_ref, part_ref, wq_ref, wo_ref, score_ref, sum_ref = refs[at_pairs + turns + 1 :]
        clip = pl.program_id(0)

        @pl.when(clip == 0)
        def _():
            state = state_refs[0][...]
            if parts == 3:
                state = state + joined(place_ref[0], state_refs[1][...], state_refs[2][...])
            state_ref[...] = state
            normed, _, _ = row_norm(state)
            x = (normed * gain_ref[...] + bias_ref[...]).astype(BF16)
            x_ref[...] = x
            wq_ref[:, :own] = wq_own_ref[...]
            wo_ref[:own, :] = wo_own_ref[...]
            for turn, halves in enumerate(more, 1):
                loaded = [None if half is None else more_refs.pop(0) for half in halves]
                keep_rows(wq_ref, 0, slice(turn * own, (turn + 1) * own), place_ref[2], *loaded[:2])
                keep_rows(wo_ref, turn * own, slice(None), place_ref[2], *loaded[2:])
            q_ref[...] = jnp.dot(x, wq_ref[...], preferred_element_type=F32).astype(BF16)
            for turn in range(turns):
                lat_ref[:, 2 * own * turn : 2 * own * (turn + 1)] = jnp.dot(
                    x, wp_refs[turn][...], preferred_element_type=F32
                ).astype(BF16)

        at = pl.ds(pl.multiple_of(clip * latent_rows, latent_rows), latent_rows)
        queries = spread(q_ref[at, :], heads)
        lat_score = mm_bt(keys_of(lat_ref, at, own), queries) * scale
        lat_top = jnp.max(lat_score, axis=0, keepdims=True)

        def over(count):
            scores, top = [], lat_top
            for frame in range(count):
                score = mm_bt(keys_of(pair_ref, slice(frame * patches, (frame + 1) * patches), own), queries) * scale
                if frame == count - 1:
                    score = jnp.where(counts_ref[clip] > frame, score, -1e30)
                score_ref[frame * patches : (frame + 1) * patches, :] = score
                top = jnp.maximum(top, jnp.max(score, axis=0, keepdims=True))
            exps = jnp.exp(lat_score - top)
            total = jnp.sum(exps, axis=0, keepdims=True)
            sums = dot_rows(values_of(lat_ref, at, own), exps.astype(BF16))
            for frame in range(count):
                here = slice(frame * patches, (frame + 1) * patches)
                exps = jnp.exp(score_ref[here, :] - top)
                total = total + jnp.sum(exps, axis=0, keepdims=True)
                sums = sums + dot_rows(values_of(pair_ref, here, own), exps.astype(BF16))
            log_ref[0] = jnp.broadcast_to(top + jnp.log(total), (8, wide))
            sum_ref[...] = jnp.transpose(sums * (1.0 / total), (1, 0))

        for count in range(2, frames + 1, 2):
            pl.when((counts_ref[clip] + 1) // 2 * 2 == count)(functools.partial(over, count))
        sums = sum_ref[...]
        attended = collect(sums, heads)
        att_ref[...] = attended
        part_ref[...] = jnp.dot(attended.astype(BF16), wo_ref[...], preferred_element_type=F32)

    clip_rows = lambda cols, count: pl.BlockSpec((count, cols), lambda clip, *_: (clip, 0))
    flat = [half for halves in more for half in halves if half is not None]
    ins = [(value, whole(value.shape)) for value in (*state_in, gain, bias)]
    ins += [(w_query, pl.BlockSpec((None, width, own), lambda *_: (depth, 0, 0))),
            (w_out, pl.BlockSpec((None, own, width), lambda *_: (depth, 0, 0)))]
    ins += [(value, whole(value.shape)) for value in (*flat, *w_pairs)]
    ins.append((media_pair, clip_rows(2 * wide, media_len)))
    outs = [
        ((rows, width), F32, whole((rows, width))),
        ((rows, width), BF16, whole((rows, width))),
        ((rows, wide), BF16, whole((rows, wide))),
        ((rows, 2 * wide), BF16, whole((rows, 2 * wide))),
        ((rows, wide), F32, clip_rows(wide, latent_rows)),
        ((samples, 8, wide), F32, pl.BlockSpec((1, 8, wide), lambda clip, *_: (clip, 0, 0))),
        ((rows, width), F32, clip_rows(width, latent_rows)),
        ((width, wide), BF16, whole((width, wide))),
        ((wide, width), BF16, whole((wide, width))),
    ]
    return call(
        body, [counts, place], (samples,), ins, outs,
        [pltpu.VMEM((media_len, wide), F32), pltpu.VMEM((wide, wide), F32)], "attend",
        2 * samples * media_len * wide * wide * 3, samples * media_len * wide * 4 + 8 * width * wide + 16 * rows * width,
        samples * media_len * wide,
    )


def gelu_parts(values):
    half_more = 0.5 * (1.0 + lax.erf(values * 0.7071067811865476))
    slope = half_more + values * jnp.exp(-0.5 * values * values) * 0.3989422804014327
    return values * half_more, slope


def feed_forward(place, state, part, part_other, gain, bias, w_up, w_down, depth, cotangent=None):
    rows, width = state.shape
    units = w_up.shape[2]
    step = min(256, units)
    steps = units // step
    back = cotangent is not None
    halved = part.shape[0] < rows

    def body(place_ref, state_ref, part_ref, other_ref, gain_ref, bias_ref, up_ref, down_ref, *refs):
        if back:
            cot_ref, mid_ref, x_ref, pre_ref, hid_ref, out_ref, du_ref, dx_ref, dyb_ref = refs
        else:
            mid_ref, x_ref, pre_ref, hid_ref, out_ref = refs
        at = pl.program_id(0)

        @pl.when(at == 0)
        def _():
            if halved:
                middle = state_ref[...] + joined(place_ref[0], part_ref[...], other_ref[...])
            else:
                middle = state_ref[...] + (part_ref[...] + other_ref[...])
            mid_ref[...] = middle
            normed, _, _ = row_norm(middle)
            x_ref[...] = (normed * gain_ref[...] + bias_ref[...]).astype(BF16)
            out_ref[...] = jnp.zeros_like(out_ref)
            if back:
                dx_ref[...] = jnp.zeros_like(dx_ref)
                dyb_ref[...] = cot_ref[...].astype(BF16)

        pre = jnp.dot(x_ref[...], up_ref[...], preferred_element_type=F32)
        pre_ref[...] = pre
        hidden, slope = gelu_parts(pre)
        hidden = hidden.astype(BF16)
        hid_ref[...] = hidden.astype(F32)
        out_ref[...] += jnp.dot(hidden, down_ref[...], preferred_element_type=F32)
        if back:
            du = (mm_bt(dyb_ref[...], down_ref[...]) * slope).astype(BF16)
            du_ref[...] = du.astype(F32)
            dx_ref[...] += mm_bt(du, up_ref[...])

    full = whole((rows, width))
    columns = pl.BlockSpec((rows, step), lambda i, *_: (0, i))
    ins = [(value, whole(value.shape)) for value in (state, part, part_other, gain, bias)]
    ins += [(w_up, pl.BlockSpec((None, width, step), lambda i, *_: (depth, 0, i))), (w_down, pl.BlockSpec((None, step, width), lambda i, *_: (depth, i, 0)))]
    outs = [
        ((rows, width), F32, full),
        ((rows, width), BF16, full),
        ((rows, units), F32, columns),
        ((rows, units), F32, columns),
        ((rows, width), F32, full),
    ]
    scratch = []
    if back:
        ins.append((cotangent, full))
        outs += [((rows, units), F32, columns), ((rows, width), F32, full)]
        scratch = [pltpu.VMEM((rows, width), BF16)]
    return call(
        body, [place], (steps,), ins, outs, scratch, "feed_forward",
        2 * rows * width * units * (4 if back else 2), 4 * width * units + 30 * rows * width, rows * units,
    )


def feed_back(middle_grad, state, grad_x, grad_x_other, gain, pre, w_up, w_down, depth):
    rows, width = state.shape
    units = w_up.shape[2]
    step = min(256, units)
    steps = units // step

    def body(grad_ref, state_ref, gx_ref, gy_ref, gain_ref, pre_ref, up_ref, down_ref, up_out, sums_ref, du_ref, dx_ref, dyb_ref):
        at = pl.program_id(0)

        @pl.when(at == 0)
        def _():
            upstream, sums = latent_back(grad_ref[...], state_ref[...], gx_ref[...] + gy_ref[...], gain_ref[...])
            up_out[...] = upstream
            sums_ref[...] = sums
            dyb_ref[...] = upstream.astype(BF16)
            dx_ref[...] = jnp.zeros_like(dx_ref)

        _, slope = gelu_parts(pre_ref[...])
        du = (mm_bt(dyb_ref[...], down_ref[...]) * slope).astype(BF16)
        du_ref[...] = du.astype(F32)
        dx_ref[...] += mm_bt(du, up_ref[...])

    full = whole((rows, width))
    columns = pl.BlockSpec((rows, step), lambda i: (0, i))
    ins = [(value, whole(value.shape)) for value in (middle_grad, state, grad_x, grad_x_other, gain)]
    ins += [(pre, columns)]
    ins += [(w_up, pl.BlockSpec((None, width, step), lambda i: (depth, 0, i))), (w_down, pl.BlockSpec((None, step, width), lambda i: (depth, i, 0)))]
    return call(
        body, [], (steps,), ins,
        [((rows, width), F32, full), ((8, width), F32, whole((8, width))), ((rows, units), F32, columns), ((rows, width), F32, full)],
        [pltpu.VMEM((rows, width), BF16)], "feed_back",
        4 * rows * width * units, 4 * width * units + 30 * rows * width, rows * units,
    )


def latent_back(middle_grad, state, grad_x, gain):
    normed, _, rstd = row_norm(state)
    upstream = middle_grad + row_norm_back(grad_x, gain, normed, rstd)
    gain_sum = jnp.sum(grad_x * normed, axis=0, keepdims=True)
    bias_sum = jnp.sum(grad_x, axis=0, keepdims=True)
    return upstream, jnp.concatenate([gain_sum, bias_sum, jnp.zeros((6, gain_sum.shape[1]), F32)], axis=0)


def latent_end(middle_grad, state, grad_x, grad_x_other, gain, latent_rows):
    rows, width = state.shape

    def body(grad_ref, state_ref, gx_ref, gy_ref, gain_ref, out_ref):
        upstream, sums = latent_back(grad_ref[...], state_ref[...], gx_ref[...] + gy_ref[...], gain_ref[...])
        total = upstream[:latent_rows]
        for clip in range(1, rows // latent_rows):
            total = total + upstream[clip * latent_rows : (clip + 1) * latent_rows]
        out_ref[...] = jnp.concatenate([sums, total], axis=0)

    ins = [(value, whole(value.shape)) for value in (middle_grad, state, grad_x, grad_x_other, gain)]
    shape = (8 + latent_rows, width)
    return call(body, [], (1,), ins, [(shape, F32, whole(shape))], [], "latent_end", rows * width * 20, rows * width * 16)[0]


def attend_back(
    upstream, middle, grad_mine, grad_other, place, counts, ff_gain, media_gain, media_bias,
    w_query, w_pairs, w_out, w_key, w_value, depth, queries, lat_pair, attended, log_total, latent_x, media_pair, media_x,
    latent_rows, frames, patches,
):
    rows, width = middle.shape
    samples = counts.shape[0]
    wide = w_query.shape[1]
    own = w_key.shape[2]
    turns = len(w_pairs)
    heads = wide // HEAD_DIM
    scale = HEAD_DIM ** (-0.5)
    media_len = frames * patches

    def body(
        counts_ref, place_ref, up_ref, mid_ref, mine_ref, other_ref, ffg_ref, mg_ref, mb_ref,
        wq_ref, wo_ref, *refs,
    ):
        wp_refs = refs[:turns]
        wk_ref, wv_ref, q_ref, lat_ref, att_ref, log_ref, x_ref, pair_ref, mx_ref = refs[turns : turns + 9]
        grad_mid_ref, grad_pair_ref, grad_x_ref, grad_w_ref, sums_ref = refs[turns + 9 : turns + 14]
        low_ref, dq_ref, dlat_ref, col_ref, sum_ref = refs[turns + 14 :]
        clip = pl.program_id(0)

        @pl.when(clip == 0)
        def _():
            grad_x = joined(place_ref[0], mine_ref[...], other_ref[...])
            normed, _, rstd = row_norm(mid_ref[...])
            sums_ref[...] = jnp.zeros_like(sums_ref)
            sums_ref[0:1, :] = jnp.sum(grad_x * normed, axis=0, keepdims=True)
            sums_ref[1:2, :] = jnp.sum(grad_x, axis=0, keepdims=True)
            grad_mid = up_ref[...] + row_norm_back(grad_x, ffg_ref[...], normed, rstd)
            grad_mid_ref[...] = grad_mid
            low_ref[...] = grad_mid.astype(BF16)
            grad_w_ref[...] = jnp.zeros_like(grad_w_ref)
            col_ref[...] = jnp.zeros_like(col_ref)

        at = pl.ds(pl.multiple_of(clip * latent_rows, latent_rows), latent_rows)
        query = spread(q_ref[at, :], heads)
        grad_rows = mm_bt(low_ref[at, :], wo_ref[...]).astype(BF16)
        grad_att = spread(grad_rows, heads)
        cross = spread(grad_rows.astype(F32) * att_ref[at, :], heads)
        cross = jnp.broadcast_to(jnp.sum(cross, axis=1, keepdims=True), (wide, 128))
        delta = jnp.transpose(cross, (1, 0))[0:1, :]
        log = log_ref[0][0:1, :]

        def grads_of(keys, values, alive):
            score = mm_bt(keys, query) * scale
            dprob = mm_bt(values, grad_att)
            probs = jnp.exp(score - log)
            if alive is not None:
                probs = jnp.where(alive, probs, 0.0)
            dscore = (probs * (dprob - delta)).astype(BF16)
            grad_key = (jnp.dot(dscore, query, preferred_element_type=F32) * scale).astype(BF16)
            grad_value = jnp.dot(probs.astype(BF16), grad_att, preferred_element_type=F32).astype(BF16)
            grad_pair = []
            for turn in range(turns):
                grad_pair += [grad_key[:, turn * own : (turn + 1) * own], grad_value[:, turn * own : (turn + 1) * own]]
            return dscore, jnp.concatenate(grad_pair, axis=1)

        lat_keys = keys_of(lat_ref, at, own)
        lat_dscore, dlat_ref[at, :] = grads_of(lat_keys, values_of(lat_ref, at, own), None)

        def over(count):
            dq = dot_rows(lat_dscore, lat_keys)
            for frame in range(count):
                here = slice(frame * patches, (frame + 1) * patches)
                keys = keys_of(pair_ref, here, own)
                alive = counts_ref[clip] > frame if frame == count - 1 else None
                dscore, grad_pair = grads_of(keys, values_of(pair_ref, here, own), alive)
                grad_pair_ref[here, :] = grad_pair
                dq = dq + dot_rows(dscore, keys)
            rows_live = slice(0, count * patches)
            grad_own = grad_pair_ref[rows_live, : 2 * own]
            grad_w_ref[: 2 * own, :] += dot_rows(grad_own, mx_ref[rows_live, :])
            col_ref[0:1, :] += jnp.sum(grad_own.astype(F32), axis=0, keepdims=True)
            sum_ref[...] = dq

        for count in range(2, frames + 1, 2):
            pl.when((counts_ref[clip] + 1) // 2 * 2 == count)(functools.partial(over, count))
        dq = sum_ref[...]
        dq_ref[at, :] = (collect(dq, heads) * scale).astype(BF16)

        @pl.when(clip == samples - 1)
        def _():
            dq_all = dq_ref[...]
            dlat = dlat_ref[...]
            grad_x = mm_bt(dq_all, wq_ref[...])
            for turn in range(turns):
                grad_x += mm_bt(dlat[:, 2 * own * turn : 2 * own * (turn + 1)], wp_refs[turn][...])
            grad_x_ref[...] = grad_x
            columns = jnp.transpose(col_ref[...], (1, 0))
            total_one = jnp.zeros((1, width), F32)
            total_two = jnp.zeros((1, width), F32)
            for slot, own_ref in enumerate((wk_ref, wv_ref)):
                weight = jnp.transpose(own_ref[...].astype(F32), (1, 0))
                column = columns[slot * own : (slot + 1) * own, 0:1]
                media_w = grad_w_ref[slot * own : (slot + 1) * own, :]
                total_one += jnp.sum(weight * (media_w - column * mb_ref[...]), axis=0, keepdims=True)
                total_two += jnp.sum(weight * column, axis=0, keepdims=True)
            sums_ref[2:3, :] = total_one / mg_ref[...]
            sums_ref[3:4, :] = total_two
            x = x_ref[...]
            grad_w_ref[: 2 * own, :] += dot_rows(dlat[:, : 2 * own], x)
            grad_w_ref[2 * own : 3 * own, :] = dot_rows(dq_all[:, :own], x)
            grad_w_ref[3 * own :, :] = dot_rows(att_ref[:, :own].astype(BF16), low_ref[...])

    clip_rows = lambda cols, count: pl.BlockSpec((count, cols), lambda clip, *_: (clip, 0))
    full = whole((rows, width))
    ins = [(value, whole(value.shape)) for value in (
        upstream, middle, grad_mine, grad_other, ff_gain, media_gain, media_bias,
        w_query, w_out, *w_pairs)]
    ins += [(value, pl.BlockSpec((None, width, own), lambda *_: (depth, 0, 0))) for value in (w_key, w_value)]
    ins += [(value, whole(value.shape)) for value in (queries, lat_pair, attended)]
    ins += [(log_total, pl.BlockSpec((1, 8, wide), lambda clip, *_: (clip, 0, 0))), (latent_x, full)]
    ins += [(media_pair, clip_rows(2 * wide, media_len)), (media_x, clip_rows(width, media_len))]
    outs = [
        ((rows, width), F32, full),
        (media_pair.shape, BF16, clip_rows(2 * wide, media_len)),
        ((rows, width), F32, full),
        ((4 * own, width), F32, whole((4 * own, width))),
        ((8, width), F32, whole((8, width))),
    ]
    scratch = [
        pltpu.VMEM((rows, width), BF16),
        pltpu.VMEM((rows, wide), BF16),
        pltpu.VMEM((rows, 2 * wide), BF16),
        pltpu.VMEM((8, 2 * own), F32),
        pltpu.VMEM((wide, wide), F32),
    ]
    return call(
        body, [counts, place], (samples,), ins, outs, scratch, "attend_back", rows * width, rows * width,
    )


def outer_sums(pairs, planes, name):
    count, wide = pairs[0][0].shape
    units = pairs[0][2].shape[1]
    chunk = wide // planes
    step = min(512, units)

    def body(*refs):
        out_ref = refs[-1]
        for pair in range(len(pairs)):
            mine, other, rows, rows_other = [ref[...].astype(BF16) for ref in refs[4 * pair : 4 * pair + 4]]
            total = dot_rows(mine, rows) + dot_rows(other, rows_other)
            for plane in range(planes):
                out_ref[plane, pair] = total[plane * chunk : (plane + 1) * chunk, :]

    ins = []
    for pair in pairs:
        ins += [(value, whole(value.shape)) for value in pair[:2]]
        ins += [(value, pl.BlockSpec((count, step), lambda i: (0, i))) for value in pair[2:]]
    shape = (planes, len(pairs), chunk, units)
    return call(
        body, [], (units // step,), ins,
        [(shape, F32, pl.BlockSpec((planes, len(pairs), chunk, step), lambda i: (0, 0, 0, i)))], [], name,
        4 * len(pairs) * count * wide * units, 4 * len(pairs) * wide * units,
    )[0]


def gathered_sums(place, gathered, columns):
    planes, count, wide = columns.shape
    units = gathered.shape[1]

    def body(place_ref, hidden_ref, column_ref, out_ref):
        turn = pl.program_id(0)
        part = dot_rows(hidden_ref[...].astype(BF16), column_ref[...].astype(BF16))

        @pl.when(turn == 0)
        def _():
            out_ref[...] = part

        @pl.when(turn > 0)
        def _():
            out_ref[...] += part

    ins = [
        (gathered, pl.BlockSpec((count, units), lambda turn, place_ref: (lax.rem(place_ref[3] + planes - turn, planes), 0))),
        (columns, pl.BlockSpec((None, count, wide), lambda turn, place_ref: (turn, 0, 0))),
    ]
    return call(
        body, [place], (planes,), ins, [((units, wide), F32, whole((units, wide)))], [], "gathered_sums",
        2 * planes * count * units * wide, 4 * planes * count * (units + wide),
    )[0]


def media_back(grad_pairs, pairs, weights, gain_means, bias_means, gains, media, time_rows, stats, counts, place, frames, patches, groups):
    rows, width = media.shape
    layers = len(pairs)
    turns = len(weights[0])
    wide2 = pairs[0].shape[1]
    chip = width // groups
    half = chip // 2
    group = frames_in_block(frames)
    groups_of = frames // group
    samples = counts.shape[0]

    def body(counts_ref, place_ref, *refs):
        grad_refs = refs[:layers]
        pair_refs = refs[layers : 2 * layers]
        weight_refs = refs[2 * layers : (2 + turns) * layers]
        gm_ref, bm_ref, gain_ref, media_ref, time_ref, stat_ref, mine_ref, theirs_ref, sum_ref = refs[(2 + turns) * layers :]
        part = wide2 // turns
        clip, at = pl.program_id(0), pl.program_id(1)
        @pl.when((clip == 0) & (at == 0))
        def _():
            sum_ref[...] = jnp.zeros_like(sum_ref)

        def work(inners):
            for inner in inners:
                here = slice(inner * patches, (inner + 1) * patches)
                total = jnp.zeros((patches, chip), F32)
                one = jnp.zeros((patches, wide2), F32)
                two = jnp.zeros((patches, wide2), F32)
                for layer in range(layers):
                    grad = grad_refs[layer][here, :]
                    product = jnp.zeros((patches, chip), F32)
                    for turn in range(turns):
                        product += mm_bt(grad[:, turn * part : (turn + 1) * part], weight_refs[layer * turns + turn][...])
                    total = total + product * gain_ref[layer : layer + 1, :]
                    grad = grad.astype(F32)
                    one = one + grad * gm_ref[layer : layer + 1, :]
                    two = two + grad * (pair_refs[layer][here, :].astype(F32) - bm_ref[layer : layer + 1, :])
                mean_one = jnp.sum(one, axis=1, keepdims=True)
                mean_two = jnp.sum(two, axis=1, keepdims=True) * (1.0 / width)
                stat = stat_ref[here, :]
                mean, rstd = stat[:, 0:1], stat[:, 64:65]
                normed = (media_ref[here, :].astype(F32) + time_ref[pl.ds(at * group + inner, 1), :] - mean) * rstd
                out = rstd * (total - mean_one - normed * mean_two)
                sum_ref[pl.ds(at * group + inner, 1), :] += jnp.sum(out, axis=0, keepdims=True)
                low, high = out[:, :half], out[:, half:]
                first = place_ref[0] == 0
                mine_ref[here, :] = jnp.where(first, low, high)
                theirs_ref[here, :] = jnp.where(first, high, low)

        def dead(inner):
            here = slice(inner * patches, (inner + 1) * patches)
            mine_ref[here, :] = jnp.zeros((patches, half), F32)
            theirs_ref[here, :] = jnp.zeros((patches, half), F32)

        by_live_spans(at, counts_ref[clip], group, work, dead)

        @pl.when(at * group >= counts_ref[clip])
        def _():
            for inner in range(group):
                dead(inner)

    block = live_block(group, groups_of)

    def chip_block(clip, at, counts_ref, place_ref):
        return (block(clip, at, counts_ref)[0], place_ref[1])

    deep = group * patches
    pair_spec = pl.BlockSpec((deep, wide2), block)
    out_spec = pl.BlockSpec((deep, half), lambda clip, at, *_: (clip * groups_of + at, 0))
    by_chip = lambda count: pl.BlockSpec((count, chip), lambda clip, at, counts_ref, place_ref: (0, place_ref[1]))
    ins = [(value, pair_spec) for value in (*grad_pairs, *pairs)]
    ins += [
        (value, pl.BlockSpec((chip, wide2 // turns), lambda clip, at, counts_ref, place_ref: (place_ref[1], 0)))
        for pieces in weights for value in pieces
    ]
    ins += [
        (gain_means, whole(gain_means.shape)), (bias_means, whole(bias_means.shape)),
        (gains, by_chip(layers)), (media, pl.BlockSpec((deep, chip), chip_block)), (time_rows, by_chip(frames)),
        (stats, pl.BlockSpec((deep, 128), block)),
    ]
    return call(
        body, [counts, place], (samples, groups_of), ins,
        [((rows, half), F32, out_spec)] * 2 + [((frames, chip), F32, whole((frames, chip)))], [], "media_back", rows * half, rows * half,
    )


def media_sum(mine, arrived):
    rows, width = mine.shape
    deep = rows // 6 if rows % 96 == 0 else rows

    def body(mine_ref, arrived_ref, out_ref):
        out_ref[...] = (mine_ref[...] + arrived_ref[...]).astype(BF16)

    spec = pl.BlockSpec((deep, width), lambda i: (i, 0))
    return call(
        body, [], (rows // deep,), [(mine, spec), (arrived, spec)], [((rows, width), BF16, spec)], [], "media_sum",
        2 * rows * width, 10 * rows * width,
    )[0]


def finish_ff(ups, downs):
    layers = len(ups)
    chunk, units = ups[0].shape

    def body(*refs):
        up_ref, down_ref = refs[2 * layers :]
        for layer in range(layers):
            up_ref[layer] = refs[layer][...]
            down = refs[layers + layer][...]
            down_ref[layer] = down if layer == 0 else jnp.transpose(down, (1, 0))

    ins = [(value, whole(value.shape)) for value in (*ups, *downs)]
    shapes = [(layers, chunk, units), (layers, units, chunk)]
    return call(
        body, [], (1,), ins, [(shape, F32, whole(shape)) for shape in shapes], [], "finish_ff",
        4 * layers * chunk * units, 16 * layers * chunk * units,
    )


def finish_attn(attn, layers, own):
    chunk = attn.shape[1]

    def body(attn_ref, query_ref, key_ref, value_ref, out_ref):
        for layer in range(layers):
            for slot, ref in enumerate((key_ref, value_ref, query_ref, out_ref)):
                at = (4 * layer + slot) * own
                part = attn_ref[at : at + own, :]
                ref[layer] = part if slot == 3 else jnp.transpose(part, (1, 0))

    shapes = [(layers, chunk, own)] * 3 + [(layers, own, chunk)]
    return call(
        body, [], (1,), [(attn, whole(attn.shape))], [(shape, F32, whole(shape)) for shape in shapes], [], "finish_attn",
        attn.size, 8 * attn.size,
    )


class Links:

    def __init__(self, zero):
        self.zero = zero
        self.planes = lax.axis_size("plane")
        self.groups = lax.axis_size("group")
        self.plane = lax.axis_index("plane")
        self.side = lax.axis_index("side")
        self.group = lax.axis_index("group")
        self.core = lax.axis_index("core")

    def rounded(self, value):
        return (value + self.zero).astype(BF16)

    def core_swap(self, value):
        return lax.ppermute(value, "core", [(0, 1), (1, 0)])

    def side_swap(self, value):
        return lax.ppermute(value, "side", [(0, 1), (1, 0)])

    def group_turn(self, value, turn):
        return lax.ppermute(value, "group", [(i, (i + turn) % self.groups) for i in range(self.groups)])

    def plane_turn(self, value, turn):
        return lax.ppermute(value, "plane", [(i, (i + turn) % self.planes) for i in range(self.planes)])

    def cut(self, value, index):
        half = value.shape[0] // 2
        return lax.dynamic_slice_in_dim(value, index * half, half, 0)

    def join(self, mine, other, index):
        first = index == 0
        return jnp.concatenate([jnp.where(first, mine, other), jnp.where(first, other, mine)], axis=0)

    def pair_join(self, mine, other, index, axis):
        first = index == 0
        return jnp.concatenate([jnp.where(first, mine, other), jnp.where(first, other, mine)], axis=axis)

    def group_join(self, value, turned, axis):
        if self.groups == 2:
            return self.pair_join(value, turned[0], self.group, axis)
        turned = jnp.stack([value] + turned)
        slots = [lax.rem(self.group - source + self.groups, self.groups) for source in range(self.groups)]
        return jnp.concatenate([lax.dynamic_index_in_dim(turned, slot, 0, keepdims=False) for slot in slots], axis=axis)

    def core_half(self, value):
        return self.cut(value, self.core) + self.core_swap(self.cut(value, 1 - self.core))

    def group_turns(self, value):
        return [self.group_turn(value, k) for k in range(1, self.groups)]

    def group_total(self, value, turned):
        if self.groups == 2:
            return value + turned[0]
        turned = jnp.stack([value] + turned)
        total = None
        for source in range(self.groups):
            slot = lax.rem(self.group - source + self.groups, self.groups)
            term = lax.dynamic_index_in_dim(turned, slot, 0, keepdims=False)
            total = term if total is None else total + term
        return total

    def tensor_halves(self, value):
        mine = self.core_half(value)
        mine = self.group_total(mine, self.group_turns(mine))
        return mine, self.core_swap(mine)

    def dp_sum(self, value):
        value = value + self.side_swap(value)
        step = 1
        while step < self.planes:
            value = value + lax.ppermute(value, "plane", [(i, i ^ step) for i in range(self.planes)])
            step *= 2
        return value

    def columns(self, value, side):
        wide = value.shape[1] // (2 * self.planes)
        cuts = [value[:, i * wide : (i + 1) * wide] for i in range(2 * self.planes)]
        return jnp.where(side == 0, jnp.concatenate(cuts[0::2], axis=1), jnp.concatenate(cuts[1::2], axis=1))

    def both_columns(self, value):
        return self.columns(value, self.side), self.side_swap(self.columns(value, 1 - self.side))

    def scatter(self, value, dimension):
        return lax.psum_scatter(value, "plane", scatter_dimension=dimension, tiled=True)


def local(
    media,
    frame_counts,
    time_embed,
    latents,
    media_gain,
    media_bias,
    latent_gain,
    latent_bias,
    ff_gain,
    ff_bias,
    w_query,
    w_key,
    w_value,
    w_out,
    w_up,
    w_down,
    cotangent,
):
    links = Links(jnp.where(frame_counts[0] > 1000000, 1.0, 0.0).astype(F32))
    samples, media_len, width = media.shape
    frames = time_embed.shape[0]
    patches = media_len // frames
    latent_rows = latents.shape[0]
    own = w_query.shape[2]
    layers = w_query.shape[0]
    wide = own * links.groups
    rows = samples * latent_rows
    tensor_size = 2 * links.groups
    turns = range(1, links.groups)
    place = jnp.stack([links.core, links.group, links.side, links.plane]).astype(jnp.int32)

    def row(value, depth):
        return value[depth : depth + 1]

    def after(values, event):
        return lax.optimization_barrier((values, event))

    def project(depth, x, pair, weight, nears, fars):
        pieces = [weight]
        for k in turns:
            far = None if fars is None else fars[k - 1]
            pair, weight, *x_made = project_more(x, frame_counts, place, pair, nears[k - 1], far, k, frames, patches)
            if x_made:
                (x,) = x_made
            pieces.append(weight)
        return x, pair, pieces

    def packed(wanted, event):
        (pairs, queries, outs), event = after(((w_key, w_value), (w_query,), (w_out,)), event)
        weights = {"pair": pairs, "query": queries, "out": outs}
        values = pack(place, [(weights[name], depth, name == "pair") for name, depth in wanted], "pack")
        return lax.optimization_barrier((values, event))

    def by_side(nears):
        return [links.side_swap(value) for value in nears]

    def more_of(depth):
        return [(query, None, out, None) for query, out in zip(nears["query", depth], nears["out", depth])]

    media_rows = media.reshape(samples * media_len, width)
    time_rows = time_embed.astype(F32)

    def prepared(depth, media_then):
        return prepare(
            media_then, frame_counts, time_rows, row(media_gain, depth), row(media_bias, depth),
            w_key, w_value, depth, links.groups, frames, patches,
        )

    nears = {}
    media_then = media_rows
    if layers > 1:
        wanted = [("pair", 1), ("query", 1), ("out", 1), ("pair", 0)]
        values, media_then = packed(wanted, media_rows)
        nears.update((name, links.group_turns(value)) for name, value in zip(wanted[:2], values[:2]))
        next_out, first_pair = values[2:]
    stats, pair, weight = prepared(0, media_then)
    media_x, media_pair, w_pairs = [None], [pair], [[weight]]
    fars = {}
    more = [[]]

    state_in = (jnp.broadcast_to(latents.astype(F32)[None], (samples, latent_rows, width)).reshape(rows, width),)
    cotangent_rows = cotangent.reshape(rows, width)
    low_cotangent, stats = after(cotangent_rows.astype(BF16).astype(F32), stats)
    upstream_cols = links.both_columns(low_cotangent)
    saved = []
    early = []

    def attended_layer(depth, state_in, more, pieces, pair):
        return attend(
            state_in, place, frame_counts, row(latent_gain, depth), row(latent_bias, depth),
            w_query, w_out, more, pieces, depth, pair, latent_rows, frames, patches,
        )

    for depth in range(layers):
        last = depth == layers - 1
        state, latent_x, queries, lat_pair, attended, log_total, part, query4, out4 = attended_layer(
            depth, state_in, more[depth], w_pairs[depth], media_pair[depth]
        )
        if depth == 0:
            if not last:
                names = [(name, 1) for name in ("pair", "query")]
                (arrived, first_pair), part = after(([nears[name] for name in names], first_pair), part)
                nears.update(zip(names, arrived))
                nears["pair", 0] = links.group_turns(first_pair)
                fars["pair", 1] = by_side(nears["pair", 1])
            mine = links.core_half(part)
            if last:
                part = links.tensor_halves(part)
            else:
                media_then, mine = after(media_rows, mine)
                first_sent, mine = packed([("query", 0), ("out", 0)], mine)
                turned = links.group_turns(mine)
                x, pair, weight = prepared(1, media_then)
                arrived = (turned, nears["pair", 0], upstream_cols, next_out, fars["pair", 1])
                (turned, nears["pair", 0], upstream_cols, next_out, fars["pair", 1]), x = after(arrived, x)
                nears["out", 1] = links.group_turns(next_out)
                mine = links.group_total(mine, turned)
                fars["pair", 1], mine = after(fars["pair", 1], mine)
                part = (mine, links.core_swap(mine))
        else:
            if depth == 1:
                fars["pair", 0], part = after(fars["pair", 0], part)
            part = (part, links.core_swap(part))
        middle, ff_x, pre, hidden, out_part, *back = feed_forward(
            place, state, *part, row(ff_gain, depth), row(ff_bias, depth),
            w_up, w_down, depth, cotangent_rows if last else None,
        )
        saved.append((state, latent_x, queries, lat_pair, attended, log_total, middle, pre, hidden, query4, out4))
        if last:
            hidden_other = links.side_swap(hidden)
            (ff_x, back[0]), hidden_other = after((ff_x, back[0]), hidden_other)
            early.append((hidden_other, links.both_columns(ff_x.astype(F32))))
            continue
        if depth == 0:
            first_hidden = lax.all_gather(hidden, "plane", axis=0, tiled=True)
        early.append((hidden, ff_x))
        mine = links.core_half(out_part)
        if depth > 0:
            media_then, mine = after(media_rows, mine)
            x, pair, weight = prepared(depth + 1, media_then)
        (x, fars["pair", depth + 1], ff_x), mine = after((x, fars["pair", depth + 1], ff_x), mine)
        ff_x_cols = links.both_columns(ff_x.astype(F32))
        turned = links.group_turns(mine)
        _, pair, pieces = project(depth + 1, x, pair, weight, nears["pair", depth + 1], fars["pair", depth + 1])
        if depth == 0:
            (turned, nears["pair", 0]), pair = after((turned, nears["pair", 0]), pair)
            fars["pair", 0] = by_side(nears["pair", 0])
        else:
            turned, pair = after(turned, pair)
        media_x.append(x)
        media_pair.append(pair)
        w_pairs.append(pieces)
        mine = links.group_total(mine, turned)
        state_in = (middle, mine, links.core_swap(mine))
        ff_x_cols, state_in = after(ff_x_cols, state_in)
        if depth == 0:
            nears["out", 1], state_in = after(nears["out", 1], state_in)
        early[depth] = (early[depth][0], ff_x_cols)
        more.append(more_of(depth + 1))
    mine, out_mine = links.core_half(back[1]), links.core_half(out_part)
    turned, out_turned = links.group_turns(mine), links.group_turns(out_mine)
    hidden_other = early[-1][0]
    if layers > 1:
        (media_then, pair), mine = after((media_rows, media_pair[0]), mine)
        source = (media_then, time_rows, row(media_gain, 0), row(media_bias, 0))
        media_x[0], media_pair[0], w_pairs[0] = project(
            0, source, pair, w_pairs[0][0], nears["pair", 0], fars["pair", 0]
        )
        arrived = (turned, out_turned, hidden_other, first_hidden)
        (turned, out_turned, hidden_other, first_hidden), media_pair[0] = after(arrived, media_pair[0])
    early[-1] = (hidden_other, early[-1][1])
    back[1] = links.group_total(mine, turned)
    out_mine = links.group_total(out_mine, out_turned)
    sums = (out_mine, links.core_swap(out_mine))
    resampled = middle + links.join(*sums, links.core)

    upstream = cotangent_rows
    grads = [None] * layers
    gains = [None] * layers
    pair_grads = [None] * layers
    attn_ws = [None] * layers
    units = w_up.shape[2]
    for depth in reversed(range(layers)):
        state, latent_x, queries, lat_pair, attended, log_total, middle, pre, hidden, query4, out4 = saved[depth]
        if depth == layers - 1:
            grad_pre, grad_ffx = back
        else:
            upstream, latent_sums, grad_pre, grad_ffx = feed_back(
                grad_middle, saved[depth + 1][0], grad_x, grad_x_other, row(latent_gain, depth + 1),
                pre, w_up, w_down, depth,
            )
            gains[depth + 1] += (latent_sums[0], latent_sums[1])
            first_low = upstream.astype(BF16).astype(F32)
            if depth == 0:
                media_pair[0], (grad_pre, up_sums) = after(media_pair[0], (grad_pre, up_sums))
                more[0] = more_of(0)
                _, latent_x, queries, lat_pair, attended, log_total, _, query4, out4 = attended_layer(
                    0, (state,), more[0], w_pairs[0], media_pair[0]
                )
                pre_other, queries = after(links.side_swap(grad_pre), queries)
        hidden_other, ff_x_cols = early[depth]
        down = (*upstream_cols, hidden, hidden_other)
        up = (*ff_x_cols, grad_pre, links.side_swap(grad_pre) if depth == layers - 1 else pre_other)
        if depth == layers - 1:
            grad_mine, grad_other = grad_ffx, links.core_swap(grad_ffx)
        else:
            grad_mine, grad_other = links.tensor_halves(grad_ffx)
        if depth == layers - 1:
            down = outer_sums([down], links.planes, "down_sums")
            grad_mine, down = after(grad_mine, down)
            if depth > 0:
                first_sent, down = after(first_sent, down)
                first_near = [links.group_turns(value) for value in first_sent]
            grad_down = links.scatter(down.reshape(-1, units), 0)
        else:
            up_sums = outer_sums([up], links.planes, "up_sums")
            grad_mine, up_sums = after(grad_mine, up_sums)
            pair_width = width // links.planes
            share = rows // tensor_size
            first_low, up_sums = after(first_low, up_sums)
            low_share = lax.dynamic_slice_in_dim(first_low, (links.group * 2 + links.core) * share, share, 0)

            def for_plane(value, turn):
                at = lax.rem(links.plane + turn, links.planes) * pair_width
                return lax.dynamic_slice_in_dim(value, at, pair_width, 1)

            columns = [links.plane_turn(for_plane(low_share, k), k) for k in range(1, links.planes)]
            above, up_sums = after(attn_ws[depth + 1], up_sums)
            attn_ws[depth + 1] = above[0] + links.side_swap(above[1])
            grad_up = links.scatter(up_sums.reshape(-1, units), 0)
            grad_down = None
        grad_middle, pair_grads[depth], grad_x, attn_w, sums = attend_back(
            upstream, middle, grad_mine, grad_other, place, frame_counts,
            row(ff_gain, depth), row(media_gain, depth), row(media_bias, depth),
            query4, w_pairs[depth], out4, w_key, w_value, depth, queries, lat_pair, attended, log_total, latent_x,
            media_pair[depth], media_x[depth], latent_rows, frames, patches,
        )
        if depth == layers - 1:
            (pre_other, cols_other, first_near), grad_x = after((up[3], up[1], first_near), grad_x)
            nears["query", 0], nears["out", 0] = first_near
            up_sums = outer_sums([(up[0], cols_other, up[2], pre_other)], links.planes, "up_sums")
            grad_up = links.scatter(up_sums.reshape(-1, units), 0)
        if depth < layers - 1:
            attn_ws[depth + 1], attn_w = after(attn_ws[depth + 1], attn_w)
        grad_x_other = links.core_swap(grad_x)
        attn_ws[depth] = (links.columns(attn_w, links.side), links.columns(attn_w, 1 - links.side))
        grads[depth] = (grad_up, grad_down)
        gains[depth] = (sums[0], sums[1], sums[2], sums[3])
    ending = latent_end(grad_middle, saved[0][0], grad_x, grad_x_other, row(latent_gain, 0), latent_rows)
    gains[0] += (ending[0], ending[1])
    latent_part = ending[8:]
    share = 1.0 / tensor_size
    gains = [(g[2], g[3], g[4] * share, g[5] * share, g[0] * share, g[1] * share) for g in gains]

    core_width = width // tensor_size

    def column_cuts(value):
        return [value[:, i * core_width : (i + 1) * core_width] for i in range(tensor_size)]

    def column_cut(value, index):
        return lax.dynamic_slice_in_dim(value, index * core_width, core_width, 1)

    gain_flat = jnp.stack([gains[l][m] for m in range(6) for l in range(layers)])
    by_core = [jnp.concatenate(column_cuts(gain_flat)[c::2], axis=1) for c in range(2)]
    core_mine = jnp.where(links.core == 0, by_core[0], by_core[1])
    core_theirs = jnp.where(links.core == 0, by_core[1], by_core[0])
    gain_share = core_mine + links.core_swap(core_theirs)
    latent_share = column_cut(latent_part, links.group * 2 + links.core)

    weight_long = [jnp.concatenate(w_pairs[l], axis=1).astype(F32) for l in range(layers)]
    gain_means = jnp.stack([jnp.sum(weight_long[l] * media_gain[l][:, None], axis=0) / width for l in range(layers)])
    bias_means = jnp.stack([jnp.sum(weight_long[l] * media_bias[l][:, None], axis=0) for l in range(layers)])
    ready = (*attn_ws[0], gain_share, latent_share)
    (attn_mine, attn_theirs, gain_share, latent_share), stats = after(ready, stats)
    attn_theirs = links.side_swap(attn_theirs)
    gain_turned = [
        links.group_turn(column_cut(gain_share, lax.rem(links.group + turn, links.groups)), turn) for turn in turns
    ]
    grads[-1], stats = after(grads[-1], stats)
    mine, theirs, time_sums = media_back(
        pair_grads, media_pair, w_pairs, gain_means, bias_means, media_gain, media_rows, time_rows, stats,
        frame_counts, place, frames, patches, links.groups,
    )
    arrived = (attn_theirs, columns, grads[0][0], gain_turned)
    (mine, theirs, time_sums), arrived = after((mine, theirs, time_sums), arrived)
    attn_theirs, columns, first_up, gain_turned = arrived
    attn_ws[0] = attn_mine + attn_theirs
    attn = links.scatter(jnp.concatenate(attn_ws, axis=0), 1)

    time_halves = [time_sums[:, :core_width], time_sums[:, core_width:]]
    time_part = jnp.where(links.core == 0, *time_halves) + links.core_swap(jnp.where(links.core == 0, *time_halves[::-1]))
    columns = jnp.stack(columns)
    columns = links.pair_join(columns, links.core_swap(columns), links.core, 1)
    theirs, (time_part, columns) = after(theirs, (time_part, columns))
    gain_sum = column_cut(gain_share, links.group)
    for value in gain_turned:
        gain_sum = gain_sum + value
    small = jnp.concatenate([gain_sum, time_part, latent_share], axis=0)
    columns = links.group_join(columns, links.group_turns(columns), 1)
    small = small + links.side_swap(small)
    columns = jnp.concatenate([for_plane(first_low, 0)[None], columns], axis=0)
    first_down = gathered_sums(place, first_hidden, columns)
    chunk = pair_width // 2
    first_theirs = lax.dynamic_slice_in_dim(first_down, (1 - links.side) * chunk, chunk, 1)
    step = 1
    while step < links.planes:
        small = small + lax.ppermute(small, "plane", [(i, i ^ step) for i in range(links.planes)])
        if step == 1:
            small, first_theirs = after(small, first_theirs)
        step *= 2
    first_down = lax.dynamic_slice_in_dim(first_down, links.side * chunk, chunk, 1) + links.side_swap(first_theirs)
    media_grad = media_sum(mine, links.core_swap(theirs))
    small, media_grad = after(small, media_grad)
    media_grad = media_grad.reshape(samples, media_len, core_width)
    pair = links.pair_join(small, links.core_swap(small), links.core, 1)
    small_all = links.group_join(pair, links.group_turns(pair), 1)
    gain_all = small_all[: 6 * layers].reshape(6, layers, width)
    time_grad = small_all[6 * layers : 6 * layers + frames]
    latents_grad = small_all[6 * layers + frames :]
    ups = [first_up] + [grads[l][0] for l in range(1, layers)]
    downs = [first_down] + [grads[l][1] for l in range(1, layers)]
    w_up_grad, w_down_grad = finish_ff(ups, downs)
    w_query_grad, w_key_grad, w_value_grad, w_out_grad = finish_attn(attn, layers, own)

    return (
        resampled.reshape(samples, latent_rows, width),
        media_grad,
        time_grad,
        latents_grad,
        gain_all[0],
        gain_all[1],
        gain_all[2],
        gain_all[3],
        gain_all[4],
        gain_all[5],
        w_query_grad,
        w_key_grad,
        w_value_grad,
        w_out_grad,
        w_up_grad,
        w_down_grad,
    )


def solution(mesh):
    dp_size, tensor_size = mesh.devices.shape
    split = jax.sharding.Mesh(
        mesh.devices.reshape(dp_size // 2, 2, tensor_size // 2, 2), ("plane", "side", "group", "core")
    )
    dp, tensor = ("plane", "side"), ("group", "core")
    in_specs = (
        P(dp, None, None),
        P(dp),
        P(),
        P(),
        P(),
        P(),
        P(),
        P(),
        P(),
        P(),
        P(None, None, tensor),
        P(None, None, tensor),
        P(None, None, tensor),
        P(None, tensor, None),
        P(None, None, tensor),
        P(None, tensor, None),
        P(dp, None, None),
    )
    out_specs = (
        P(dp, None, None),
        P(dp, None, tensor),
        P(),
        P(),
        P(),
        P(),
        P(),
        P(),
        P(),
        P(),
        P(None, dp, tensor),
        P(None, dp, tensor),
        P(None, dp, tensor),
        P(None, tensor, dp),
        P(None, dp, tensor),
        P(None, tensor, dp),
    )
    return jax.shard_map(local, mesh=split, in_specs=in_specs, out_specs=out_specs, check_vma=False)
```
